32 devices in a mesh: section: 2 (over x), dp: 4 (over y, core), expert: 4 (over z).
Axes of the slice: x: 2, y: 2, z: 4, core: 2. Of those that a mesh axis runs over, the one named last changes fastest.
Arguments:
- inputs: bfloat16 [2, 4, 1024, 1024], P(None, 'dp', 'expert'), may hold values from -6 to 6
- cotangent: bfloat16 [2, 4, 1024, 1024], P(None, 'dp', 'expert'), may hold values from -6 to 6
- gain_attn: float32 [2, 1024], P('section'), may hold values from 0.5 to 1.5
- w_query: bfloat16 [2, 1024, 1024], P('section'), may hold values from -0.1875 to 0.1875
- w_key: bfloat16 [2, 1024, 512], P('section'), may hold values from -0.1875 to 0.1875
- w_value: bfloat16 [2, 1024, 512], P('section'), may hold values from -0.1875 to 0.1875
- w_out: bfloat16 [2, 1024, 1024], P('section'), may hold values from -0.75 to 0.75
- gain_moe: float32 [2, 1024], P('section'), may hold values from 0.5 to 1.5
- w_router: bfloat16 [2, 1024, 32], P('section'), may hold values from -0.09375 to 0.09375
- w_gate: bfloat16 [2, 32, 1024, 512], P('section', 'expert'), may hold values from -0.1875 to 0.1875
- w_up: bfloat16 [2, 32, 1024, 512], P('section', 'expert'), may hold values from -0.1875 to 0.1875
- w_down: bfloat16 [2, 32, 512, 1024], P('section', 'expert'), may hold values from -0.75 to 0.75
- doc_lengths: int32 [2, 4, 4], P(None, 'dp'), may hold values from 0 to 1024, as said below
- routes: int32 [2, 2, 4, 1024, 8], P('section', None, 'dp', 'expert'), may hold values from 0 to 31, all different within a row
Outputs:
- layer_outputs: bfloat16 [2, 2, 4, 1024, 1024], P('section', None, 'dp', 'expert')
- input_grads: bfloat16 [2, 2, 4, 1024, 1024], P('section', None, 'dp', 'expert')
- grad_gain_attn: float32 [2, 1024], P('section', ('dp', 'expert'))
- grad_query: float32 [2, 1024, 1024], P('section', ('dp', 'expert'))
- grad_key: float32 [2, 1024, 512], P('section', ('dp', 'expert'))
- grad_value: float32 [2, 1024, 512], P('section', ('dp', 'expert'))
- grad_out: float32 [2, 1024, 1024], P('section', ('dp', 'expert'))
- grad_gain_moe: float32 [2, 1024], P('section', ('dp', 'expert'))
- grad_router: float32 [2, 1024, 32], P('section', ('dp', 'expert'))
- grad_gate: float32 [2, 32, 1024, 512], P('section', 'expert', 'dp')
- grad_up: float32 [2, 32, 1024, 512], P('section', 'expert', 'dp')
- grad_down: float32 [2, 32, 512, 1024], P('section', 'expert', 'dp')
The draws below stay inside these ranges and needn't reach their ends.
Inputs may be any that keep to these rules, and one draw needn't show every extreme that they name: `doc_lengths`: each sequence's lengths sum to 1024 or less; in every group of 4 sequences each sequence has one micro-batch in which a single document fills all 1024 positions, the other lengths being 0. `routes`: each token names 8 different experts.
All inputs are finite; a program needn't handle non-finite values.
Results may differ from the reference program's by a relative error of at most 0.023.
Values may be sent and summed in bfloat16 or wider, within the bound.
No kernel may reach another device: no remote copies, remote signals or barrier semaphores. Data moves between devices by JAX's collectives and lax.ppermute only.
A program may use at most 384 MiB of HBM per device.

```python
import jax
import jax.numpy as jnp
from jax import lax

D = 1024
HEADS = 16
KV_HEADS = 8
HEAD_DIM = 64
FF = 512
EXPERTS = 32
TOPK = 8
WINDOW = 512
SEQ = 1024
NDOC = 4
MB = 2
LAYERS = 2
SEQS = 4
SEQ_DEV = 256
CAP = 64
N_EXPERT = 4


def draw_doc_lengths(key, part):
    key = jax.random.fold_in(key, 11)
    pick_key, length_key = jax.random.split(key)
    whole_batch = jax.random.randint(pick_key, (SEQS,), 0, MB)
    pieces = jax.random.randint(length_key, (MB, SEQS, NDOC), SEQ // 8, SEQ // NDOC + 1)
    single = (jnp.arange(NDOC) == 0).astype(jnp.int32) * SEQ
    marked = jnp.arange(MB)[:, None] == whole_batch[None, :]
    return jnp.where(marked[:, :, None], single[None, None, :], pieces).astype(jnp.int32)


def block_scale(key, extent, cuts, least, high):
    level = 1.0
    for position, parts in cuts:
        steps = jax.random.uniform(jax.random.fold_in(jax.random.fold_in(key, 6), position), (parts,), jnp.float32, least / len(cuts), high / len(cuts))
        level = level * jnp.repeat(jnp.exp(steps), extent[position] // parts).reshape((-1,) + (1,) * (len(extent) - 1 - position))
    return level


def distinct(rng, rows, number_of, top, lift):
    sequence = jax.random.permutation(jax.random.fold_in(rng, 1), number_of)
    pull = sequence
    for power in range(3):
        pull = pull * pull // number_of
    pull = pull * lift // number_of
    lots = jax.random.randint(jax.random.fold_in(rng, 2), (rows, number_of), 0, 4096) + pull
    fixed_rows = jax.random.permutation(jax.random.fold_in(rng, 3), rows)[jnp.arange(number_of) % rows]
    lots = jnp.where(jnp.arange(rows)[:, None] == fixed_rows[None, :], 1 << 14, lots)
    priority = lots * number_of + jnp.arange(number_of)
    return lax.top_k(priority.astype(jnp.int32), top)[1].astype(jnp.int32)


def gaussian(own_key, shape, spread, limit, cuts=(), held_as=jnp.bfloat16):
    drawn = jax.random.normal(own_key, shape, jnp.float32) * spread
    if len(cuts) > 0:
        drawn = block_scale(own_key, shape, cuts, -0.22, 0.18) * drawn
    return jnp.clip(drawn, min=-limit, max=limit).astype(held_as)


def setup_inputs(seed: int = 0) -> dict:
    key_list = jax.random.split(jax.random.key(seed), 15)
    inputs = gaussian(key_list[0], (MB, SEQS, SEQ, D), 1.0, 6.0, ((1, 4), (2, 4)))
    cotangent = gaussian(key_list[1], (MB, SEQS, SEQ, D), 1.0, 6.0, ((1, 4), (2, 4)))
    gain_attn = jnp.clip(1.0 + 0.1 * jax.random.normal(key_list[2], (LAYERS, D), jnp.float32), 0.5, 1.5)
    w_query = gaussian(key_list[3], (LAYERS, D, D), D ** -0.5, 0.1875, ((0, 2),))
    w_key = gaussian(key_list[4], (LAYERS, D, KV_HEADS * HEAD_DIM), D ** -0.5, 0.1875, ((0, 2),))
    w_value = gaussian(key_list[5], (LAYERS, D, KV_HEADS * HEAD_DIM), D ** -0.5, 0.1875, ((0, 2),))
    w_out = gaussian(key_list[6], (LAYERS, D, D), HEAD_DIM ** -0.5, 0.75, ((0, 2),))
    gain_moe = jnp.clip(1.0 + 0.1 * jax.random.normal(key_list[7], (LAYERS, D), jnp.float32), 0.5, 1.5)
    w_router = gaussian(key_list[8], (LAYERS, D, EXPERTS), (4 * D) ** -0.5, 0.09375, ((0, 2),))
    w_gate = gaussian(key_list[9], (LAYERS, EXPERTS, D, FF), D ** -0.5, 0.1875, ((0, 2), (1, 4)))
    w_up = gaussian(key_list[10], (LAYERS, EXPERTS, D, FF), D ** -0.5, 0.1875, ((0, 2), (1, 4)))
    w_down = gaussian(key_list[11], (LAYERS, EXPERTS, FF, D), (FF // 8) ** -0.5, 0.75, ((0, 2), (1, 4)))
    doc_lengths = draw_doc_lengths(jax.random.fold_in(key_list[14], 71), 0)
    routes = distinct(key_list[13], LAYERS * MB * SEQS * SEQ, EXPERTS, TOPK, 2048).reshape((LAYERS, MB, SEQS, SEQ, TOPK))
    return {"inputs": inputs, "cotangent": cotangent, "gain_attn": gain_attn, "w_query": w_query, "w_key": w_key, "w_value": w_value, "w_out": w_out, "gain_moe": gain_moe, "w_router": w_router, "w_gate": w_gate, "w_up": w_up, "w_down": w_down, "doc_lengths": doc_lengths, "routes": routes}


epsilon = 1e-06
highest = lax.Precision.HIGHEST

@jax.custom_vjp
def low(v):
    return lax.optimization_barrier(v.astype(jnp.bfloat16)).astype(jnp.float32)

@jax.custom_vjp
def low_back(v):
    return v

def low_keep(v):
    return (low(v), None)

def low_pass(kept, grad):
    return (grad,)

def back_keep(v):
    return (v, None)

def back_low(kept, grad):
    return (low(grad),)
low.defvjp(low_keep, low_pass)
low_back.defvjp(back_keep, back_low)

def matmul(left, right):
    return jnp.dot(left, right, precision=highest, preferred_element_type=jnp.float32)

def rms_scale(values):
    return lax.rsqrt(lax.optimization_barrier(jnp.mean(values * values, axis=-1, keepdims=True)) + epsilon)

def rope_tables(positions):
    half_dim = HEAD_DIM // 2
    inverse = 10000.0 ** (-(jnp.arange(half_dim, dtype=jnp.float32) * (2.0 / HEAD_DIM)))
    angles = positions.astype(jnp.float32)[:, None] * inverse[None, :]
    return (jnp.cos(angles), jnp.sin(angles))

def rotate(vectors, cosine, sine):
    half_dim = HEAD_DIM // 2
    first = vectors[..., :half_dim]
    second = vectors[..., half_dim:]
    cosine = cosine[:, None, :]
    sine = sine[:, None, :]
    return jnp.concatenate([first * cosine - second * sine, second * cosine + first * sine], axis=-1)

def doc_ids(lengths, positions):
    endings = jnp.cumsum(lengths)
    return lax.optimization_barrier(jnp.sum((positions[:, None] >= endings[None, :]).astype(jnp.int32), axis=1))

def slot_table(chosen, usable, capacity):
    experts_iota = jnp.arange(EXPERTS, dtype=jnp.int32)
    onehot = ((chosen[:, :, None] == experts_iota[None, None, :]) & usable[:, None, None]).astype(jnp.int32)
    flat_hot = onehot.reshape(-1, EXPERTS)
    ranking = jnp.cumsum(flat_hot, axis=0) - 1
    placed = lax.optimization_barrier(jnp.sum(ranking * flat_hot, axis=1)).reshape(chosen.shape)
    retained = usable[:, None] & (placed < capacity)
    slot_index = jnp.where(retained, chosen * capacity + placed, EXPERTS * capacity)
    return (slot_index.astype(jnp.int32), retained)

def attention(query, key_rows, value_rows, positions, documents):
    group_size = HEADS // KV_HEADS
    block_rows = min(512, SEQ)
    block_count = SEQ // block_rows
    query_blocks = query.reshape(block_count, block_rows, KV_HEADS, group_size, HEAD_DIM)
    place_blocks = positions.reshape(block_count, block_rows)
    doc_blocks = documents.reshape(block_count, block_rows)

    def one_block(pieces):
        query_part, place_part, doc_part = pieces
        scores = jnp.einsum('qhgd,khd->hgqk', query_part, key_rows, precision=highest) * HEAD_DIM ** (-0.5)
        scores = low_back(scores)
        distance = place_part[:, None] - positions[None, :]
        allowed = (distance >= 0) & (distance < WINDOW) & (doc_part[:, None] == documents[None, :])
        scores = jnp.where(allowed[None, None], scores, -1e+30)
        weights = jax.nn.softmax(scores, axis=-1)
        mixed = jnp.einsum('hgqk,khd->qhgd', low(weights), value_rows, precision=highest)
        return mixed.reshape(block_rows, HEADS * HEAD_DIM)
    result = lax.map(jax.checkpoint(one_block), (query_blocks, place_blocks, doc_blocks))
    return result.reshape(SEQ, HEADS * HEAD_DIM)

def layer(hidden_in, params, lengths, chosen):
    gain_attn, w_query, w_key, w_value, w_out, gain_moe, w_router, w_gate, w_up, w_down = params
    group_size = HEADS // KV_HEADS
    positions = jnp.arange(SEQ, dtype=jnp.int32)
    documents = doc_ids(lengths, positions)
    cosine, sine = rope_tables(positions)
    normed = low(hidden_in * rms_scale(hidden_in) * gain_attn)
    query = low(rotate(low_back(matmul(normed, w_query)).reshape(SEQ, HEADS, HEAD_DIM), cosine, sine))
    key_rows = low(rotate(low_back(matmul(normed, w_key)).reshape(SEQ, KV_HEADS, HEAD_DIM), cosine, sine))
    value_rows = low(low_back(matmul(normed, w_value))).reshape(SEQ, KV_HEADS, HEAD_DIM)
    query = query.reshape(SEQ, KV_HEADS, group_size, HEAD_DIM)
    mixed = low(low_back(attention(query, key_rows, value_rows, positions, documents)))
    middle = hidden_in + low_back(matmul(mixed, w_out))
    routed_in = low(middle * rms_scale(middle) * gain_moe)
    logits = matmul(routed_in, w_router)
    gates = jax.nn.softmax(jnp.take_along_axis(logits, chosen, axis=1), axis=-1)
    usable = documents < NDOC
    slot_index, retained = jax.vmap(lambda c, u: slot_table(c, u, CAP))(chosen.reshape(N_EXPERT, SEQ_DEV, TOPK), usable.reshape(N_EXPERT, SEQ_DEV))

    def fill(block_in, block_slots):
        buffer = jnp.zeros((EXPERTS * CAP + 1, D), jnp.float32)
        return buffer.at[block_slots.reshape(-1)].add(jnp.repeat(block_in, TOPK, axis=0))[:EXPERTS * CAP]
    buffers = jax.vmap(fill)(routed_in.reshape(N_EXPERT, SEQ_DEV, D), slot_index)
    buffers = buffers.reshape(N_EXPERT, EXPERTS, CAP, D).transpose(1, 0, 2, 3).reshape(EXPERTS, N_EXPERT * CAP, D)
    buffers = low_back(buffers)
    gate_pre = low_back(jnp.einsum('erd,edf->erf', buffers, w_gate, precision=highest))
    up_pre = low_back(jnp.einsum('erd,edf->erf', buffers, w_up, precision=highest))
    activated = low(jax.nn.silu(gate_pre) * up_pre)
    produced = low(low_back(jnp.einsum('erf,efd->erd', activated, w_down, precision=highest)))
    produced = produced.reshape(EXPERTS, N_EXPERT, CAP, D).transpose(1, 0, 2, 3).reshape(N_EXPERT, EXPERTS * CAP, D)
    produced = jnp.concatenate([produced, jnp.zeros((N_EXPERT, 1, D), jnp.float32)], axis=1)
    fetched = jax.vmap(lambda p, s: p[s])(produced, slot_index)
    weighting = gates.reshape(N_EXPERT, SEQ_DEV, TOPK) * retained
    mixture = lax.optimization_barrier(jnp.sum(weighting[..., None] * fetched, axis=2)).reshape(SEQ, D)
    return middle + mixture

def reference(inputs, cotangent, gain_attn, w_query, w_key, w_value, w_out, gain_moe, w_router, w_gate, w_up, w_down, doc_lengths, routes):
    weights = tuple((w.astype(jnp.float32) for w in (gain_attn, w_query, w_key, w_value, w_out, gain_moe, w_router, w_gate, w_up, w_down)))
    first_params = tuple((w[0] for w in weights))
    second_params = tuple((w[1] for w in weights))
    lengths_flat = doc_lengths.reshape(MB * SEQS, NDOC)

    def section_pass(activations, params, layer_id):
        chosen_flat = routes[layer_id].reshape(MB * SEQS, SEQ, TOPK)

        def per_sequence(pieces):
            return layer(pieces[0], params, pieces[1], pieces[2])
        result = lax.map(jax.checkpoint(per_sequence), (activations.reshape(MB * SEQS, SEQ, D), lengths_flat, chosen_flat))
        return result.reshape(MB, SEQS, SEQ, D)

    def forward(start, probe, params_one, params_two):
        between = low(low_back(section_pass(start, params_one, 0) + probe))
        final = section_pass(between, params_two, 1)
        return (between, final)
    start = inputs.astype(jnp.float32)
    probe = jnp.zeros_like(start)
    (between, final), pullback = jax.vjp(forward, start, probe, first_params, second_params)
    grad_start, grad_probe, grads_one, grads_two = pullback((jnp.zeros_like(between), cotangent.astype(jnp.float32)))
    stacked = [jnp.stack([a, b]) for a, b in zip(grads_one, grads_two)]
    layer_outputs = jnp.stack([between, final]).astype(jnp.bfloat16)
    input_grads = jnp.stack([grad_start, grad_probe]).astype(jnp.bfloat16)
    return (layer_outputs, input_grads, stacked[0], stacked[1], stacked[2], stacked[3], stacked[4], stacked[5], stacked[6], stacked[7], stacked[8], stacked[9])
```

```python
import functools

import jax
import jax.numpy as jnp
from jax import lax
from jax.experimental import pallas as pl
from jax.experimental.pallas import tpu as pltpu
from jax.sharding import PartitionSpec as P

HEADS = 16
KV_HEADS = 8
HEAD_DIM = 64
EXPERTS = 32
TOPK = 8
WINDOW = 512
NDOC = 4
EPSILON = 1e-06
MASKED = -1e30
LANES = 128
VMEM_BYTES = 56 * 1024 * 1024
bf16 = jnp.bfloat16
f32 = jnp.float32


def shifted(value, axis, steps, sources=None):
    count = lax.axis_size(axis)
    initial, last = (max(0, -steps), min(count, count - steps))
    names = range(initial, last) if sources is None else sources
    return lax.ppermute(value, axis, [(source, source + steps) for source in names])


def swapped(value, axis, bit):
    count = lax.axis_size(axis)
    return lax.ppermute(value, axis, [(source, source ^ bit) for source in range(count)])


def line_gather(block):
    ups, downs = [], []
    up, down = block, block
    for _ in range(lax.axis_size("expert") - 1):
        up = shifted(up, "expert", 1)
        down = shifted(down, "expert", -1)
        ups.append(up)
        downs.append(down)
    return ups, downs


def line_reduce(parts):
    ranks = lax.axis_size("expert")
    me = lax.axis_index("expert")

    def pick(index):
        return lax.dynamic_index_in_dim(parts, jnp.clip(index, 0, ranks - 1), 0, False)

    up = down = None
    for step in range(1, ranks):
        up_part = pick(me + ranks - step)
        down_part = pick(me - ranks + step)
        up = up_part if up is None else (up.astype(f32) + up_part.astype(f32)).astype(bf16)
        down = down_part if down is None else (down.astype(f32) + down_part.astype(f32)).astype(bf16)
        up = shifted(up, "expert", 1, range(0, step))
        down = shifted(down, "expert", -1, range(ranks - step, ranks))
    return pick(me).astype(f32) + up.astype(f32) + down.astype(f32)


def dp_bits():
    bits, bit = [], 1
    while bit < lax.axis_size("dp"):
        bits.append(bit)
        bit *= 2
    return bits


def fetch_pieces(piece):
    pieces = {0: swapped(piece, "section", 1)}
    for bit in reversed(dp_bits()):
        for k in list(pieces):
            pieces[k | bit] = swapped(pieces[k], "dp", bit)
    return [pieces[k] for k in range(len(pieces))]


def dp_reduce(keep, send):
    for bit in dp_bits():
        total = (keep.astype(f32) + swapped(send, "dp", bit).astype(f32)).astype(bf16)
        if total.shape[0] > 1:
            keep, send = total[0::2], total[1::2]
    return total[0]


def to_owner(value, layer):
    return lax.ppermute(value, "section", [(1 - layer, layer)])


def call(kernel, out_shape, in_specs, out_specs, scratch, grid=None, flops=0, bytes_accessed=0, name=None):
    extra = {} if grid is None else {"grid": grid}
    return pl.pallas_call(
        kernel,
        out_shape=out_shape,
        in_specs=in_specs,
        out_specs=out_specs,
        scratch_shapes=scratch,
        compiler_params=pltpu.CompilerParams(vmem_limit_bytes=VMEM_BYTES),
        cost_estimate=pl.CostEstimate(flops=flops, bytes_accessed=bytes_accessed, transcendentals=0),
        name=name,
        **extra,
    )


SMEM = pl.BlockSpec(memory_space=pltpu.SMEM)
VMEM = pl.BlockSpec(memory_space=pltpu.VMEM)
ANY = pl.BlockSpec(memory_space=pl.ANY)


def struct(shape, dtype):
    return jax.ShapeDtypeStruct(shape, dtype)


def dot(left, right, left_dim=1, right_dim=0):
    return lax.dot_general(left, right, (((left_dim,), (right_dim,)), ((), ())), preferred_element_type=f32)


def upper_lanes(shape):
    return lax.broadcasted_iota(jnp.int32, shape, 1) % LANES >= HEAD_DIM


def half_swap(tile):
    lane = lax.broadcasted_iota(jnp.int32, tile.shape, 1)
    half = HEAD_DIM // 2
    return jnp.where(
        lane % HEAD_DIM < half, pltpu.roll(tile, LANES - half, 1), pltpu.roll(tile, half, 1)
    )


def load_dense(info, owns, pieces, first, width, target, sem):
    rows = target.shape[0] // len(pieces)

    @pl.when(info[0] == 1)
    def _():
        start = 0
        for own in owns:
            size = own.shape[1]
            pltpu.make_async_copy(own, target.at[:, pl.ds(start, size)], sem).start()
            start += size

    @pl.when(info[0] == 0)
    def _():
        for k, piece in enumerate(pieces):
            place = pl.multiple_of((info[1] ^ k) * rows, rows)
            pltpu.make_async_copy(
                piece.at[:, pl.ds(first, width)], target.at[pl.ds(place, rows), :], sem
            ).start()


def wait_dense(target, sem):
    pltpu.make_async_copy(target, target, sem).wait()


def load_experts(info, owns, chunks, expert, slot, buffers, sems):
    gate_buf, up_buf, down_buf = buffers
    per_chunk = chunks[0][0].shape[0]
    pieces = len(chunks[0])
    wide = gate_buf.shape[1] // pieces
    narrow = down_buf.shape[1] // pieces
    half = down_buf.shape[2] // 2

    @pl.when(info[0] == 1)
    def _():
        for own, buf, index in zip(owns, buffers, range(3)):
            pltpu.make_async_copy(own.at[expert], buf.at[slot], sems.at[slot, index]).start()

    for c, chunk in enumerate(chunks):

        @pl.when((info[0] == 0) & (expert // per_chunk == c))
        def _():
            local = expert - c * per_chunk
            for k, piece in enumerate(chunk):
                owner = info[1] ^ k
                row = pl.multiple_of(owner * wide, wide)
                low = pl.multiple_of(owner * narrow, narrow)
                pltpu.make_async_copy(
                    piece.at[local, pl.ds(0, wide)], gate_buf.at[slot, pl.ds(row, wide)], sems.at[slot, 0]
                ).start()
                pltpu.make_async_copy(
                    piece.at[local, pl.ds(wide, wide)], up_buf.at[slot, pl.ds(row, wide)], sems.at[slot, 1]
                ).start()
                for side in range(2):
                    pltpu.make_async_copy(
                        piece.at[local, pl.ds(2 * wide + side * narrow, narrow)],
                        down_buf.at[slot, pl.ds(low, narrow), pl.ds(side * half, half)],
                        sems.at[slot, 2],
                    ).start()


def wait_experts(slot, index, buffers, sems):
    pltpu.make_async_copy(buffers[index].at[slot], buffers[index].at[slot], sems.at[slot, index]).wait()


def load_line(info, own, ups, downs, target, sem):
    ranks = target.shape[0]
    me = info[2]
    pltpu.make_async_copy(own, target.at[me], sem).start()
    for s in range(1, ranks):

        @pl.when(me >= s)
        def _():
            pltpu.make_async_copy(ups[s - 1], target.at[me - s], sem).start()

        @pl.when(me < s)
        def _():
            pltpu.make_async_copy(downs[ranks - s - 1], target.at[me - s + ranks], sem).start()


def wait_line(target, sem):
    pltpu.make_async_copy(target, target, sem).wait()


def write_pieces(info, value, keep, send, place):
    pieces = 2 * keep.shape[0]
    rows = value.shape[0] // pieces
    for p in range(pieces):
        k = info[1] ^ p
        part = value[p * rows : (p + 1) * rows].astype(keep.dtype)

        @pl.when(k % 2 == 0)
        def _():
            keep[(k // 2,) + place] = part

        @pl.when(k % 2 == 1)
        def _():
            send[(k // 2,) + place] = part


def rms(values):
    return lax.rsqrt(jnp.mean(values * values, axis=-1, keepdims=True) + EPSILON)


def mask_bias(info, query_docs, key_docs, bias):
    rows, keys = bias.shape
    row = lax.broadcasted_iota(jnp.int32, (rows, keys), 0)
    col = lax.broadcasted_iota(jnp.int32, (rows, keys), 1)
    distance = row + (keys - rows) - col
    allowed = (distance >= 0) & (distance < WINDOW) & (query_docs[...] == key_docs[...])
    bias[...] = jnp.where(allowed, 0.0, MASKED)


def load_keys(own, earlier, target, sem):
    rows = own.shape[0]
    reach = len(earlier)
    pltpu.make_async_copy(own, target.at[pl.ds(reach * rows, rows)], sem).start()
    for s, part in enumerate(earlier):
        pltpu.make_async_copy(part, target.at[pl.ds((reach - 1 - s) * rows, rows)], sem).start()


def doubled(pair, which):
    wide = pair.astype(f32)
    turned = pltpu.roll(wide, HEAD_DIM, 1)
    upper = upper_lanes(wide.shape)
    picked = jnp.where(upper, turned, wide) if which == 0 else jnp.where(upper, wide, turned)
    return picked.astype(bf16)


def one_head(tile, which, upper):
    return jnp.where(upper, tile, 0.0) if which == 1 else jnp.where(upper, 0.0, tile)


def project_kernel(pieces, info, x, gain, cosine, sine, w_query, w_key, w_value, *rest):
    parts = rest[:pieces]
    query, keyval, weights, sem = rest[pieces:]
    width = weights.shape[1]
    load_dense(info, (w_query, w_key, w_value), parts, 0, width, weights, sem)
    hidden = x[...].astype(f32)
    normed = (hidden * rms(hidden) * gain[...]).astype(bf16)
    wait_dense(weights, sem)
    q_width, k_width = w_query.shape[1], w_key.shape[1]
    cos, sin = cosine[...], sine[...]
    step = 2 * LANES
    for begin in range(0, width, step):
        product = dot(normed, weights[:, begin : begin + step])
        for inner in range(0, step, LANES):
            tile = product[:, inner : inner + LANES]
            place = begin + inner
            if place < q_width + k_width:
                tile = tile * cos + half_swap(tile) * sin
            if place < q_width:
                query[:, place : place + LANES] = tile.astype(bf16)
            else:
                place -= q_width
                keyval[:, place : place + LANES] = tile.astype(bf16)


def attend_kernel(pieces, reach, info, query, own_kv, *rest):
    earlier = rest[:reach]
    query_docs, key_docs, x, gain, w_out = rest[reach : reach + 5]
    parts = rest[reach + 5 : reach + 5 + pieces]
    mixed, log_total, middle, routed = rest[reach + 5 + pieces : reach + 9 + pieces]
    keyval, bias, weights, kv_sem, w_sem = rest[reach + 9 + pieces :]
    load_keys(own_kv, earlier, keyval, kv_sem)
    first = 2 * x.shape[1]
    load_dense(info, (w_out,), parts, first, x.shape[1], weights, w_sem)
    mask_bias(info, query_docs, key_docs, bias)
    log_total[...] = jnp.zeros_like(log_total)
    pltpu.make_async_copy(keyval, keyval, kv_sem).wait()
    kv_width = KV_HEADS * HEAD_DIM
    rows = query.shape[0]
    upper = upper_lanes((rows, LANES))
    lane = lax.broadcasted_iota(jnp.int32, (rows, LANES), 1)

    @pl.loop(0, KV_HEADS // 2)
    def _(pair):
        k_pair = keyval[:, pl.ds(pl.multiple_of(pair * LANES, LANES), LANES)]
        v_pair = keyval[:, pl.ds(pl.multiple_of(kv_width + pair * LANES, LANES), LANES)]
        for head in range(2):
            keys, values = doubled(k_pair, head), doubled(v_pair, head)
            place = pl.multiple_of((pair * 2 + head) * LANES, LANES)
            tile = query[:, pl.ds(place, LANES)].astype(f32) * HEAD_DIM ** (-0.5)
            results = []
            for g in range(2):
                scores = dot(one_head(tile, g, upper).astype(bf16), keys, 1, 1) + bias[...]
                peak = jnp.max(scores, axis=1, keepdims=True)
                expo = jnp.exp(scores - peak)
                total = jnp.sum(expo, axis=1, keepdims=True)
                results.append(dot(expo.astype(bf16), values) * (1.0 / total))
                index = (pair * 2 + head) * 2 + g
                log_total[...] = jnp.where(lane == index, peak + jnp.log(total), log_total[...])
            mixed[:, pl.ds(place, LANES)] = jnp.where(upper, results[1], results[0]).astype(bf16)

    wait_dense(weights, w_sem)
    between = x[...].astype(f32) + dot(mixed[...], weights[...])
    middle[...] = between
    routed[...] = (between * rms(between) * gain[...]).astype(bf16)


def attend_back_kernel(pieces, reach, info, d_routed, grad, middle, gain, mixed, query, log_total, own_kv, *rest):
    earlier = rest[:reach]
    query_docs, key_docs, cosine, sine, w_out = rest[reach : reach + 5]
    rest = rest[reach + 5 :]
    parts = rest[:pieces]
    rest = rest[pieces:]
    d_middle, d_query, d_own = rest[:3]
    d_earlier = rest[3 : 3 + reach]
    keep, send, grad_gain = rest[3 + reach : 6 + reach]
    keyval, bias, weights, d_mixed, d_kv, kv_sem, w_sem = rest[6 + reach :]
    load_keys(own_kv, earlier, keyval, kv_sem)
    first = 2 * middle.shape[1]
    load_dense(info, (w_out,), parts, first, middle.shape[1], weights, w_sem)
    mask_bias(info, query_docs, key_docs, bias)
    between = middle[...]
    scale = rms(between)
    normal = between * scale
    routed = d_routed[...]
    grad_gain[...] = jnp.sum(routed * normal, axis=0, keepdims=True)
    d_norm = routed * gain[...]
    total = grad[...].astype(f32) + scale * (
        d_norm - normal * jnp.mean(d_norm * normal, axis=1, keepdims=True)
    )
    d_middle[...] = total
    branch = total.astype(bf16)
    wait_dense(weights, w_sem)
    d_mixed[...] = dot(branch, weights[...], 1, 1).astype(bf16)
    write_pieces(info, dot(mixed[...], branch, 0, 0), keep, send, ())
    pltpu.make_async_copy(keyval, keyval, kv_sem).wait()
    kv_width = KV_HEADS * HEAD_DIM
    rows = query.shape[0]
    upper = upper_lanes((rows, LANES))
    lane = lax.broadcasted_iota(jnp.int32, (rows, LANES), 1)
    cos, sin = cosine[...], sine[...]

    @pl.loop(0, KV_HEADS // 2)
    def _(pair):
        k_pair = keyval[:, pl.ds(pl.multiple_of(pair * LANES, LANES), LANES)]
        v_pair = keyval[:, pl.ds(pl.multiple_of(kv_width + pair * LANES, LANES), LANES)]
        for head in range(2):
            keys, values = doubled(k_pair, head), doubled(v_pair, head)
            place = pl.multiple_of((pair * 2 + head) * LANES, LANES)
            tile = query[:, pl.ds(place, LANES)].astype(f32) * HEAD_DIM ** (-0.5)
            d_tile = d_mixed[:, pl.ds(place, LANES)].astype(f32)
            inner = d_tile * mixed[:, pl.ds(place, LANES)].astype(f32)
            dq, dk, dv = [], None, None
            for g in range(2):
                index = (pair * 2 + head) * 2 + g
                log_column = jnp.sum(jnp.where(lane == index, log_total[...], 0.0), axis=1, keepdims=True)
                weight = jnp.sum(one_head(inner, g, upper), axis=1, keepdims=True)
                own_query = one_head(tile, g, upper).astype(bf16)
                own_grad = one_head(d_tile, g, upper).astype(bf16)
                scores = dot(own_query, keys, 1, 1) + bias[...]
                probs = jnp.exp(scores - log_column)
                d_probs = dot(own_grad, values, 1, 1)
                d_scores = (probs * (d_probs - weight)).astype(bf16)
                dq.append(dot(d_scores, keys))
                k_term = dot(own_query, d_scores, 0, 0)
                v_term = dot(own_grad, probs.astype(bf16), 0, 0)
                dk = k_term if dk is None else dk + k_term
                dv = v_term if dv is None else dv + v_term
            whole = jnp.where(upper, dq[1], dq[0]) * HEAD_DIM ** (-0.5)
            whole = whole * cos - half_swap(whole) * sin
            d_query[:, pl.ds(place, LANES)] = whole.astype(bf16)
            k_row = pl.multiple_of((pair * 2 + head) * HEAD_DIM, HEAD_DIM)
            v_row = pl.multiple_of(kv_width + (pair * 2 + head) * HEAD_DIM, HEAD_DIM)
            d_kv[pl.ds(k_row, HEAD_DIM), :] = dk[:HEAD_DIM] + dk[HEAD_DIM:]
            d_kv[pl.ds(v_row, HEAD_DIM), :] = dv[:HEAD_DIM] + dv[HEAD_DIM:]

    for block in range(reach + 1):
        turned = d_kv[:, block * rows : (block + 1) * rows].T
        if block == reach:
            d_own[...] = turned
        else:
            d_earlier[reach - 1 - block][...] = turned.astype(bf16)


def query_back_kernel(pieces, info, x, gain, d_query, w_query, *rest):
    parts = rest[:pieces]
    d_normed, keep, send, weights, sem = rest[pieces:]
    load_dense(info, (w_query,), parts, 0, weights.shape[1], weights, sem)
    hidden = x[...].astype(f32)
    normed = (hidden * rms(hidden) * gain[...]).astype(bf16)
    write_pieces(info, dot(normed, d_query[...], 0, 0), keep, send, ())
    wait_dense(weights, sem)
    d_normed[...] = dot(d_query[...], weights[...], 1, 1)


def keyval_back_kernel(pieces, info, x, gain, d_own, d_others, d_normed, d_middle, cosine, sine, w_key, w_value, *rest):
    parts = rest[:pieces]
    d_x, keep, send, grad_gain, weights, d_pre, sem = rest[pieces:]
    load_dense(info, (w_key, w_value), parts, x.shape[1], weights.shape[1], weights, sem)
    hidden = x[...].astype(f32)
    scale = rms(hidden)
    normal = hidden * scale
    normed = (normal * gain[...]).astype(bf16)
    cos, sin = cosine[...], sine[...]
    width = w_key.shape[1]
    for place in range(0, 2 * width, LANES):
        tile = d_own[:, place : place + LANES] + d_others[:, place : place + LANES].astype(f32)
        if place < width:
            tile = tile * cos - half_swap(tile) * sin
        d_pre[:, place : place + LANES] = tile.astype(bf16)
    wait_dense(weights, sem)
    total = d_normed[...] + dot(d_pre[...], weights[...], 1, 1)
    grad_gain[...] = jnp.sum(total * normal, axis=0, keepdims=True)
    d_norm = total * gain[...]
    d_x[...] = (
        d_middle[...]
        + scale * (d_norm - normal * jnp.mean(d_norm * normal, axis=1, keepdims=True))
    ).astype(bf16)
    write_pieces(info, dot(normed, d_pre[...], 0, 0), keep, send, ())


def slot_rows(info, table, local, experts_here):
    row = lax.broadcasted_iota(jnp.int32, table.shape, 0)
    picked = jnp.where(row == info[2] * experts_here + local, table, 0.0)
    return jnp.sum(picked, axis=0, keepdims=True)


def slot_hits(codes, capacity):
    slot = lax.broadcasted_iota(jnp.int32, (capacity, codes.shape[1]), 0).astype(f32)
    return slot == codes


def experts_kernel(pieces, ranks, chunk_count, info, own, *rest):
    ups, downs = rest[: ranks - 1], rest[ranks - 1 : 2 * ranks - 2]
    rest = rest[2 * ranks - 2 :]
    routes, usable, router, w_gate, w_up, w_down = rest[:6]
    rest = rest[6:]
    chunks = [rest[c * pieces : (c + 1) * pieces] for c in range(chunk_count)]
    rest = rest[chunk_count * pieces :]
    sums, everyone, rows, gates, codes, gate_out, up_out = rest[:7]
    hits, results, gate_buf, up_buf, down_buf, sems, line_sem = rest[7:]
    expert, count = pl.program_id(0), pl.num_programs(0)
    buffers = (gate_buf, up_buf, down_buf)
    owns = (w_gate, w_up, w_down)
    experts_here = w_gate.shape[0]
    tokens = own.shape[0]
    capacity = tokens * TOPK // EXPERTS
    slot = expert % 2

    @pl.when(expert == 0)
    def _():
        load_line(info, own, ups, downs, everyone, line_sem)
        load_experts(info, owns, chunks, 0, 0, buffers, sems)
        earlier = lax.broadcasted_iota(jnp.int32, (tokens, tokens), 0)
        later = lax.broadcasted_iota(jnp.int32, (tokens, tokens), 1)
        triangle = jnp.where(earlier < later, 1.0, 0.0).astype(bf16)
        number = lax.broadcasted_iota(jnp.int32, (EXPERTS, tokens), 0)
        wait_line(everyone, line_sem)
        for block in range(ranks):
            span = slice(block * tokens, (block + 1) * tokens)
            named = routes[0:1, span] == number
            for k in range(1, TOPK):
                named = named | (routes[k : k + 1, span] == number)
            logits = jnp.where(named, dot(router[...], everyone[block], 1, 1), MASKED)
            expo = jnp.where(named, jnp.exp(logits - jnp.max(logits, axis=0, keepdims=True)), 0.0)
            weight = expo / jnp.sum(expo, axis=0, keepdims=True)
            held = named & (usable[:, span] > 0)
            rank = dot(jnp.where(held, 1.0, 0.0).astype(bf16), triangle)
            code = jnp.where(held & (rank < capacity), rank, -1.0)
            gates[block] = weight
            codes[block] = code
            for e in range(experts_here):
                hit = slot_hits(slot_rows(info, code, e, experts_here), capacity)
                hits[block, e * capacity : (e + 1) * capacity, :] = jnp.where(hit, 1.0, 0.0).astype(bf16)
            rows[block] = dot(hits[block], everyone[block]).astype(bf16)

    @pl.when(expert + 1 < count)
    def _():
        load_experts(info, owns, chunks, expert + 1, 1 - slot, buffers, sems)

    place = pl.multiple_of(expert * capacity, capacity)
    mine = jnp.concatenate([rows[block, pl.ds(place, capacity), :] for block in range(ranks)], axis=0)
    wait_experts(slot, 0, buffers, sems)
    gate_pre = dot(mine, gate_buf[slot])
    wait_experts(slot, 1, buffers, sems)
    up_pre = dot(mine, up_buf[slot])
    gate_out[0] = gate_pre.astype(bf16)
    up_out[0] = up_pre.astype(bf16)
    activated = (gate_pre * jax.nn.sigmoid(gate_pre) * up_pre).astype(bf16)
    wait_experts(slot, 2, buffers, sems)
    produced = dot(activated, down_buf[slot]).astype(bf16)
    for block in range(ranks):
        results[block, pl.ds(place, capacity), :] = produced[block * capacity : (block + 1) * capacity]

    @pl.when(expert + 1 == count)
    def _():
        for block in range(ranks):
            weighted = []
            for e in range(experts_here):
                weight = slot_rows(info, gates[block], e, experts_here)
                hit = hits[block, e * capacity : (e + 1) * capacity, :].astype(f32)
                weighted.append((hit * weight).astype(bf16))
            sums[block] = dot(jnp.concatenate(weighted, axis=0), results[block], 0, 0).astype(bf16)


def experts_back_kernel(pieces, ranks, chunk_count, info, own, *rest):
    ups, downs = rest[: ranks - 1], rest[ranks - 1 : 2 * ranks - 2]
    rest = rest[2 * ranks - 2 :]
    everyone, gates, codes, router, gate_pre, up_pre, w_gate, w_up, w_down = rest[:9]
    rest = rest[9:]
    chunks = [rest[c * pieces : (c + 1) * pieces] for c in range(chunk_count)]
    rest = rest[chunk_count * pieces :]
    sums, grad_router, grad_rows, gate_out, up_out, active_out = rest[:6]
    incoming, hits, columns, d_gates, d_rows, gate_buf, up_buf, down_buf, sems, line_sem = rest[6:]
    expert, count = pl.program_id(0), pl.num_programs(0)
    buffers = (gate_buf, up_buf, down_buf)
    owns = (w_gate, w_up, w_down)
    experts_here = w_gate.shape[0]
    tokens = own.shape[0]
    capacity = tokens * TOPK // EXPERTS
    slot = expert % 2

    @pl.when(expert == 0)
    def _():
        load_line(info, own, ups, downs, incoming, line_sem)
        load_experts(info, owns, chunks, 0, 0, buffers, sems)
        for block in range(ranks):
            for e in range(experts_here):
                hit = slot_hits(slot_rows(info, codes[block], e, experts_here), capacity)
                span = slice(e * capacity, (e + 1) * capacity)
                hits[block, span, :] = jnp.where(hit, 1.0, 0.0).astype(bf16)
                weight = slot_rows(info, gates[block], e, experts_here)
                column = jnp.sum(jnp.where(hit, weight, 0.0), axis=1, keepdims=True)
                columns[block, span, :] = jnp.broadcast_to(column, (capacity, LANES))
        wait_line(incoming, line_sem)
        for block in range(ranks):
            grad_rows[block] = dot(hits[block], incoming[block]).astype(bf16)

    @pl.when(expert + 1 < count)
    def _():
        load_experts(info, owns, chunks, expert + 1, 1 - slot, buffers, sems)

    place = pl.multiple_of(expert * capacity, capacity)
    mine = jnp.concatenate([grad_rows[block, pl.ds(place, capacity), :] for block in range(ranks)], axis=0)
    weight = jnp.concatenate(
        [columns[block, pl.ds(place, capacity), :] for block in range(ranks)], axis=0
    )[:, :1]
    gate = gate_pre[0].astype(f32)
    up = up_pre[0].astype(f32)
    sigma = jax.nn.sigmoid(gate)
    silu = gate * sigma
    activated = silu * up
    wait_experts(slot, 2, buffers, sems)
    unweighted = dot(mine, down_buf[slot], 1, 1)
    d_weight = jnp.sum(unweighted * activated, axis=1, keepdims=True)
    for block in range(ranks):
        hit = hits[block, pl.ds(place, capacity), :].astype(f32)
        spread = hit * d_weight[block * capacity : (block + 1) * capacity]
        d_gates[block, pl.ds(expert, 1), :] = jnp.sum(spread, axis=0, keepdims=True)
    d_active = unweighted * weight
    active_out[0] = (activated * weight).astype(bf16)
    d_gate = (d_active * up * sigma * (1.0 + gate * (1.0 - sigma))).astype(bf16)
    d_up = (d_active * silu).astype(bf16)
    gate_out[0] = d_gate
    up_out[0] = d_up
    wait_experts(slot, 0, buffers, sems)
    wait_experts(slot, 1, buffers, sems)
    produced = (dot(d_gate, gate_buf[slot], 1, 1) + dot(d_up, up_buf[slot], 1, 1)).astype(bf16)
    for block in range(ranks):
        d_rows[block, pl.ds(place, capacity), :] = produced[block * capacity : (block + 1) * capacity]

    @pl.when(expert + 1 == count)
    def _():
        number = lax.broadcasted_iota(jnp.int32, (EXPERTS, tokens), 0)
        router_total = jnp.zeros(grad_router.shape, f32)
        for block in range(ranks):
            weight = gates[block]
            own_grads = jnp.zeros((EXPERTS, tokens), f32)
            for e in range(experts_here):
                here = number == info[2] * experts_here + e
                own_grads = jnp.where(here, d_gates[block, e : e + 1, :], own_grads)
            inner = jnp.sum(weight * own_grads, axis=0, keepdims=True)
            d_logits = (weight * (own_grads - inner)).astype(bf16)
            router_total = router_total + dot(d_logits, everyone[block])
            back = dot(hits[block], d_rows[block], 0, 0) + dot(d_logits, router[...], 0, 0)
            sums[block] = back.astype(bf16)
        grad_router[...] = router_total


def expert_grads_kernel(info, rows, grad_rows, d_gate, d_up, activated, keep, send):
    capacity, width = rows.shape[1], rows.shape[2]
    mine = rows[...].reshape(rows.shape[0] * capacity, width)
    incoming = grad_rows[...].reshape(rows.shape[0] * capacity, width)
    pieces = 2 * keep.shape[0]
    wide = width // pieces
    narrow = activated.shape[2] // pieces
    half = width // 2
    write_pieces(info, dot(mine, d_gate[0], 0, 0), keep, send, (0, slice(0, wide)))
    write_pieces(info, dot(mine, d_up[0], 0, 0), keep, send, (0, slice(wide, 2 * wide)))
    down = dot(activated[0], incoming, 0, 0)
    for side in range(2):
        begin = 2 * wide + side * narrow
        write_pieces(
            info, down[:, side * half : (side + 1) * half], keep, send, (0, slice(begin, begin + narrow))
        )


def layer_forward(x, weights, tables, info, routes):
    (gain_attn, gain_moe, router, owns, dense_parts, expert_parts) = weights
    w_query, w_key, w_value, w_out, w_gate, w_up, w_down = owns
    cosine, sine, query_docs, key_docs, usable, reach = tables
    rows, width = x.shape
    ranks = lax.axis_size("expert")
    pieces = lax.axis_size("dp")
    kv_width = 2 * KV_HEADS * HEAD_DIM
    keys = (reach + 1) * rows
    query, keyval = call(
        functools.partial(project_kernel, pieces),
        (struct((rows, width), bf16), struct((rows, kv_width), bf16)),
        [SMEM] + [VMEM] * 4 + [ANY] * (3 + pieces),
        (VMEM, VMEM),
        [pltpu.VMEM((width, width + kv_width), bf16), pltpu.SemaphoreType.DMA],
        flops=2 * rows * width * (width + kv_width),
        bytes_accessed=2 * width * (width + kv_width),
        name="project",
    )(info, x, gain_attn, cosine, sine, w_query, w_key, w_value, *dense_parts)
    earlier, moving = [], keyval
    for _ in range(reach):
        moving = shifted(moving, "expert", 1)
        earlier.append(moving)
    mixed, log_total, middle, routed = call(
        functools.partial(attend_kernel, pieces, reach),
        (
            struct((rows, width), bf16),
            struct((rows, LANES), f32),
            struct((rows, width), f32),
            struct((rows, width), bf16),
        ),
        [SMEM, VMEM] + [ANY] * (1 + reach) + [VMEM] * 4 + [ANY] * (1 + pieces),
        (VMEM,) * 4,
        [
            pltpu.VMEM((keys, kv_width), bf16),
            pltpu.VMEM((rows, keys), f32),
            pltpu.VMEM((width, width), bf16),
            pltpu.SemaphoreType.DMA,
            pltpu.SemaphoreType.DMA,
        ],
        flops=16 * rows * keys * width,
        bytes_accessed=2 * width * width,
        name="attend",
    )(info, query, keyval, *earlier, query_docs, key_docs, x, gain_moe, w_out, *dense_parts)
    ups, downs = line_gather(routed)
    experts_here, _, hidden = w_gate.shape
    capacity = rows * TOPK // EXPERTS
    slots = experts_here * capacity
    sums, everyone, expert_rows, gates, codes, gate_pre, up_pre = call(
        functools.partial(experts_kernel, pieces, ranks, len(expert_parts)),
        (
            struct((ranks, rows, width), bf16),
            struct((ranks, rows, width), bf16),
            struct((ranks, slots, width), bf16),
            struct((ranks, EXPERTS, rows), f32),
            struct((ranks, EXPERTS, rows), f32),
            struct((experts_here, ranks * capacity, hidden), bf16),
            struct((experts_here, ranks * capacity, hidden), bf16),
        ),
        [SMEM] + [ANY] * (2 * ranks - 1) + [VMEM] * 3 + [ANY] * (3 + pieces * len(expert_parts)),
        (VMEM,) * 5
        + (pl.BlockSpec((1, ranks * capacity, hidden), lambda e: (e, 0, 0)),) * 2,
        [
            pltpu.VMEM((ranks, slots, rows), bf16),
            pltpu.VMEM((ranks, slots, width), bf16),
            pltpu.VMEM((2, width, hidden), bf16),
            pltpu.VMEM((2, width, hidden), bf16),
            pltpu.VMEM((2, hidden, width), bf16),
            pltpu.SemaphoreType.DMA((2, 3)),
            pltpu.SemaphoreType.DMA,
        ],
        grid=(experts_here,),
        flops=6 * experts_here * ranks * capacity * width * hidden,
        bytes_accessed=6 * experts_here * width * hidden,
        name="experts",
    )(
        info, routed, *ups, *downs, routes, usable, router, w_gate, w_up, w_down,
        *[piece for chunk in expert_parts for piece in chunk],
    )
    result = (middle + line_reduce(sums)).astype(bf16)
    kept = (x, query, keyval, earlier, mixed, log_total, middle, everyone, expert_rows, gates, codes, gate_pre, up_pre)
    return result, kept


def layer_backward(grad, grad_line, kept, weights, tables, info):
    (gain_attn, gain_moe, router, owns, dense_parts, expert_parts) = weights
    w_query, w_key, w_value, w_out, w_gate, w_up, w_down = owns
    cosine, sine, query_docs, key_docs, usable, reach = tables
    (x, query, keyval, earlier, mixed, log_total, middle, everyone, expert_rows, gates, codes, gate_pre, up_pre) = kept
    rows, width = x.shape
    ranks = lax.axis_size("expert")
    pieces = lax.axis_size("dp")
    kv_width = 2 * KV_HEADS * HEAD_DIM
    keys = (reach + 1) * rows
    experts_here, _, hidden = w_gate.shape
    capacity = rows * TOPK // EXPERTS
    slots = experts_here * capacity
    ups, downs = grad_line
    per_expert = pl.BlockSpec((1, ranks * capacity, hidden), lambda e: (e, 0, 0))
    sums, grad_router, grad_rows, d_gate, d_up, activated = call(
        functools.partial(experts_back_kernel, pieces, ranks, len(expert_parts)),
        (
            struct((ranks, rows, width), bf16),
            struct((EXPERTS, width), f32),
            struct((ranks, slots, width), bf16),
        )
        + (struct((experts_here, ranks * capacity, hidden), bf16),) * 3,
        [SMEM] + [ANY] * (2 * ranks - 1) + [VMEM] * 4 + [per_expert] * 2
        + [ANY] * (3 + pieces * len(expert_parts)),
        (VMEM,) * 3 + (per_expert,) * 3,
        [
            pltpu.VMEM((ranks, rows, width), bf16),
            pltpu.VMEM((ranks, slots, rows), bf16),
            pltpu.VMEM((ranks, slots, LANES), f32),
            pltpu.VMEM((ranks, max(8, experts_here), rows), f32),
            pltpu.VMEM((ranks, slots, width), bf16),
            pltpu.VMEM((2, width, hidden), bf16),
            pltpu.VMEM((2, width, hidden), bf16),
            pltpu.VMEM((2, hidden, width), bf16),
            pltpu.SemaphoreType.DMA((2, 3)),
            pltpu.SemaphoreType.DMA,
        ],
        grid=(experts_here,),
        flops=6 * experts_here * ranks * capacity * width * hidden,
        bytes_accessed=6 * experts_here * width * hidden,
        name="experts_back",
    )(
        info, grad, *ups, *downs, everyone, gates, codes, router, gate_pre, up_pre, w_gate, w_up, w_down,
        *[piece for chunk in expert_parts for piece in chunk],
    )
    chunk_count = len(expert_parts)
    per_chunk = experts_here // chunk_count
    wide, narrow = width // pieces, hidden // pieces
    piece_rows = 2 * wide + 2 * narrow
    expert_sums = []
    for c in range(chunk_count):
        place = functools.partial(lambda c, e: (c * per_chunk + e, 0, 0), c)
        row_place = functools.partial(lambda c, e: (0, c * per_chunk + e, 0), c)
        keep, send = call(
            expert_grads_kernel,
            (struct((pieces // 2, per_chunk, piece_rows, hidden), bf16),) * 2,
            [SMEM]
            + [pl.BlockSpec((ranks, capacity, width), row_place)] * 2
            + [pl.BlockSpec((1, ranks * capacity, hidden), place)] * 3,
            (pl.BlockSpec((pieces // 2, 1, piece_rows, hidden), lambda e: (0, e, 0, 0)),) * 2,
            [],
            grid=(per_chunk,),
            flops=6 * per_chunk * ranks * capacity * width * hidden,
            bytes_accessed=6 * per_chunk * width * hidden,
            name="expert_grads",
        )(info, expert_rows, grad_rows, d_gate, d_up, activated)
        expert_sums.append(dp_reduce(keep, send))
    d_routed = line_reduce(sums)
    outs = call(
        functools.partial(attend_back_kernel, pieces, reach),
        (
            struct((rows, width), f32),
            struct((rows, width), bf16),
            struct((rows, kv_width), f32),
        )
        + (struct((rows, kv_width), bf16),) * reach
        + (struct((pieces // 2, width // pieces, width), bf16),) * 2
        + (struct((1, width), f32),),
        [SMEM] + [VMEM] * 7 + [ANY] * (1 + reach) + [VMEM] * 4 + [ANY] * (1 + pieces),
        (VMEM,) * (6 + reach),
        [
            pltpu.VMEM((keys, kv_width), bf16),
            pltpu.VMEM((rows, keys), f32),
            pltpu.VMEM((width, width), bf16),
            pltpu.VMEM((rows, width), bf16),
            pltpu.VMEM((kv_width, keys), f32),
            pltpu.SemaphoreType.DMA,
            pltpu.SemaphoreType.DMA,
        ],
        flops=40 * rows * keys * width,
        bytes_accessed=2 * width * width,
        name="attend_back",
    )(
        info, d_routed, grad, middle, gain_moe, mixed, query, log_total, keyval, *earlier,
        query_docs, key_docs, cosine, sine, w_out, *dense_parts,
    )
    d_middle, d_query, d_own = outs[:3]
    d_earlier = outs[3 : 3 + reach]
    out_keep, out_send, grad_gain_moe = outs[3 + reach :]
    moving = d_earlier[reach - 1]
    for s in reversed(range(reach)):
        moving = shifted(moving, "expert", -1)
        if s > 0:
            moving = (moving.astype(f32) + d_earlier[s - 1].astype(f32)).astype(bf16)
    piece_struct = struct((pieces // 2, width // pieces, width), bf16)
    d_normed, query_keep, query_send = call(
        functools.partial(query_back_kernel, pieces),
        (struct((rows, width), f32), piece_struct, piece_struct),
        [SMEM] + [VMEM] * 3 + [ANY] * (1 + pieces),
        (VMEM,) * 3,
        [pltpu.VMEM((width, width), bf16), pltpu.SemaphoreType.DMA],
        flops=4 * rows * width * width,
        bytes_accessed=4 * width * width,
        name="query_back",
    )(info, x, gain_attn, d_query, w_query, *dense_parts)
    d_x, kv_keep, kv_send, grad_gain_attn = call(
        functools.partial(keyval_back_kernel, pieces),
        (struct((rows, width), bf16), piece_struct, piece_struct, struct((1, width), f32)),
        [SMEM] + [VMEM] * 8 + [ANY] * (2 + pieces),
        (VMEM,) * 4,
        [
            pltpu.VMEM((width, kv_width), bf16),
            pltpu.VMEM((rows, kv_width), bf16),
            pltpu.SemaphoreType.DMA,
        ],
        flops=4 * rows * width * kv_width,
        bytes_accessed=4 * width * kv_width,
        name="keyval_back",
    )(
        info, x, gain_attn, d_own, moving, d_normed, d_middle, cosine, sine, w_key, w_value, *dense_parts,
    )
    dense_sums = []
    for keep, send in ((out_keep, out_send), (query_keep, query_send), (kv_keep, kv_send)):
        mine = dp_reduce(keep, send)
        dense_sums.append(line_reduce(mine.reshape(ranks, -1, width)))
    small = jnp.concatenate([grad_router, grad_gain_moe, grad_gain_attn], axis=0).T
    small = lax.psum_scatter(small, ("dp", "expert"), scatter_dimension=0, tiled=True)
    return d_x, expert_sums, dense_sums, small


def doc_ids(lengths, positions):
    endings = jnp.cumsum(lengths)
    return jnp.sum((positions[:, None] >= endings[None, :]).astype(jnp.int32), axis=1)


def per_device(
    inputs, cotangent, gain_attn, w_query, w_key, w_value, w_out, gain_moe, w_router, w_gate, w_up, w_down,
    doc_lengths, routes,
):
    rows, width = inputs.shape[2:]
    ranks = lax.axis_size("expert")
    pieces = lax.axis_size("dp")
    section = lax.axis_index("section")
    place = lax.axis_index("dp")
    line = lax.axis_index("expert")
    experts_here, _, hidden = w_gate.shape[1:]
    first = section == 0

    def mine(values):
        return lax.dynamic_index_in_dim(values, section, 0, False)

    def other(values):
        return lax.dynamic_index_in_dim(values, 1 - section, 0, False)

    x = mine(inputs[:, 0])
    top = mine(cotangent[:, 0])
    lengths = mine(doc_lengths[:, 0])

    wide, narrow = width // pieces, hidden // pieces

    def rows_of(matrix, axis, size):
        return lax.dynamic_slice_in_dim(matrix, place * size, size, axis)

    dense_piece = jnp.concatenate(
        [rows_of(w[0], 0, wide) for w in (w_query, w_key, w_value, w_out)], axis=1
    )
    dense_parts = fetch_pieces(dense_piece)
    small = jnp.concatenate([w_router[0].T.astype(f32), gain_attn, gain_moe], axis=0)
    other_small = swapped(small, "section", 1)
    chunk_count = 4 if experts_here % 4 == 0 else 1
    per_chunk = experts_here // chunk_count
    expert_parts = []
    for c in range(chunk_count):
        span = slice(c * per_chunk, (c + 1) * per_chunk)
        down = rows_of(w_down[0, span], 1, narrow)
        piece = jnp.concatenate(
            [
                rows_of(w_gate[0, span], 1, wide),
                rows_of(w_up[0, span], 1, wide),
                down[:, :, : width // 2],
                down[:, :, width // 2 :],
            ],
            axis=1,
        )
        expert_parts.append(fetch_pieces(piece))

    owns = (w_query[0], w_key[0], w_value[0], w_out[0], w_gate[0], w_up[0], w_down[0])
    here = routes[0, :, 0]
    my_routes = mine(here)
    other_routes = swapped(other(here), "section", 1)
    both = jnp.stack([jnp.where(first, my_routes, other_routes), jnp.where(first, other_routes, my_routes)])
    both = lax.all_gather(both, "expert", axis=1, tiled=True).transpose(0, 2, 1)
    layers, infos = [], []
    for layer in range(2):
        held = section == layer
        table = jnp.where(held, small, other_small)
        layers.append((table[EXPERTS : EXPERTS + 1], table[EXPERTS + 1 :], table[:EXPERTS].astype(bf16), owns, dense_parts, expert_parts))
        infos.append(jnp.stack([held.astype(jnp.int32), place, line]).astype(jnp.int32))

    offset = line * rows
    reach = min((WINDOW - 1) // rows + 1, ranks - 1)
    positions = offset + jnp.arange(rows, dtype=jnp.int32)
    key_places = offset - reach * rows + jnp.arange((reach + 1) * rows, dtype=jnp.int32)
    query_docs = doc_ids(lengths, positions)[:, None]
    key_docs = jnp.where(key_places >= 0, doc_ids(lengths, key_places), -1)[None, :]
    usable = (doc_ids(lengths, jnp.arange(ranks * rows, dtype=jnp.int32)) < NDOC).astype(jnp.int32)[None, :]
    half = HEAD_DIM // 2
    inverse = 10000.0 ** (-(jnp.arange(half, dtype=f32) * (2.0 / HEAD_DIM)))
    angles = positions.astype(f32)[:, None] * inverse[None, :]
    cosine = jnp.tile(jnp.cos(angles), (1, 4))
    sine = jnp.sin(angles)
    sine = jnp.concatenate([-sine, sine, -sine, sine], axis=1)
    tables = (cosine, sine, query_docs, key_docs, usable, reach)

    top_line = line_gather(top)
    between, kept_first = layer_forward(x, layers[0], tables, infos[0], both[0])
    final, kept_second = layer_forward(between, layers[1], tables, infos[1], both[1])
    d_between, experts_second, dense_second, small_second = layer_backward(
        top, top_line, kept_second, layers[1], tables, infos[1]
    )
    d_first, experts_first, dense_first, small_first = layer_backward(
        d_between, line_gather(d_between), kept_first, layers[0], tables, infos[0]
    )

    def by_section(of_first, of_second):
        held = jnp.where(first, of_first, of_second)
        got = swapped(jnp.where(first, of_second, of_first), "section", 1)
        return jnp.stack([jnp.where(first, held, got), jnp.where(first, got, held)])

    def total(of_first, of_second):
        got = to_owner(of_first, 0), to_owner(of_second, 1)
        return jnp.where(
            first, of_first.astype(f32) + got[0].astype(f32), of_second.astype(f32) + got[1].astype(f32)
        )

    outputs = by_section(between, final)
    input_grads = by_section(d_first, d_between)
    chunks = [total(a, b) for a, b in zip(experts_first, experts_second)]
    grad_gate = jnp.concatenate([c[:, :wide] for c in chunks], axis=0)
    grad_up = jnp.concatenate([c[:, wide : 2 * wide] for c in chunks], axis=0)
    grad_down = jnp.concatenate(
        [
            jnp.concatenate([c[:, 2 * wide : 2 * wide + narrow], c[:, 2 * wide + narrow :]], axis=2)
            for c in chunks
        ],
        axis=0,
    )
    grad_out, grad_query, grad_keyval = [
        total(a.astype(bf16), b.astype(bf16)) for a, b in zip(dense_first, dense_second)
    ]
    vectors = total(small_first, small_second)
    kv_half = KV_HEADS * HEAD_DIM
    return (
        outputs[None, :, None],
        input_grads[None, :, None],
        vectors[:, EXPERTS + 1][None],
        grad_query[None],
        grad_keyval[:, :kv_half][None],
        grad_keyval[:, kv_half:][None],
        grad_out[None],
        vectors[:, EXPERTS][None],
        vectors[:, :EXPERTS][None],
        grad_gate[None],
        grad_up[None],
        grad_down[None],
    )


def solution(mesh):
    placed = (
        P(None, "dp", "expert", None),
        P(None, "dp", "expert", None),
        P("section", None),
        P("section", None, None),
        P("section", None, None),
        P("section", None, None),
        P("section", None, None),
        P("section", None),
        P("section", None, None),
        P("section", "expert", None, None),
        P("section", "expert", None, None),
        P("section", "expert", None, None),
        P(None, "dp", None),
        P("section", None, "dp", "expert", None),
    )
    return jax.shard_map(
        per_device,
        mesh=mesh,
        in_specs=placed,
        out_specs=(
            P("section", None, "dp", "expert", None),
            P("section", None, "dp", "expert", None),
            P("section", ("dp", "expert")),
            P("section", ("dp", "expert"), None),
            P("section", ("dp", "expert"), None),
            P("section", ("dp", "expert"), None),
            P("section", ("dp", "expert"), None),
            P("section", ("dp", "expert")),
            P("section", ("dp", "expert"), None),
            P("section", "expert", "dp", None),
            P("section", "expert", "dp", None),
            P("section", "expert", "dp", None),
        ),
        check_vma=False,
    )
```

```python
import functools

import jax
import jax.numpy as jnp
from jax import lax
from jax.experimental import pallas as pl
from jax.experimental.pallas import tpu as pltpu
from jax.sharding import PartitionSpec as P

HEADS = 16
KV_HEADS = 8
HEAD_DIM = 64
EXPERTS = 32
TOPK = 8
WINDOW = 512
NDOC = 4
EPSILON = 1e-06
MASKED = -1e30
LANES = 128
VMEM_BYTES = 56 * 1024 * 1024
bf16 = jnp.bfloat16
f32 = jnp.float32


def shifted(value, axis, steps, sources=None):
    count = lax.axis_size(axis)
    initial, last = (max(0, -steps), min(count, count - steps))
    names = range(initial, last) if sources is None else sources
    return lax.ppermute(value, axis, [(source, source + steps) for source in names])


def swapped(value, axis, bit):
    count = lax.axis_size(axis)
    return lax.ppermute(value, axis, [(source, source ^ bit) for source in range(count)])


def tie(*values):
    return lax.optimization_barrier(values)


def line_gather(block):
    ups, downs = [], []
    up, down = block, block
    for _ in range(lax.axis_size("expert") - 1):
        up = shifted(up, "expert", 1)
        down = shifted(down, "expert", -1)
        ups.append(up)
        downs.append(down)
    return ups, downs


def line_reduce(parts, ties={}, marks=None):
    ranks = lax.axis_size("expert")
    me = lax.axis_index("expert")

    def pick(index):
        return lax.dynamic_index_in_dim(parts, jnp.clip(index, 0, ranks - 1), 0, False)

    up = down = None
    for step in range(1, ranks):
        up_part = pick(me + ranks - step)
        down_part = pick(me - ranks + step)
        up = up_part if up is None else (up.astype(f32) + up_part.astype(f32)).astype(bf16)
        down = down_part if down is None else (down.astype(f32) + down_part.astype(f32)).astype(bf16)
        if step in ties:
            up, down, *ties[step] = tie(up, down, *ties[step])
        up = shifted(up, "expert", 1, range(0, step))
        down = shifted(down, "expert", -1, range(ranks - step, ranks))
        if marks is not None:
            marks.append([up, down])
    return pick(me).astype(f32) + up.astype(f32) + down.astype(f32)


def dp_size():
    return lax.axis_size("far") * lax.axis_size("near")


def dp_swapped(value, bit):
    return swapped(value, "near", 1) if bit == 1 else swapped(value, "far", bit // 2)


def fetch_bits():
    bits, bit = [], dp_size() // 2
    while bit >= 1:
        bits.append(bit)
        bit //= 2
    return bits


def spread_pieces(piece, before=None):
    pieces = {0: piece}
    for bit in fetch_bits():
        for k in list(pieces):
            if before is not None and k == max(pieces):
                pieces[k] = before(pieces[k], bit)
            pieces[k | bit] = dp_swapped(pieces[k], bit)
    return [pieces[k] for k in range(len(pieces))]


def near_sum(keep, send):
    return (keep.astype(f32) + swapped(send, "near", 1).astype(f32)).astype(bf16)


def call(
    kernel, out_shape, in_specs, out_specs, scratch, grid=None, flops=0, bytes_accessed=0, name=None, waits=()
):
    extra = {} if grid is None else {"grid": grid}
    begin, end = len(in_specs), len(in_specs) + len(waits)
    run = pl.pallas_call(
        lambda *refs: kernel(*refs[:begin], *refs[end:]),
        out_shape=out_shape,
        in_specs=[*in_specs, *[ANY] * len(waits)],
        out_specs=out_specs,
        scratch_shapes=scratch,
        compiler_params=pltpu.CompilerParams(vmem_limit_bytes=VMEM_BYTES),
        cost_estimate=pl.CostEstimate(flops=flops, bytes_accessed=bytes_accessed, transcendentals=0),
        name=name,
        **extra,
    )
    return lambda *args: run(*args, *waits)


SMEM = pl.BlockSpec(memory_space=pltpu.SMEM)
VMEM = pl.BlockSpec(memory_space=pltpu.VMEM)
ANY = pl.BlockSpec(memory_space=pl.ANY)


def struct(shape, dtype):
    return jax.ShapeDtypeStruct(shape, dtype)


def dot(left, right, left_dim=1, right_dim=0):
    return lax.dot_general(left, right, (((left_dim,), (right_dim,)), ((), ())), preferred_element_type=f32)


def upper_lanes(shape):
    return lax.broadcasted_iota(jnp.int32, shape, 1) % LANES >= HEAD_DIM


def half_swap(tile):
    lane = lax.broadcasted_iota(jnp.int32, tile.shape, 1)
    half = HEAD_DIM // 2
    return jnp.where(
        lane % HEAD_DIM < half, pltpu.roll(tile, LANES - half, 1), pltpu.roll(tile, half, 1)
    )


def load_dense(info, owns, pieces, first, width, target, sem):
    rows = target.shape[0] // len(pieces)

    @pl.when(info[0] == 1)
    def _():
        start = 0
        for own in owns:
            size = own.shape[1]
            pltpu.make_async_copy(own, target.at[:, pl.ds(start, size)], sem).start()
            start += size

    @pl.when(info[0] == 0)
    def _():
        for k, piece in enumerate(pieces):
            place = pl.multiple_of((info[1] ^ k) * rows, rows)
            pltpu.make_async_copy(
                piece.at[:, pl.ds(first, width)], target.at[pl.ds(place, rows), :], sem
            ).start()


def wait_dense(target, sem):
    pltpu.make_async_copy(target, target, sem).wait()


def load_experts(info, owns, chunks, expert, slot, buffers, sems):
    gate_buf, up_buf, down_buf = buffers
    pieces = len(chunks[0])
    wide = gate_buf.shape[1] // pieces
    narrow = down_buf.shape[1] // pieces
    half = down_buf.shape[2] // 2

    @pl.when(info[0] == 1)
    def _():
        for own, buf, index in zip(owns, buffers, range(3)):
            pltpu.make_async_copy(own.at[expert], buf.at[slot], sems.at[slot, index]).start()

    begin = 0
    for chunk in chunks:
        first, begin = begin, begin + chunk[0].shape[0]

        @pl.when((info[0] == 0) & (expert >= first) & (expert < begin))
        def _():
            local = expert - first
            for k, piece in enumerate(chunk):
                owner = info[1] ^ k
                row = pl.multiple_of(owner * wide, wide)
                low = pl.multiple_of(owner * narrow, narrow)
                pltpu.make_async_copy(
                    piece.at[local, pl.ds(0, wide)], gate_buf.at[slot, pl.ds(row, wide)], sems.at[slot, 0]
                ).start()
                pltpu.make_async_copy(
                    piece.at[local, pl.ds(wide, wide)], up_buf.at[slot, pl.ds(row, wide)], sems.at[slot, 1]
                ).start()
                for side in range(2):
                    pltpu.make_async_copy(
                        piece.at[local, pl.ds(2 * wide + side * narrow, narrow)],
                        down_buf.at[slot, pl.ds(low, narrow), pl.ds(side * half, half)],
                        sems.at[slot, 2],
                    ).start()


def wait_experts(slot, index, buffers, sems):
    pltpu.make_async_copy(buffers[index].at[slot], buffers[index].at[slot], sems.at[slot, index]).wait()


def load_line(info, own, ups, downs, target, sem):
    ranks = target.shape[0]
    me = info[2]
    columns = pl.ds(0, target.shape[2])
    pltpu.make_async_copy(own.at[:, columns], target.at[me], sem).start()
    for s in range(1, ranks):

        @pl.when(me >= s)
        def _():
            pltpu.make_async_copy(ups[s - 1].at[:, columns], target.at[me - s], sem).start()

        @pl.when(me < s)
        def _():
            pltpu.make_async_copy(downs[ranks - s - 1].at[:, columns], target.at[me - s + ranks], sem).start()


def wait_line(target, sem):
    pltpu.make_async_copy(target, target, sem).wait()


def write_pieces(info, value, keep, send, place):
    pieces = 2 * keep.shape[0]
    rows = value.shape[0] // pieces
    for p in range(pieces):
        part = value[p * rows : (p + 1) * rows].astype(keep.dtype)
        same = info[1] % 2 == p % 2

        @pl.when(same)
        def _():
            keep[(p // 2,) + place] = part

        @pl.when(jnp.logical_not(same))
        def _():
            send[(p // 2,) + place] = part


def rms(values):
    return lax.rsqrt(jnp.mean(values * values, axis=-1, keepdims=True) + EPSILON)


def mask_bias(info, query_docs, key_docs, bias):
    rows, keys = bias.shape
    row = lax.broadcasted_iota(jnp.int32, (rows, keys), 0)
    col = lax.broadcasted_iota(jnp.int32, (rows, keys), 1)
    distance = row + (keys - rows) - col
    allowed = (distance >= 0) & (distance < WINDOW) & (query_docs[...] == key_docs[...])
    bias[...] = jnp.where(allowed, 0.0, MASKED)


def load_keys(own, earlier, target, sem):
    rows = own.shape[0]
    reach = len(earlier)
    pltpu.make_async_copy(own, target.at[pl.ds(reach * rows, rows)], sem).start()
    for s, part in enumerate(earlier):
        pltpu.make_async_copy(part, target.at[pl.ds((reach - 1 - s) * rows, rows)], sem).start()


def doubled(pair, which):
    wide = pair.astype(f32)
    turned = pltpu.roll(wide, HEAD_DIM, 1)
    upper = upper_lanes(wide.shape)
    picked = jnp.where(upper, turned, wide) if which == 0 else jnp.where(upper, wide, turned)
    return picked.astype(bf16)


def one_head(tile, which, upper):
    return jnp.where(upper, tile, 0.0) if which == 1 else jnp.where(upper, 0.0, tile)


def pack_dense_kernel(info, *refs):
    begin = 0
    for matrix in refs[:-1]:
        width = matrix.shape[1]
        refs[-1][:, begin : begin + width] = matrix[...]
        begin += width


def pack_experts_kernel(info, gate, up, down, out):
    wide, narrow = gate.shape[1], down.shape[1]
    half = out.shape[2]
    out[0, :wide] = gate[0]
    out[0, wide : 2 * wide] = up[0]
    out[0, 2 * wide : 2 * wide + narrow] = down[0, :, :half]
    out[0, 2 * wide + narrow :] = down[0, :, half:]


def packed(kernel, out_shape, grid, in_specs, out_specs, name):
    size = 4 * functools.reduce(lambda a, b: a * b, out_shape.shape)
    return pl.pallas_call(
        kernel,
        out_shape=out_shape,
        grid_spec=pltpu.PrefetchScalarGridSpec(
            num_scalar_prefetch=1, grid=grid, in_specs=in_specs, out_specs=out_specs
        ),
        cost_estimate=pl.CostEstimate(flops=0, bytes_accessed=size, transcendentals=0),
        name=name,
    )


def pack_dense(info, matrices, pieces):
    rows = matrices[0].shape[0] // pieces
    total = sum(matrix.shape[1] for matrix in matrices)
    return packed(
        pack_dense_kernel,
        struct((rows, total), bf16),
        (1,),
        [pl.BlockSpec((rows, matrix.shape[1]), lambda i, info: (info[1], 0)) for matrix in matrices],
        pl.BlockSpec((rows, total), lambda i, info: (0, 0)),
        "pack_dense",
    )(info, *matrices)


def pack_experts(info, matrices, pieces, first, count):
    gate, up, down = matrices
    wide, narrow = gate.shape[1] // pieces, down.shape[1] // pieces
    hidden, width = gate.shape[2], down.shape[2]

    def own(e, info):
        return (first + e, info[1], 0)

    return packed(
        pack_experts_kernel,
        struct((count, 2 * wide + 2 * narrow, hidden), bf16),
        (count,),
        [
            pl.BlockSpec((1, wide, hidden), own),
            pl.BlockSpec((1, wide, hidden), own),
            pl.BlockSpec((1, narrow, width), own),
        ],
        pl.BlockSpec((1, 2 * wide + 2 * narrow, hidden), lambda e, info: (e, 0, 0)),
        "pack_experts",
    )(info, gate, up, down)


def project_kernel(pieces, info, x, gain, cosine, sine, w_query, w_key, w_value, *rest):
    parts = rest[:pieces]
    query, keyval, weights, sem = rest[pieces:]
    width = weights.shape[1]
    load_dense(info, (w_query, w_key, w_value), parts, 0, width, weights, sem)
    hidden = x[...].astype(f32)
    normed = (hidden * rms(hidden) * gain[...]).astype(bf16)
    wait_dense(weights, sem)
    q_width, k_width = w_query.shape[1], w_key.shape[1]
    cos, sin = cosine[...], sine[...]
    step = 2 * LANES
    for begin in range(0, width, step):
        product = dot(normed, weights[:, begin : begin + step])
        for inner in range(0, step, LANES):
            tile = product[:, inner : inner + LANES]
            place = begin + inner
            if place < q_width + k_width:
                tile = tile * cos + half_swap(tile) * sin
            if place < q_width:
                query[:, place : place + LANES] = tile.astype(bf16)
            else:
                place -= q_width
                keyval[:, place : place + LANES] = tile.astype(bf16)


def attend_kernel(pieces, reach, info, query, own_kv, *rest):
    earlier = rest[:reach]
    query_docs, key_docs, x, gain, w_out = rest[reach : reach + 5]
    parts = rest[reach + 5 : reach + 5 + pieces]
    mixed, log_total, middle, routed = rest[reach + 5 + pieces : reach + 9 + pieces]
    keyval, bias, weights, kv_sem, w_sem = rest[reach + 9 + pieces :]
    load_keys(own_kv, earlier, keyval, kv_sem)
    first = 2 * x.shape[1]
    load_dense(info, (w_out,), parts, first, x.shape[1], weights, w_sem)
    mask_bias(info, query_docs, key_docs, bias)
    log_total[...] = jnp.zeros_like(log_total)
    pltpu.make_async_copy(keyval, keyval, kv_sem).wait()
    kv_width = KV_HEADS * HEAD_DIM
    rows = query.shape[0]
    upper = upper_lanes((rows, LANES))
    lane = lax.broadcasted_iota(jnp.int32, (rows, LANES), 1)

    @pl.loop(0, KV_HEADS // 2)
    def _(pair):
        k_pair = keyval[:, pl.ds(pl.multiple_of(pair * LANES, LANES), LANES)]
        v_pair = keyval[:, pl.ds(pl.multiple_of(kv_width + pair * LANES, LANES), LANES)]
        for head in range(2):
            keys, values = doubled(k_pair, head), doubled(v_pair, head)
            place = pl.multiple_of((pair * 2 + head) * LANES, LANES)
            tile = query[:, pl.ds(place, LANES)].astype(f32) * HEAD_DIM ** (-0.5)
            results = []
            for g in range(2):
                scores = dot(one_head(tile, g, upper).astype(bf16), keys, 1, 1) + bias[...]
                peak = jnp.max(scores, axis=1, keepdims=True)
                expo = jnp.exp(scores - peak)
                total = jnp.sum(expo, axis=1, keepdims=True)
                results.append(dot(expo.astype(bf16), values) * (1.0 / total))
                index = (pair * 2 + head) * 2 + g
                log_total[...] = jnp.where(lane == index, peak + jnp.log(total), log_total[...])
            mixed[:, pl.ds(place, LANES)] = jnp.where(upper, results[1], results[0]).astype(bf16)

    wait_dense(weights, w_sem)
    between = x[...].astype(f32) + dot(mixed[...], weights[...])
    middle[...] = between
    routed[...] = (between * rms(between) * gain[...]).astype(bf16)


def attend_back_kernel(pieces, reach, info, d_routed, grad, middle, gain, mixed, query, log_total, own_kv, *rest):
    earlier = rest[:reach]
    query_docs, key_docs, cosine, sine, w_out = rest[reach : reach + 5]
    rest = rest[reach + 5 :]
    parts = rest[:pieces]
    rest = rest[pieces:]
    d_middle, d_query, d_own = rest[:3]
    d_earlier = rest[3 : 3 + reach]
    keep, send, grad_gain = rest[3 + reach : 6 + reach]
    keyval, bias, weights, d_mixed, d_kv, kv_sem, w_sem = rest[6 + reach :]
    load_keys(own_kv, earlier, keyval, kv_sem)
    first = 2 * middle.shape[1]
    load_dense(info, (w_out,), parts, first, middle.shape[1], weights, w_sem)
    mask_bias(info, query_docs, key_docs, bias)
    between = middle[...]
    scale = rms(between)
    normal = between * scale
    routed = d_routed[...]
    grad_gain[...] = jnp.sum(routed * normal, axis=0, keepdims=True)
    d_norm = routed * gain[...]
    total = grad[...].astype(f32) + scale * (
        d_norm - normal * jnp.mean(d_norm * normal, axis=1, keepdims=True)
    )
    d_middle[...] = total
    branch = total.astype(bf16)
    wait_dense(weights, w_sem)
    d_mixed[...] = dot(branch, weights[...], 1, 1).astype(bf16)
    write_pieces(info, dot(mixed[...], branch, 0, 0), keep, send, ())
    pltpu.make_async_copy(keyval, keyval, kv_sem).wait()
    kv_width = KV_HEADS * HEAD_DIM
    rows = query.shape[0]
    upper = upper_lanes((rows, LANES))
    lane = lax.broadcasted_iota(jnp.int32, (rows, LANES), 1)
    cos, sin = cosine[...], sine[...]

    @pl.loop(0, KV_HEADS // 2)
    def _(pair):
        k_pair = keyval[:, pl.ds(pl.multiple_of(pair * LANES, LANES), LANES)]
        v_pair = keyval[:, pl.ds(pl.multiple_of(kv_width + pair * LANES, LANES), LANES)]
        for head in range(2):
            keys, values = doubled(k_pair, head), doubled(v_pair, head)
            place = pl.multiple_of((pair * 2 + head) * LANES, LANES)
            tile = query[:, pl.ds(place, LANES)].astype(f32) * HEAD_DIM ** (-0.5)
            d_tile = d_mixed[:, pl.ds(place, LANES)].astype(f32)
            inner = d_tile * mixed[:, pl.ds(place, LANES)].astype(f32)
            dq, dk, dv = [], None, None
            for g in range(2):
                index = (pair * 2 + head) * 2 + g
                log_column = jnp.sum(jnp.where(lane == index, log_total[...], 0.0), axis=1, keepdims=True)
                weight = jnp.sum(one_head(inner, g, upper), axis=1, keepdims=True)
                own_query = one_head(tile, g, upper).astype(bf16)
                own_grad = one_head(d_tile, g, upper).astype(bf16)
                scores = dot(own_query, keys, 1, 1) + bias[...]
                probs = jnp.exp(scores - log_column)
                d_probs = dot(own_grad, values, 1, 1)
                d_scores = (probs * (d_probs - weight)).astype(bf16)
                dq.append(dot(d_scores, keys))
                k_term = dot(own_query, d_scores, 0, 0)
                v_term = dot(own_grad, probs.astype(bf16), 0, 0)
                dk = k_term if dk is None else dk + k_term
                dv = v_term if dv is None else dv + v_term
            whole = jnp.where(upper, dq[1], dq[0]) * HEAD_DIM ** (-0.5)
            whole = whole * cos - half_swap(whole) * sin
            d_query[:, pl.ds(place, LANES)] = whole.astype(bf16)
            k_row = pl.multiple_of((pair * 2 + head) * HEAD_DIM, HEAD_DIM)
            v_row = pl.multiple_of(kv_width + (pair * 2 + head) * HEAD_DIM, HEAD_DIM)
            d_kv[pl.ds(k_row, HEAD_DIM), :] = dk[:HEAD_DIM] + dk[HEAD_DIM:]
            d_kv[pl.ds(v_row, HEAD_DIM), :] = dv[:HEAD_DIM] + dv[HEAD_DIM:]

    for block in range(reach + 1):
        turned = d_kv[:, block * rows : (block + 1) * rows].T
        if block == reach:
            d_own[...] = turned
        else:
            d_earlier[reach - 1 - block][...] = turned.astype(bf16)


def query_back_kernel(pieces, info, x, gain, d_query, w_query, *rest):
    parts = rest[:pieces]
    d_normed, keep, send, weights, sem = rest[pieces:]
    load_dense(info, (w_query,), parts, 0, weights.shape[1], weights, sem)
    hidden = x[...].astype(f32)
    normed = (hidden * rms(hidden) * gain[...]).astype(bf16)
    write_pieces(info, dot(normed, d_query[...], 0, 0), keep, send, ())
    wait_dense(weights, sem)
    d_normed[...] = dot(d_query[...], weights[...], 1, 1)


def keyval_back_kernel(
    pieces, info, x, gain, d_own, d_others, d_normed, d_middle, cosine, sine, grad_router, grad_gain_moe,
    w_key, w_value, *rest,
):
    parts = rest[:pieces]
    d_x, keep, send, weights, d_pre, sem = rest[pieces:]
    load_dense(info, (w_key, w_value), parts, x.shape[1], weights.shape[1], weights, sem)
    hidden = x[...].astype(f32)
    scale = rms(hidden)
    normal = hidden * scale
    normed = (normal * gain[...]).astype(bf16)
    cos, sin = cosine[...], sine[...]
    width = w_key.shape[1]
    for place in range(0, 2 * width, LANES):
        tile = d_own[:, place : place + LANES] + d_others[:, place : place + LANES].astype(f32)
        if place < width:
            tile = tile * cos - half_swap(tile) * sin
        d_pre[:, place : place + LANES] = tile.astype(bf16)
    wait_dense(weights, sem)
    total = d_normed[...] + dot(d_pre[...], weights[...], 1, 1)
    grad_gain = jnp.sum(total * normal, axis=0, keepdims=True)
    tall = jnp.concatenate(
        [grad_router[...], jnp.zeros((LANES - EXPERTS, total.shape[1]), f32)], axis=0
    )
    row = lax.broadcasted_iota(jnp.int32, tall.shape, 0)
    tall = jnp.where(row == EXPERTS, grad_gain_moe[...], jnp.where(row == EXPERTS + 1, grad_gain, tall))
    d_norm = total * gain[...]
    d_x[...] = (
        d_middle[...]
        + scale * (d_norm - normal * jnp.mean(d_norm * normal, axis=1, keepdims=True))
    ).astype(bf16)
    both = 2 * width
    write_pieces(info, dot(normed, d_pre[...], 0, 0), keep, send, (slice(None), slice(0, both)))
    write_pieces(info, tall.T, keep, send, (slice(None), slice(both, both + LANES)))


def slot_rows(info, table, local, experts_here):
    row = lax.broadcasted_iota(jnp.int32, table.shape, 0)
    picked = jnp.where(row == info[2] * experts_here + local, table, 0.0)
    return jnp.sum(picked, axis=0, keepdims=True)


def slot_hits(codes, capacity):
    slot = lax.broadcasted_iota(jnp.int32, (capacity, codes.shape[1]), 0).astype(f32)
    return slot == codes


def experts_kernel(pieces, ranks, chunk_count, info, own, *rest):
    ups, downs = rest[: ranks - 1], rest[ranks - 1 : 2 * ranks - 2]
    rest = rest[2 * ranks - 2 :]
    routes, usable, router, w_gate, w_up, w_down = rest[:6]
    rest = rest[6:]
    chunks = [rest[c * pieces : (c + 1) * pieces] for c in range(chunk_count)]
    rest = rest[chunk_count * pieces :]
    sums, everyone, rows, gates, codes, gate_out, up_out = rest[:7]
    hits, results, gate_buf, up_buf, down_buf, sems, line_sem = rest[7:]
    expert, count = pl.program_id(0), pl.num_programs(0)
    buffers = (gate_buf, up_buf, down_buf)
    owns = (w_gate, w_up, w_down)
    experts_here = w_gate.shape[0]
    tokens = own.shape[0]
    capacity = tokens * TOPK // EXPERTS
    slot = expert % 2

    @pl.when(expert == 0)
    def _():
        load_line(info, own, ups, downs, everyone, line_sem)
        load_experts(info, owns, chunks, 0, 0, buffers, sems)
        earlier = lax.broadcasted_iota(jnp.int32, (tokens, tokens), 0)
        later = lax.broadcasted_iota(jnp.int32, (tokens, tokens), 1)
        triangle = jnp.where(earlier < later, 1.0, 0.0).astype(bf16)
        number = lax.broadcasted_iota(jnp.int32, (EXPERTS, tokens), 0)
        wait_line(everyone, line_sem)
        for block in range(ranks):
            span = slice(block * tokens, (block + 1) * tokens)
            named = routes[0:1, span] == number
            for k in range(1, TOPK):
                named = named | (routes[k : k + 1, span] == number)
            logits = jnp.where(named, dot(router[...], everyone[block], 1, 1), MASKED)
            expo = jnp.where(named, jnp.exp(logits - jnp.max(logits, axis=0, keepdims=True)), 0.0)
            weight = expo / jnp.sum(expo, axis=0, keepdims=True)
            held = named & (usable[:, span] > 0)
            rank = dot(jnp.where(held, 1.0, 0.0).astype(bf16), triangle)
            code = jnp.where(held & (rank < capacity), rank, -1.0)
            gates[block] = weight
            codes[block] = code
            for e in range(experts_here):
                hit = slot_hits(slot_rows(info, code, e, experts_here), capacity)
                hits[block, e * capacity : (e + 1) * capacity, :] = jnp.where(hit, 1.0, 0.0).astype(bf16)
            rows[block] = dot(hits[block], everyone[block]).astype(bf16)

    @pl.when(expert + 1 < count)
    def _():
        load_experts(info, owns, chunks, expert + 1, 1 - slot, buffers, sems)

    place = pl.multiple_of(expert * capacity, capacity)
    mine = jnp.concatenate([rows[block, pl.ds(place, capacity), :] for block in range(ranks)], axis=0)
    wait_experts(slot, 0, buffers, sems)
    gate_pre = dot(mine, gate_buf[slot])
    wait_experts(slot, 1, buffers, sems)
    up_pre = dot(mine, up_buf[slot])
    gate_out[0] = gate_pre.astype(bf16)
    up_out[0] = up_pre.astype(bf16)
    activated = (gate_pre * jax.nn.sigmoid(gate_pre) * up_pre).astype(bf16)
    wait_experts(slot, 2, buffers, sems)
    produced = dot(activated, down_buf[slot]).astype(bf16)
    for block in range(ranks):
        results[block, pl.ds(place, capacity), :] = produced[block * capacity : (block + 1) * capacity]

    @pl.when(expert + 1 == count)
    def _():
        for block in range(ranks):
            weighted = []
            for e in range(experts_here):
                weight = slot_rows(info, gates[block], e, experts_here)
                hit = hits[block, e * capacity : (e + 1) * capacity, :].astype(f32)
                weighted.append((hit * weight).astype(bf16))
            sums[block] = dot(jnp.concatenate(weighted, axis=0), results[block], 0, 0).astype(bf16)


def experts_back_kernel(pieces, ranks, chunk_count, info, own, *rest):
    ups, downs = rest[: ranks - 1], rest[ranks - 1 : 2 * ranks - 2]
    rest = rest[2 * ranks - 2 :]
    everyone, gates, codes, router, gate_pre, up_pre, w_gate, w_up, w_down = rest[:9]
    rest = rest[9:]
    chunks = [rest[c * pieces : (c + 1) * pieces] for c in range(chunk_count)]
    rest = rest[chunk_count * pieces :]
    sums, grad_router, grad_rows, gate_out, up_out, active_out = rest[:6]
    incoming, hits, columns, d_gates, d_rows, gate_buf, up_buf, down_buf, sems, line_sem = rest[6:]
    expert, count = pl.program_id(0), pl.num_programs(0)
    buffers = (gate_buf, up_buf, down_buf)
    owns = (w_gate, w_up, w_down)
    experts_here = w_gate.shape[0]
    tokens = own.shape[0]
    capacity = tokens * TOPK // EXPERTS
    slot = expert % 2

    @pl.when(expert == 0)
    def _():
        load_line(info, own, ups, downs, incoming, line_sem)
        load_experts(info, owns, chunks, 0, 0, buffers, sems)
        for block in range(ranks):
            for e in range(experts_here):
                hit = slot_hits(slot_rows(info, codes[block], e, experts_here), capacity)
                span = slice(e * capacity, (e + 1) * capacity)
                hits[block, span, :] = jnp.where(hit, 1.0, 0.0).astype(bf16)
                weight = slot_rows(info, gates[block], e, experts_here)
                column = jnp.sum(jnp.where(hit, weight, 0.0), axis=1, keepdims=True)
                columns[block, span, :] = jnp.broadcast_to(column, (capacity, LANES))
        wait_line(incoming, line_sem)
        for block in range(ranks):
            grad_rows[block] = dot(hits[block], incoming[block]).astype(bf16)

    @pl.when(expert + 1 < count)
    def _():
        load_experts(info, owns, chunks, expert + 1, 1 - slot, buffers, sems)

    place = pl.multiple_of(expert * capacity, capacity)
    mine = jnp.concatenate([grad_rows[block, pl.ds(place, capacity), :] for block in range(ranks)], axis=0)
    weight = jnp.concatenate(
        [columns[block, pl.ds(place, capacity), :] for block in range(ranks)], axis=0
    )[:, :1]
    gate = gate_pre[0].astype(f32)
    up = up_pre[0].astype(f32)
    sigma = jax.nn.sigmoid(gate)
    silu = gate * sigma
    activated = silu * up
    wait_experts(slot, 2, buffers, sems)
    unweighted = dot(mine, down_buf[slot], 1, 1)
    d_weight = jnp.sum(unweighted * activated, axis=1, keepdims=True)
    for block in range(ranks):
        hit = hits[block, pl.ds(place, capacity), :].astype(f32)
        spread = hit * d_weight[block * capacity : (block + 1) * capacity]
        d_gates[block, pl.ds(expert, 1), :] = jnp.sum(spread, axis=0, keepdims=True)
    d_active = unweighted * weight
    active_out[0] = (activated * weight).astype(bf16)
    d_gate = (d_active * up * sigma * (1.0 + gate * (1.0 - sigma))).astype(bf16)
    d_up = (d_active * silu).astype(bf16)
    gate_out[0] = d_gate
    up_out[0] = d_up
    wait_experts(slot, 0, buffers, sems)
    wait_experts(slot, 1, buffers, sems)
    produced = (dot(d_gate, gate_buf[slot], 1, 1) + dot(d_up, up_buf[slot], 1, 1)).astype(bf16)
    for block in range(ranks):
        d_rows[block, pl.ds(place, capacity), :] = produced[block * capacity : (block + 1) * capacity]

    @pl.when(expert + 1 == count)
    def _():
        number = lax.broadcasted_iota(jnp.int32, (EXPERTS, tokens), 0)
        router_total = jnp.zeros(grad_router.shape, f32)
        for block in range(ranks):
            weight = gates[block]
            own_grads = jnp.zeros((EXPERTS, tokens), f32)
            for e in range(experts_here):
                here = number == info[2] * experts_here + e
                own_grads = jnp.where(here, d_gates[block, e : e + 1, :], own_grads)
            inner = jnp.sum(weight * own_grads, axis=0, keepdims=True)
            d_logits = (weight * (own_grads - inner)).astype(bf16)
            router_total = router_total + dot(d_logits, everyone[block])
            back = dot(hits[block], d_rows[block], 0, 0) + dot(d_logits, router[...], 0, 0)
            sums[block] = back.astype(bf16)
        grad_router[...] = router_total


def expert_grads_kernel(info, *refs):
    *arrays, out = refs
    ranks, capacity, width = arrays[0].shape
    pairs = out.shape[0]
    hidden = arrays[4].shape[2]
    wide, narrow, half = width // (2 * pairs), hidden // (2 * pairs), width // 2
    sides = [arrays[:5], arrays[5:]]
    incoming = [grad_rows[...].reshape(ranks * capacity, width) for rows, grad_rows, *_ in sides]
    for pair in range(pairs):
        owner = 2 * pair + info[1] % 2
        column = pl.multiple_of(owner * wide, wide)
        gate = up = None
        for rows, grad_rows, d_gate, d_up, activated in sides:
            mine = rows[:, :, pl.ds(column, wide)].reshape(ranks * capacity, wide)
            gate_term, up_term = dot(mine, d_gate[0], 0, 0), dot(mine, d_up[0], 0, 0)
            gate = gate_term if gate is None else gate + gate_term
            up = up_term if up is None else up + up_term
        out[pair, 0, :wide] = gate.astype(bf16)
        out[pair, 0, wide : 2 * wide] = up.astype(bf16)
        if narrow % LANES == 0:
            column = pl.multiple_of(owner * narrow, narrow)
            down = sum(
                dot(side[4][0, :, pl.ds(column, narrow)], rows, 0, 0) for side, rows in zip(sides, incoming)
            ).astype(bf16)
            out[pair, 0, 2 * wide : 2 * wide + narrow] = down[:, :half]
            out[pair, 0, 2 * wide + narrow :] = down[:, half:]
    if narrow % LANES:
        down = sum(dot(side[4][0], rows, 0, 0) for side, rows in zip(sides, incoming)).astype(bf16)
        for p in range(2 * pairs):

            @pl.when(info[1] % 2 == p % 2)
            def _():
                part = down[p * narrow : (p + 1) * narrow]
                out[p // 2, 0, 2 * wide : 2 * wide + narrow] = part[:, :half]
                out[p // 2, 0, 2 * wide + narrow :] = part[:, half:]


def layer_project(x, weights, tables, info, waits=()):
    (gain_attn, gain_moe, router, owns, dense_parts) = weights
    w_query, w_key, w_value, w_out = owns[:4]
    cosine, sine = tables[:2]
    rows, width = x.shape
    pieces = dp_size()
    kv_width = 2 * KV_HEADS * HEAD_DIM
    return call(
        functools.partial(project_kernel, pieces),
        (struct((rows, width), bf16), struct((rows, kv_width), bf16)),
        [SMEM] + [VMEM] * 4 + [ANY] * (3 + pieces),
        (VMEM, VMEM),
        [pltpu.VMEM((width, width + kv_width), bf16), pltpu.SemaphoreType.DMA],
        flops=2 * rows * width * (width + kv_width),
        bytes_accessed=2 * width * (width + kv_width),
        name="project",
        waits=waits,
    )(info, x, gain_attn, cosine, sine, w_query, w_key, w_value, *dense_parts)


def earlier_keys(keyval, tables):
    earlier, moving = [], keyval
    for _ in range(tables[-1]):
        moving = shifted(moving, "expert", 1)
        earlier.append(moving)
    return earlier


def layer_attend(x, query, keyval, earlier, weights, tables, info, waits=()):
    (gain_attn, gain_moe, router, owns, dense_parts) = weights
    w_out = owns[3]
    cosine, sine, query_docs, key_docs, usable, reach = tables
    rows, width = x.shape
    pieces = dp_size()
    kv_width = 2 * KV_HEADS * HEAD_DIM
    keys = (reach + 1) * rows
    return call(
        functools.partial(attend_kernel, pieces, reach),
        (
            struct((rows, width), bf16),
            struct((rows, LANES), f32),
            struct((rows, width), f32),
            struct((rows, width), bf16),
        ),
        [SMEM, VMEM] + [ANY] * (1 + reach) + [VMEM] * 4 + [ANY] * (1 + pieces),
        (VMEM,) * 4,
        [
            pltpu.VMEM((keys, kv_width), bf16),
            pltpu.VMEM((rows, keys), f32),
            pltpu.VMEM((width, width), bf16),
            pltpu.SemaphoreType.DMA,
            pltpu.SemaphoreType.DMA,
        ],
        flops=16 * rows * keys * width,
        bytes_accessed=2 * width * width,
        name="attend",
        waits=waits,
    )(info, query, keyval, *earlier, query_docs, key_docs, x, gain_moe, w_out, *dense_parts)


def layer_experts(x, query, keyval, earlier, attended, line_blocks, weights, tables, info, routes, waits=()):
    (gain_attn, gain_moe, router, owns, dense_parts, expert_parts) = weights
    w_gate, w_up, w_down = owns[4:]
    usable = tables[4]
    mixed, log_total, middle, routed = attended
    ups, downs = line_blocks
    rows, width = x.shape
    pieces = dp_size()
    ranks = lax.axis_size("expert")
    experts_here, _, hidden = w_gate.shape
    capacity = rows * TOPK // EXPERTS
    slots = experts_here * capacity
    sums, everyone, expert_rows, gates, codes, gate_pre, up_pre = call(
        functools.partial(experts_kernel, pieces, ranks, len(expert_parts)),
        (
            struct((ranks, rows, width), bf16),
            struct((ranks, rows, width), bf16),
            struct((ranks, slots, width), bf16),
            struct((ranks, EXPERTS, rows), f32),
            struct((ranks, EXPERTS, rows), f32),
            struct((experts_here, ranks * capacity, hidden), bf16),
            struct((experts_here, ranks * capacity, hidden), bf16),
        ),
        [SMEM] + [ANY] * (2 * ranks - 1) + [VMEM] * 3 + [ANY] * (3 + pieces * len(expert_parts)),
        (VMEM,) * 5
        + (pl.BlockSpec((1, ranks * capacity, hidden), lambda e: (e, 0, 0)),) * 2,
        [
            pltpu.VMEM((ranks, slots, rows), bf16),
            pltpu.VMEM((ranks, slots, width), bf16),
            pltpu.VMEM((2, width, hidden), bf16),
            pltpu.VMEM((2, width, hidden), bf16),
            pltpu.VMEM((2, hidden, width), bf16),
            pltpu.SemaphoreType.DMA((2, 3)),
            pltpu.SemaphoreType.DMA,
        ],
        grid=(experts_here,),
        flops=6 * experts_here * ranks * capacity * width * hidden,
        bytes_accessed=6 * experts_here * width * hidden,
        name="experts",
        waits=waits,
    )(
        info, routed, *ups, *downs, routes, usable, router, w_gate, w_up, w_down,
        *[piece for chunk in expert_parts for piece in chunk],
    )
    kept = (x, query, keyval, earlier, mixed, log_total, middle, everyone, expert_rows, gates, codes, gate_pre, up_pre)
    return middle, sums, kept


def layer_result(middle, sums, ties={}):
    return (middle + line_reduce(sums, ties)).astype(bf16)


def layer_backward(layer, grad, grad_line, kept, weights, tables, info, waits={}):
    (gain_attn, gain_moe, router, owns, dense_parts, expert_parts) = weights
    w_query, w_key, w_value, w_out, w_gate, w_up, w_down = owns
    cosine, sine, query_docs, key_docs, usable, reach = tables
    (x, query, keyval, earlier, mixed, log_total, middle, everyone, expert_rows, gates, codes, gate_pre, up_pre) = kept
    rows, width = x.shape
    ranks = lax.axis_size("expert")
    pieces = dp_size()
    kv_width = 2 * KV_HEADS * HEAD_DIM
    keys = (reach + 1) * rows
    experts_here, _, hidden = w_gate.shape
    capacity = rows * TOPK // EXPERTS
    slots = experts_here * capacity
    ups, downs = grad_line
    per_expert = pl.BlockSpec((1, ranks * capacity, hidden), lambda e: (e, 0, 0))
    sums, grad_router, grad_rows, d_gate, d_up, activated = call(
        functools.partial(experts_back_kernel, pieces, ranks, len(expert_parts)),
        (
            struct((ranks, rows, width), bf16),
            struct((EXPERTS, width), f32),
            struct((ranks, slots, width), bf16),
        )
        + (struct((experts_here, ranks * capacity, hidden), bf16),) * 3,
        [SMEM] + [ANY] * (2 * ranks - 1) + [VMEM] * 4 + [per_expert] * 2
        + [ANY] * (3 + pieces * len(expert_parts)),
        (VMEM,) * 3 + (per_expert,) * 3,
        [
            pltpu.VMEM((ranks, rows, width), bf16),
            pltpu.VMEM((ranks, slots, rows), bf16),
            pltpu.VMEM((ranks, slots, LANES), f32),
            pltpu.VMEM((ranks, max(8, experts_here), rows), f32),
            pltpu.VMEM((ranks, slots, width), bf16),
            pltpu.VMEM((2, width, hidden), bf16),
            pltpu.VMEM((2, width, hidden), bf16),
            pltpu.VMEM((2, hidden, width), bf16),
            pltpu.SemaphoreType.DMA((2, 3)),
            pltpu.SemaphoreType.DMA,
        ],
        grid=(experts_here,),
        flops=6 * experts_here * ranks * capacity * width * hidden,
        bytes_accessed=6 * experts_here * width * hidden,
        name="experts_back",
        waits=waits.get("experts_back", ()),
    )(
        info, grad, *ups, *downs, everyone, gates, codes, router, gate_pre, up_pre, w_gate, w_up, w_down,
        *[piece for chunk in expert_parts for piece in chunk],
    )
    wide, narrow = width // pieces, hidden // pieces
    piece_rows = 2 * wide + 2 * narrow
    chunk_count = min(2 if layer == 1 else 4, experts_here)
    per_chunk = experts_here // chunk_count
    marks = []
    if "reduce" in waits:
        sums, *waits["reduce"] = tie(sums, *waits["reduce"])
    d_routed = line_reduce(sums, marks=marks)
    marks += marks[-1:] * 2
    own_terms = (expert_rows, grad_rows, d_gate, d_up, activated)
    near_terms = [swapped(term, "near", 1) for term in own_terms]
    pairs = []

    def gradients(*others):
        c = len(pairs)
        place = functools.partial(lambda c, e: (c * per_chunk + e, 0, 0), c)
        row_place = functools.partial(lambda c, e: (0, c * per_chunk + e, 0), c)
        in_specs = [pl.BlockSpec((ranks, capacity, width), row_place)] * 2 + [
            pl.BlockSpec((1, ranks * capacity, hidden), place)
        ] * 3
        pairs.append(
            call(
                expert_grads_kernel,
                struct((pieces // 2, per_chunk, piece_rows, hidden), bf16),
                [SMEM] + in_specs * 2,
                pl.BlockSpec((pieces // 2, 1, piece_rows, hidden), lambda e: (0, e, 0, 0)),
                [],
                grid=(per_chunk,),
                flops=6 * per_chunk * ranks * capacity * width * hidden,
                bytes_accessed=9 * per_chunk * width * hidden,
                name="expert_grads",
                waits=[*others, *pairs[-1:]],
            )(info, *own_terms, *near_terms)
        )

    gradients(*marks[0], *waits.get("expert_grads", ()))
    if layer == 0:
        gradients(*marks[1])
    outs = call(
        functools.partial(attend_back_kernel, pieces, reach),
        (
            struct((rows, width), f32),
            struct((rows, width), bf16),
            struct((rows, kv_width), f32),
        )
        + (struct((rows, kv_width), bf16),) * reach
        + (struct((pieces // 2, width // pieces, width), bf16),) * 2
        + (struct((1, width), f32),),
        [SMEM] + [VMEM] * 7 + [ANY] * (1 + reach) + [VMEM] * 4 + [ANY] * (1 + pieces),
        (VMEM,) * (6 + reach),
        [
            pltpu.VMEM((keys, kv_width), bf16),
            pltpu.VMEM((rows, keys), f32),
            pltpu.VMEM((width, width), bf16),
            pltpu.VMEM((rows, width), bf16),
            pltpu.VMEM((kv_width, keys), f32),
            pltpu.SemaphoreType.DMA,
            pltpu.SemaphoreType.DMA,
        ],
        flops=40 * rows * keys * width,
        bytes_accessed=2 * width * width,
        name="attend_back",
        waits=pairs[:1],
    )(
        info, d_routed, grad[:, :width], middle, gain_moe, mixed, query, log_total, keyval, *earlier,
        query_docs, key_docs, cosine, sine, w_out, *dense_parts,
    )
    d_middle, d_query, d_own = outs[:3]
    d_earlier = outs[3 : 3 + reach]
    out_keep, out_send, grad_gain_moe = outs[3 + reach :]
    gradients(d_query)
    moving = d_earlier[reach - 1]
    for s in reversed(range(reach)):
        moving = shifted(moving, "expert", -1)
        if s > 0:
            moving = (moving.astype(f32) + d_earlier[s - 1].astype(f32)).astype(bf16)
    piece_struct = struct((pieces // 2, width // pieces, width), bf16)
    d_normed, query_keep, query_send = call(
        functools.partial(query_back_kernel, pieces),
        (struct((rows, width), f32), piece_struct, piece_struct),
        [SMEM] + [VMEM] * 3 + [ANY] * (1 + pieces),
        (VMEM,) * 3,
        [pltpu.VMEM((width, width), bf16), pltpu.SemaphoreType.DMA],
        flops=4 * rows * width * width,
        bytes_accessed=4 * width * width,
        name="query_back",
        waits=pairs[-1:],
    )(info, x, gain_attn, d_query, w_query, *dense_parts)
    if layer == 0:
        gradients(d_normed)
    kv_struct = struct((pieces // 2, width // pieces, kv_width + LANES), bf16)
    d_x, kv_keep, kv_send = call(
        functools.partial(keyval_back_kernel, pieces),
        (struct((rows, width), bf16), kv_struct, kv_struct),
        [SMEM] + [VMEM] * 10 + [ANY] * (2 + pieces),
        (VMEM,) * 3,
        [
            pltpu.VMEM((width, kv_width), bf16),
            pltpu.VMEM((rows, kv_width), bf16),
            pltpu.SemaphoreType.DMA,
        ],
        flops=4 * rows * width * kv_width,
        bytes_accessed=4 * width * kv_width,
        name="keyval_back",
        waits=pairs[-1:] if layer == 0 else (),
    )(
        info, x, gain_attn, d_own, moving, d_normed, d_middle, cosine, sine, grad_router, grad_gain_moe,
        w_key, w_value, *dense_parts,
    )
    dense = jnp.concatenate(
        [
            near_sum(keep, send)
            for keep, send in ((out_keep, out_send), (query_keep, query_send), (kv_keep, kv_send))
        ],
        axis=2,
    )
    expert_sums = [lax.psum_scatter(pair, "far", scatter_dimension=0, tiled=True)[0] for pair in pairs]
    return d_x, expert_sums, dense


def doc_ids(lengths, positions):
    endings = jnp.cumsum(lengths)
    return jnp.sum((positions[:, None] >= endings[None, :]).astype(jnp.int32), axis=1)


def per_device(
    inputs, cotangent, gain_attn, w_query, w_key, w_value, w_out, gain_moe, w_router, w_gate, w_up, w_down,
    doc_lengths, routes,
):
    rows, width = inputs.shape[2:]
    ranks = lax.axis_size("expert")
    pieces = dp_size()
    section = lax.axis_index("section")
    place = lax.axis_index("far") * 2 + lax.axis_index("near")
    line = lax.axis_index("expert")
    experts_here, _, hidden = w_gate.shape[1:]
    first = section == 0

    def mine(values):
        return lax.dynamic_index_in_dim(values, section, 0, False)

    def other(values):
        return lax.dynamic_index_in_dim(values, 1 - section, 0, False)

    x = mine(inputs[:, 0])
    top = mine(cotangent[:, 0])
    lengths = mine(doc_lengths[:, 0])

    wide, narrow = width // pieces, hidden // pieces
    where = jnp.stack([jnp.int32(0), place, line]).astype(jnp.int32)
    dense_own = (w_query[0], w_key[0], w_value[0], w_out[0])
    small = jnp.concatenate([w_router[0].T.astype(f32), gain_attn, gain_moe], axis=0)
    other_small = swapped(small, "section", 1)
    here = routes[0, :, 0]
    my_routes = mine(here)
    other_routes = swapped(other(here), "section", 1)
    dense_piece, other_small, other_routes = tie(pack_dense(where, dense_own, pieces), other_small, other_routes)
    dense_first_hop = swapped(dense_piece, "section", 1)
    both = jnp.concatenate(
        [jnp.where(first, my_routes, other_routes), jnp.where(first, other_routes, my_routes)], axis=1
    )
    named = jnp.pad(both.astype(bf16), ((0, 0), (0, LANES - 2 * TOPK)))
    top_named = jnp.concatenate([top, named], axis=1)
    top_line = line_gather(top_named)
    dense_first_hop, top_line[0][0], top_line[1][0] = tie(dense_first_hop, top_line[0][0], top_line[1][0])
    cyclic = [top_named] + [
        jnp.where(line >= s, top_line[0][s - 1], top_line[1][ranks - s - 1]) for s in range(1, ranks)
    ]
    cyclic = jnp.stack([block[:, width : width + 2 * TOPK] for block in cyclic[::-1]] * 2)
    both = lax.dynamic_slice_in_dim(cyclic, ranks - 1 - line, ranks, 0).reshape(ranks * rows, 2 * TOPK)
    both = both.T.astype(jnp.int32).reshape(2, TOPK, ranks * rows)
    def with_line(piece, bit):
        if bit == 1:
            piece, top_line[0][-1], top_line[1][-1] = tie(piece, top_line[0][-1], top_line[1][-1])
        return piece

    dense_parts = spread_pieces(dense_first_hop, with_line)
    sizes = [2, 2, 2, 1, 1] if experts_here == 8 else [1] * experts_here
    packs = [
        pack_experts(where, (w_gate[0], w_up[0], w_down[0]), pieces, sum(sizes[:c]), size)
        for c, size in enumerate(sizes)
    ]

    owns = (w_query[0], w_key[0], w_value[0], w_out[0], w_gate[0], w_up[0], w_down[0])
    offset = line * rows
    reach = min((WINDOW - 1) // rows + 1, ranks - 1)
    positions = offset + jnp.arange(rows, dtype=jnp.int32)
    key_places = offset - reach * rows + jnp.arange((reach + 1) * rows, dtype=jnp.int32)
    query_docs = doc_ids(lengths, positions)[:, None]
    key_docs = jnp.where(key_places >= 0, doc_ids(lengths, key_places), -1)[None, :]
    usable = (doc_ids(lengths, jnp.arange(ranks * rows, dtype=jnp.int32)) < NDOC).astype(jnp.int32)[None, :]
    half = HEAD_DIM // 2
    inverse = 10000.0 ** (-(jnp.arange(half, dtype=f32) * (2.0 / HEAD_DIM)))
    angles = positions.astype(f32)[:, None] * inverse[None, :]
    cosine = jnp.tile(jnp.cos(angles), (1, 4))
    sine = jnp.sin(angles)
    sine = jnp.concatenate([-sine, sine, -sine, sine], axis=1)
    tables = (cosine, sine, query_docs, key_docs, usable, reach)

    weights = []
    infos = []
    for layer in range(2):
        held = section == layer
        table = jnp.where(held, small, other_small)
        vectors = (table[EXPERTS : EXPERTS + 1], table[EXPERTS + 1 :], table[:EXPERTS].astype(bf16))
        weights.append(vectors + (owns, dense_parts))
        infos.append(jnp.stack([held.astype(jnp.int32), place, line]).astype(jnp.int32))

    marks = []

    def next_chunk(*mark):
        chunk, = crossing[:1]
        del crossing[0]
        if mark:
            chunk, seen = tie(chunk, *mark)
            marks.append(seen)
        expert_parts.append(spread_pieces(chunk))
        if packs:
            piece, _ = tie(packs.pop(0), chunk)
            crossing.append(swapped(piece, "section", 1))

    expert_parts = []
    piece, dense_gone = tie(packs.pop(0), dense_first_hop)
    crossing = [swapped(piece, "section", 1)]
    if packs:
        crossing.append(swapped(packs.pop(0), "section", 1))
    query, keyval = layer_project(x, weights[0], tables, infos[0], [dense_gone])
    next_chunk()
    earlier = earlier_keys(keyval, tables)
    next_chunk(earlier[-1])
    attended = layer_attend(x, query, keyval, earlier, weights[0], tables, infos[0])
    line_blocks = line_gather(attended[-1])
    for block in line_blocks[0]:
        if crossing:
            next_chunk(block)
    while crossing:
        next_chunk()
    layers = [weight + (expert_parts,) for weight in weights]
    middle, sums, kept_first = layer_experts(
        x, query, keyval, earlier, attended, line_blocks, layers[0], tables, infos[0], both[0], marks
    )
    between = layer_result(middle, sums)
    query, keyval = layer_project(between, weights[1], tables, infos[1])
    earlier = earlier_keys(keyval, tables)
    attended = layer_attend(between, query, keyval, earlier, weights[1], tables, infos[1])
    middle, sums, kept_second = layer_experts(
        between, query, keyval, earlier, attended, line_gather(attended[-1]), layers[1], tables, infos[1], both[1]
    )
    d_between, experts_second, dense_second = layer_backward(
        1, top_named, top_line, kept_second, layers[1], tables, infos[1]
    )
    between_line = line_gather(d_between)
    half = experts_second[0].shape[0] // 2
    def to_give(of_first, of_second):
        return jnp.where(first, of_second, of_first)

    dense_second = lax.psum_scatter(dense_second, "far", scatter_dimension=0, tiled=True)[0]
    waits = {"experts_back": experts_second[:1], "reduce": experts_second[1:], "expert_grads": [dense_second]}
    d_first, experts_first, dense_first = layer_backward(
        0, d_between, between_line, kept_first, layers[0], tables, infos[0], waits
    )
    experts_second[1:] = waits["reduce"]
    second = [part for of_second in experts_second for part in (of_second[:half], of_second[half:])]
    sums, d_first, dense_first = tie(sums, d_first, dense_first)
    got = [swapped(to_give(a, b), "section", 1) for a, b in zip(experts_first[:2], second)]
    for bit in fetch_bits()[:-1]:
        parts = dense_first.reshape((2, -1) + dense_first.shape[1:])
        high = (place // bit) % 2
        keep = lax.dynamic_index_in_dim(parts, high, 0, False)
        send = lax.dynamic_index_in_dim(parts, 1 - high, 0, False)
        dense_first = (keep.astype(f32) + dp_swapped(send, bit).astype(f32)).astype(bf16)
    ties = {2: got, 3: [dense_first]}
    final = layer_result(middle, sums, ties)
    dense_first, got = ties[3][0], list(ties[2])
    last = len(experts_first) - 1
    got += [None] * (last - 1)
    behind = 0
    for c in range(2, last + 1):
        experts_first[c], got[behind] = tie(experts_first[c], got[behind])
        got[c] = swapped(to_give(experts_first[c], second[c]), "section", 1)
        behind = c
    dense = jnp.concatenate([dense_first.reshape(dense_second.shape), dense_second], axis=1)
    ties = {2: got[2:3]}
    dense = line_reduce(dense.reshape(ranks, -1, dense.shape[1]), ties).astype(bf16)
    dense_first, dense_second = jnp.split(dense, 2, axis=1)
    got[2], d_first, final = tie(*ties[2], d_first, final)

    def by_section(of_first, of_second, got=None):
        held = jnp.where(first, of_first, of_second)
        if got is None:
            got = swapped(jnp.where(first, of_second, of_first), "section", 1)
        return jnp.stack([jnp.where(first, held, got), jnp.where(first, got, held)])

    def total(of_first, of_second, got):
        return jnp.where(first, of_first, of_second).astype(f32) + got.astype(f32)

    outputs = by_section(between, final)
    input_grads = by_section(d_first, d_between)
    chunks = [total(*terms) for terms in zip(experts_first, second, got)]
    grad_gate = jnp.concatenate([c[:, :wide] for c in chunks], axis=0)
    grad_up = jnp.concatenate([c[:, wide : 2 * wide] for c in chunks], axis=0)
    grad_down = jnp.concatenate(
        [
            jnp.concatenate([c[:, 2 * wide : 2 * wide + narrow], c[:, 2 * wide + narrow :]], axis=2)
            for c in chunks
        ],
        axis=0,
    )
    dense = total(dense_first, dense_second, swapped(to_give(dense_first, dense_second), "section", 1))
    grad_out, grad_query, grad_keyval = dense[:, :width], dense[:, width : 2 * width], dense[:, 2 * width : 3 * width]
    vectors = dense[:, 3 * width :]
    kv_half = KV_HEADS * HEAD_DIM
    return (
        outputs[None, :, None],
        input_grads[None, :, None],
        vectors[:, EXPERTS + 1][None],
        grad_query[None],
        grad_keyval[:, :kv_half][None],
        grad_keyval[:, kv_half:][None],
        grad_out[None],
        vectors[:, EXPERTS][None],
        vectors[:, :EXPERTS][None],
        grad_gate[None],
        grad_up[None],
        grad_down[None],
    )


def solution(mesh):
    placed = (
        P(None, ("far", "near"), "expert", None),
        P(None, ("far", "near"), "expert", None),
        P("section", None),
        P("section", None, None),
        P("section", None, None),
        P("section", None, None),
        P("section", None, None),
        P("section", None),
        P("section", None, None),
        P("section", "expert", None, None),
        P("section", "expert", None, None),
        P("section", "expert", None, None),
        P(None, ("far", "near"), None),
        P("section", None, ("far", "near"), "expert", None),
    )
    sections, dp, ranks = mesh.devices.shape
    devices = mesh.devices.reshape(sections, dp // 2, 2, ranks)
    split = jax.sharding.Mesh(devices, ("section", "far", "near", "expert"))
    return jax.shard_map(
        per_device,
        mesh=split,
        in_specs=placed,
        out_specs=(
            P("section", None, ("far", "near"), "expert", None),
            P("section", None, ("far", "near"), "expert", None),
            P("section", ("far", "near", "expert")),
            P("section", ("far", "near", "expert"), None),
            P("section", ("far", "near", "expert"), None),
            P("section", ("far", "near", "expert"), None),
            P("section", ("far", "near", "expert"), None),
            P("section", ("far", "near", "expert")),
            P("section", ("far", "near", "expert"), None),
            P("section", "expert", ("far", "near"), None),
            P("section", "expert", ("far", "near"), None),
            P("section", "expert", ("far", "near"), None),
        ),
        check_vma=False,
    )
```

```python
import functools

import jax
import jax.numpy as jnp
from jax import lax
from jax.experimental import pallas as pl
from jax.experimental.pallas import tpu as pltpu
from jax.sharding import PartitionSpec as P

HEADS = 16
KV_HEADS = 8
HEAD_DIM = 64
EXPERTS = 32
TOPK = 8
WINDOW = 512
NDOC = 4
EPSILON = 1e-06
MASKED = -1e30
LANES = 128
VMEM_BYTES = 56 * 1024 * 1024
bf16 = jnp.bfloat16
f32 = jnp.float32


def shifted(value, axis, steps, sources=None):
    count = lax.axis_size(axis)
    initial, last = (max(0, -steps), min(count, count - steps))
    names = range(initial, last) if sources is None else sources
    return lax.ppermute(value, axis, [(source, source + steps) for source in names])


def swapped(value, axis, bit):
    count = lax.axis_size(axis)
    return lax.ppermute(value, axis, [(source, source ^ bit) for source in range(count)])


def tie(*values):
    return lax.optimization_barrier(values)


def line_gather(block):
    ups, downs = [], []
    up, down = block, block
    for _ in range(lax.axis_size("expert") - 1):
        up = shifted(up, "expert", 1)
        down = shifted(down, "expert", -1)
        ups.append(up)
        downs.append(down)
    return ups, downs


def line_reduce(parts, ties={}, marks=None):
    ranks = lax.axis_size("expert")
    me = lax.axis_index("expert")

    def pick(index):
        return lax.dynamic_index_in_dim(parts, jnp.clip(index, 0, ranks - 1), 0, False)

    up = down = None
    for step in range(1, ranks):
        up_part = pick(me + ranks - step)
        down_part = pick(me - ranks + step)
        up = up_part if up is None else (up.astype(f32) + up_part.astype(f32)).astype(bf16)
        down = down_part if down is None else (down.astype(f32) + down_part.astype(f32)).astype(bf16)
        if step in ties:
            up, down, *ties[step] = tie(up, down, *ties[step])
        up = shifted(up, "expert", 1, range(0, step))
        down = shifted(down, "expert", -1, range(ranks - step, ranks))
        if marks is not None:
            marks.append([up, down])
    return pick(me).astype(f32) + up.astype(f32) + down.astype(f32)


def dp_size():
    return lax.axis_size("far") * lax.axis_size("near")


def dp_swapped(value, bit):
    return swapped(value, "near", 1) if bit == 1 else swapped(value, "far", bit // 2)


def fetch_bits():
    bits, bit = [], dp_size() // 2
    while bit >= 1:
        bits.append(bit)
        bit //= 2
    return bits


def spread_pieces(piece, before=None):
    pieces = {0: piece}
    for bit in fetch_bits():
        for k in list(pieces):
            if before is not None and k == max(pieces):
                pieces[k] = before(pieces[k], bit)
            pieces[k | bit] = dp_swapped(pieces[k], bit)
    return [pieces[k] for k in range(len(pieces))]


def near_sum(keep, send):
    return (keep.astype(f32) + swapped(send, "near", 1).astype(f32)).astype(bf16)


def call(
    kernel, out_shape, in_specs, out_specs, scratch, grid=None, flops=0, bytes_accessed=0, name=None, waits=()
):
    extra = {} if grid is None else {"grid": grid}
    begin, end = len(in_specs), len(in_specs) + len(waits)
    run = pl.pallas_call(
        lambda *refs: kernel(*refs[:begin], *refs[end:]),
        out_shape=out_shape,
        in_specs=[*in_specs, *[ANY] * len(waits)],
        out_specs=out_specs,
        scratch_shapes=scratch,
        compiler_params=pltpu.CompilerParams(vmem_limit_bytes=VMEM_BYTES),
        cost_estimate=pl.CostEstimate(flops=flops, bytes_accessed=bytes_accessed, transcendentals=0),
        name=name,
        **extra,
    )
    return lambda *args: run(*args, *waits)


SMEM = pl.BlockSpec(memory_space=pltpu.SMEM)
VMEM = pl.BlockSpec(memory_space=pltpu.VMEM)
ANY = pl.BlockSpec(memory_space=pl.ANY)


def struct(shape, dtype):
    return jax.ShapeDtypeStruct(shape, dtype)


def dot(left, right, left_dim=1, right_dim=0):
    return lax.dot_general(left, right, (((left_dim,), (right_dim,)), ((), ())), preferred_element_type=f32)


def upper_lanes(shape):
    return lax.broadcasted_iota(jnp.int32, shape, 1) % LANES >= HEAD_DIM


def half_swap(tile):
    lane = lax.broadcasted_iota(jnp.int32, tile.shape, 1)
    half = HEAD_DIM // 2
    return jnp.where(
        lane % HEAD_DIM < half, pltpu.roll(tile, LANES - half, 1), pltpu.roll(tile, half, 1)
    )


def load_dense(info, owns, pieces, first, width, target, sem):
    rows = target.shape[0] // len(pieces)

    @pl.when(info[0] == 1)
    def _():
        start = 0
        for own in owns:
            size = own.shape[1]
            pltpu.make_async_copy(own, target.at[:, pl.ds(start, size)], sem).start()
            start += size

    @pl.when(info[0] == 0)
    def _():
        for k, piece in enumerate(pieces):
            place = pl.multiple_of((info[1] ^ k) * rows, rows)
            pltpu.make_async_copy(
                piece.at[:, pl.ds(first, width)], target.at[pl.ds(place, rows), :], sem
            ).start()


def wait_dense(target, sem):
    pltpu.make_async_copy(target, target, sem).wait()


def load_experts(info, owns, chunks, expert, slot, buffers, sems):
    gate_buf, up_buf, down_buf = buffers
    pieces = len(chunks[0])
    wide = gate_buf.shape[1] // pieces
    narrow = down_buf.shape[1] // pieces
    half = down_buf.shape[2] // 2

    @pl.when(info[0] == 1)
    def _():
        for own, buf, index in zip(owns, buffers, range(3)):
            pltpu.make_async_copy(own.at[expert], buf.at[slot], sems.at[slot, index]).start()

    begin = 0
    for chunk in chunks:
        first, begin = begin, begin + chunk[0].shape[0]

        @pl.when((info[0] == 0) & (expert >= first) & (expert < begin))
        def _():
            local = expert - first
            for k, piece in enumerate(chunk):
                owner = info[1] ^ k
                row = pl.multiple_of(owner * wide, wide)
                low = pl.multiple_of(owner * narrow, narrow)
                pltpu.make_async_copy(
                    piece.at[local, pl.ds(0, wide)], gate_buf.at[slot, pl.ds(row, wide)], sems.at[slot, 0]
                ).start()
                pltpu.make_async_copy(
                    piece.at[local, pl.ds(wide, wide)], up_buf.at[slot, pl.ds(row, wide)], sems.at[slot, 1]
                ).start()
                for side in range(2):
                    pltpu.make_async_copy(
                        piece.at[local, pl.ds(2 * wide + side * narrow, narrow)],
                        down_buf.at[slot, pl.ds(low, narrow), pl.ds(side * half, half)],
                        sems.at[slot, 2],
                    ).start()


def wait_experts(slot, index, buffers, sems):
    pltpu.make_async_copy(buffers[index].at[slot], buffers[index].at[slot], sems.at[slot, index]).wait()


def load_line(info, own, ups, downs, target, sem):
    ranks = target.shape[0]
    me = info[2]
    columns = pl.ds(0, target.shape[2])
    pltpu.make_async_copy(own.at[:, columns], target.at[me], sem).start()
    for s in range(1, ranks):

        @pl.when(me >= s)
        def _():
            pltpu.make_async_copy(ups[s - 1].at[:, columns], target.at[me - s], sem).start()

        @pl.when(me < s)
        def _():
            pltpu.make_async_copy(downs[ranks - s - 1].at[:, columns], target.at[me - s + ranks], sem).start()


def wait_line(target, sem):
    pltpu.make_async_copy(target, target, sem).wait()


def write_pieces(info, value, keep, send, place):
    pieces = 2 * keep.shape[0]
    rows = value.shape[0] // pieces
    for p in range(pieces):
        part = value[p * rows : (p + 1) * rows].astype(keep.dtype)
        same = info[1] % 2 == p % 2

        @pl.when(same)
        def _():
            keep[(p // 2,) + place] = part

        @pl.when(jnp.logical_not(same))
        def _():
            send[(p // 2,) + place] = part


def rms(values):
    return lax.rsqrt(jnp.mean(values * values, axis=-1, keepdims=True) + EPSILON)


def mask_bias(info, query_docs, key_docs, bias):
    rows, keys = bias.shape
    row = lax.broadcasted_iota(jnp.int32, (rows, keys), 0)
    col = lax.broadcasted_iota(jnp.int32, (rows, keys), 1)
    distance = row + (keys - rows) - col
    allowed = (distance >= 0) & (distance < WINDOW) & (query_docs[...] == key_docs[...])
    bias[...] = jnp.where(allowed, 0.0, MASKED)


def load_keys(own, earlier, target, sem):
    rows = own.shape[0]
    reach = len(earlier)
    pltpu.make_async_copy(own, target.at[pl.ds(reach * rows, rows)], sem).start()
    for s, part in enumerate(earlier):
        pltpu.make_async_copy(part, target.at[pl.ds((reach - 1 - s) * rows, rows)], sem).start()


def doubled(pair, which):
    wide = pair.astype(f32)
    turned = pltpu.roll(wide, HEAD_DIM, 1)
    upper = upper_lanes(wide.shape)
    picked = jnp.where(upper, turned, wide) if which == 0 else jnp.where(upper, wide, turned)
    return picked.astype(bf16)


def one_head(tile, which, upper):
    return jnp.where(upper, tile, 0.0) if which == 1 else jnp.where(upper, 0.0, tile)


def pack_dense_kernel(info, *refs):
    begin = 0
    for matrix in refs[:-1]:
        width = matrix.shape[1]
        refs[-1][:, begin : begin + width] = matrix[...]
        begin += width


def pack_experts_kernel(info, gate, up, down, out):
    wide, narrow = gate.shape[1], down.shape[1]
    half = out.shape[2]
    out[0, :wide] = gate[0]
    out[0, wide : 2 * wide] = up[0]
    out[0, 2 * wide : 2 * wide + narrow] = down[0, :, :half]
    out[0, 2 * wide + narrow :] = down[0, :, half:]


def packed(kernel, out_shape, grid, in_specs, out_specs, name):
    size = 4 * functools.reduce(lambda a, b: a * b, out_shape.shape)
    return pl.pallas_call(
        kernel,
        out_shape=out_shape,
        grid_spec=pltpu.PrefetchScalarGridSpec(
            num_scalar_prefetch=1, grid=grid, in_specs=in_specs, out_specs=out_specs
        ),
        cost_estimate=pl.CostEstimate(flops=0, bytes_accessed=size, transcendentals=0),
        name=name,
    )


def pack_dense(info, matrices, pieces):
    rows = matrices[0].shape[0] // pieces
    total = sum(matrix.shape[1] for matrix in matrices)
    return packed(
        pack_dense_kernel,
        struct((rows, total), bf16),
        (1,),
        [pl.BlockSpec((rows, matrix.shape[1]), lambda i, info: (info[1], 0)) for matrix in matrices],
        pl.BlockSpec((rows, total), lambda i, info: (0, 0)),
        "pack_dense",
    )(info, *matrices)


def pack_experts(info, matrices, pieces, first, count):
    gate, up, down = matrices
    wide, narrow = gate.shape[1] // pieces, down.shape[1] // pieces
    hidden, width = gate.shape[2], down.shape[2]

    def own(e, info):
        return (first + e, info[1], 0)

    return packed(
        pack_experts_kernel,
        struct((count, 2 * wide + 2 * narrow, hidden), bf16),
        (count,),
        [
            pl.BlockSpec((1, wide, hidden), own),
            pl.BlockSpec((1, wide, hidden), own),
            pl.BlockSpec((1, narrow, width), own),
        ],
        pl.BlockSpec((1, 2 * wide + 2 * narrow, hidden), lambda e, info: (e, 0, 0)),
        "pack_experts",
    )(info, gate, up, down)


def project_kernel(pieces, info, x, gain, cosine, sine, w_query, w_key, w_value, *rest):
    parts = rest[:pieces]
    query, keyval, weights, sem = rest[pieces:]
    width = weights.shape[1]
    load_dense(info, (w_query, w_key, w_value), parts, 0, width, weights, sem)
    hidden = x[...].astype(f32)
    normed = (hidden * rms(hidden) * gain[...]).astype(bf16)
    wait_dense(weights, sem)
    q_width, k_width = w_query.shape[1], w_key.shape[1]
    cos, sin = cosine[...], sine[...]
    step = 2 * LANES
    for begin in range(0, width, step):
        product = dot(normed, weights[:, begin : begin + step])
        for inner in range(0, step, LANES):
            tile = product[:, inner : inner + LANES]
            place = begin + inner
            if place < q_width + k_width:
                tile = tile * cos + half_swap(tile) * sin
            if place < q_width:
                query[:, place : place + LANES] = tile.astype(bf16)
            else:
                place -= q_width
                keyval[:, place : place + LANES] = tile.astype(bf16)


def attend_kernel(pieces, reach, info, query, own_kv, *rest):
    earlier = rest[:reach]
    query_docs, key_docs, x, gain, w_out = rest[reach : reach + 5]
    parts = rest[reach + 5 : reach + 5 + pieces]
    mixed, log_total, middle, routed = rest[reach + 5 + pieces : reach + 9 + pieces]
    keyval, bias, weights, kv_sem, w_sem = rest[reach + 9 + pieces :]
    load_keys(own_kv, earlier, keyval, kv_sem)
    first = 2 * x.shape[1]
    load_dense(info, (w_out,), parts, first, x.shape[1], weights, w_sem)
    mask_bias(info, query_docs, key_docs, bias)
    log_total[...] = jnp.zeros_like(log_total)
    pltpu.make_async_copy(keyval, keyval, kv_sem).wait()
    kv_width = KV_HEADS * HEAD_DIM
    rows = query.shape[0]
    upper = upper_lanes((rows, LANES))
    lane = lax.broadcasted_iota(jnp.int32, (rows, LANES), 1)

    @pl.loop(0, KV_HEADS // 2)
    def _(pair):
        k_pair = keyval[:, pl.ds(pl.multiple_of(pair * LANES, LANES), LANES)]
        v_pair = keyval[:, pl.ds(pl.multiple_of(kv_width + pair * LANES, LANES), LANES)]
        for head in range(2):
            keys, values = doubled(k_pair, head), doubled(v_pair, head)
            place = pl.multiple_of((pair * 2 + head) * LANES, LANES)
            tile = query[:, pl.ds(place, LANES)].astype(f32) * HEAD_DIM ** (-0.5)
            results = []
            for g in range(2):
                scores = dot(one_head(tile, g, upper).astype(bf16), keys, 1, 1) + bias[...]
                peak = jnp.max(scores, axis=1, keepdims=True)
                expo = jnp.exp(scores - peak)
                total = jnp.sum(expo, axis=1, keepdims=True)
                results.append(dot(expo.astype(bf16), values) * (1.0 / total))
                index = (pair * 2 + head) * 2 + g
                log_total[...] = jnp.where(lane == index, peak + jnp.log(total), log_total[...])
            mixed[:, pl.ds(place, LANES)] = jnp.where(upper, results[1], results[0]).astype(bf16)

    wait_dense(weights, w_sem)
    between = x[...].astype(f32) + dot(mixed[...], weights[...])
    middle[...] = between
    routed[...] = (between * rms(between) * gain[...]).astype(bf16)


def attend_back_kernel(pieces, reach, info, d_routed, grad, middle, gain, mixed, query, log_total, own_kv, *rest):
    earlier = rest[:reach]
    query_docs, key_docs, cosine, sine, w_out = rest[reach : reach + 5]
    rest = rest[reach + 5 :]
    parts = rest[:pieces]
    rest = rest[pieces:]
    d_middle, d_query, d_own = rest[:3]
    d_earlier = rest[3 : 3 + reach]
    keep, send, grad_gain = rest[3 + reach : 6 + reach]
    keyval, bias, weights, d_mixed, d_kv, kv_sem, w_sem = rest[6 + reach :]
    load_keys(own_kv, earlier, keyval, kv_sem)
    first = 2 * middle.shape[1]
    load_dense(info, (w_out,), parts, first, middle.shape[1], weights, w_sem)
    mask_bias(info, query_docs, key_docs, bias)
    between = middle[...]
    scale = rms(between)
    normal = between * scale
    routed = d_routed[...]
    grad_gain[...] = jnp.sum(routed * normal, axis=0, keepdims=True)
    d_norm = routed * gain[...]
    total = grad[...].astype(f32) + scale * (
        d_norm - normal * jnp.mean(d_norm * normal, axis=1, keepdims=True)
    )
    d_middle[...] = total
    branch = total.astype(bf16)
    wait_dense(weights, w_sem)
    d_mixed[...] = dot(branch, weights[...], 1, 1).astype(bf16)
    write_pieces(info, dot(mixed[...], branch, 0, 0), keep, send, ())
    pltpu.make_async_copy(keyval, keyval, kv_sem).wait()
    kv_width = KV_HEADS * HEAD_DIM
    rows = query.shape[0]
    upper = upper_lanes((rows, LANES))
    lane = lax.broadcasted_iota(jnp.int32, (rows, LANES), 1)
    cos, sin = cosine[...], sine[...]

    @pl.loop(0, KV_HEADS // 2)
    def _(pair):
        k_pair = keyval[:, pl.ds(pl.multiple_of(pair * LANES, LANES), LANES)]
        v_pair = keyval[:, pl.ds(pl.multiple_of(kv_width + pair * LANES, LANES), LANES)]
        for head in range(2):
            keys, values = doubled(k_pair, head), doubled(v_pair, head)
            place = pl.multiple_of((pair * 2 + head) * LANES, LANES)
            tile = query[:, pl.ds(place, LANES)].astype(f32) * HEAD_DIM ** (-0.5)
            d_tile = d_mixed[:, pl.ds(place, LANES)].astype(f32)
            inner = d_tile * mixed[:, pl.ds(place, LANES)].astype(f32)
            dq, dk, dv = [], None, None
            for g in range(2):
                index = (pair * 2 + head) * 2 + g
                log_column = jnp.sum(jnp.where(lane == index, log_total[...], 0.0), axis=1, keepdims=True)
                weight = jnp.sum(one_head(inner, g, upper), axis=1, keepdims=True)
                own_query = one_head(tile, g, upper).astype(bf16)
                own_grad = one_head(d_tile, g, upper).astype(bf16)
                scores = dot(own_query, keys, 1, 1) + bias[...]
                probs = jnp.exp(scores - log_column)
                d_probs = dot(own_grad, values, 1, 1)
                d_scores = (probs * (d_probs - weight)).astype(bf16)
                dq.append(dot(d_scores, keys))
                k_term = dot(own_query, d_scores, 0, 0)
                v_term = dot(own_grad, probs.astype(bf16), 0, 0)
                dk = k_term if dk is None else dk + k_term
                dv = v_term if dv is None else dv + v_term
            whole = jnp.where(upper, dq[1], dq[0]) * HEAD_DIM ** (-0.5)
            whole = whole * cos - half_swap(whole) * sin
            d_query[:, pl.ds(place, LANES)] = whole.astype(bf16)
            k_row = pl.multiple_of((pair * 2 + head) * HEAD_DIM, HEAD_DIM)
            v_row = pl.multiple_of(kv_width + (pair * 2 + head) * HEAD_DIM, HEAD_DIM)
            d_kv[pl.ds(k_row, HEAD_DIM), :] = dk[:HEAD_DIM] + dk[HEAD_DIM:]
            d_kv[pl.ds(v_row, HEAD_DIM), :] = dv[:HEAD_DIM] + dv[HEAD_DIM:]

    for block in range(reach + 1):
        turned = d_kv[:, block * rows : (block + 1) * rows].T
        if block == reach:
            d_own[...] = turned
        else:
            d_earlier[reach - 1 - block][...] = turned.astype(bf16)


def query_back_kernel(pieces, info, x, gain, d_query, w_query, *rest):
    parts = rest[:pieces]
    d_normed, keep, send, weights, sem = rest[pieces:]
    load_dense(info, (w_query,), parts, 0, weights.shape[1], weights, sem)
    hidden = x[...].astype(f32)
    normed = (hidden * rms(hidden) * gain[...]).astype(bf16)
    write_pieces(info, dot(normed, d_query[...], 0, 0), keep, send, ())
    wait_dense(weights, sem)
    d_normed[...] = dot(d_query[...], weights[...], 1, 1)


def keyval_back_kernel(
    pieces, info, x, gain, d_own, d_others, d_normed, d_middle, cosine, sine, grad_router, grad_gain_moe,
    w_key, w_value, *rest,
):
    parts = rest[:pieces]
    d_x, keep, send, weights, d_pre, sem = rest[pieces:]
    load_dense(info, (w_key, w_value), parts, x.shape[1], weights.shape[1], weights, sem)
    hidden = x[...].astype(f32)
    scale = rms(hidden)
    normal = hidden * scale
    normed = (normal * gain[...]).astype(bf16)
    cos, sin = cosine[...], sine[...]
    width = w_key.shape[1]
    for place in range(0, 2 * width, LANES):
        tile = d_own[:, place : place + LANES] + d_others[:, place : place + LANES].astype(f32)
        if place < width:
            tile = tile * cos - half_swap(tile) * sin
        d_pre[:, place : place + LANES] = tile.astype(bf16)
    wait_dense(weights, sem)
    total = d_normed[...] + dot(d_pre[...], weights[...], 1, 1)
    grad_gain = jnp.sum(total * normal, axis=0, keepdims=True)
    tall = jnp.concatenate(
        [grad_router[...], jnp.zeros((LANES - EXPERTS, total.shape[1]), f32)], axis=0
    )
    row = lax.broadcasted_iota(jnp.int32, tall.shape, 0)
    tall = jnp.where(row == EXPERTS, grad_gain_moe[...], jnp.where(row == EXPERTS + 1, grad_gain, tall))
    d_norm = total * gain[...]
    d_x[...] = (
        d_middle[...]
        + scale * (d_norm - normal * jnp.mean(d_norm * normal, axis=1, keepdims=True))
    ).astype(bf16)
    both = 2 * width
    write_pieces(info, dot(normed, d_pre[...], 0, 0), keep, send, (slice(None), slice(0, both)))
    write_pieces(info, tall.T, keep, send, (slice(None), slice(both, both + LANES)))


def slot_rows(info, table, local, experts_here):
    row = lax.broadcasted_iota(jnp.int32, table.shape, 0)
    picked = jnp.where(row == info[2] * experts_here + local, table, 0.0)
    return jnp.sum(picked, axis=0, keepdims=True)


def slot_hits(codes, capacity):
    slot = lax.broadcasted_iota(jnp.int32, (capacity, codes.shape[1]), 0).astype(f32)
    return slot == codes


def experts_kernel(pieces, ranks, chunk_count, info, own, *rest):
    ups, downs = rest[: ranks - 1], rest[ranks - 1 : 2 * ranks - 2]
    rest = rest[2 * ranks - 2 :]
    routes, usable, router, w_gate, w_up, w_down = rest[:6]
    rest = rest[6:]
    chunks = [rest[c * pieces : (c + 1) * pieces] for c in range(chunk_count)]
    rest = rest[chunk_count * pieces :]
    sums, everyone_out, rows_out, gates, codes, gate_out, up_out = rest[:7]
    hits, results, gate_buf, up_buf, down_buf, everyone, rows, sems, line_sem, out_sems = rest[7:]
    kept = [
        pltpu.make_async_copy(everyone, everyone_out, out_sems.at[0]),
        pltpu.make_async_copy(rows, rows_out, out_sems.at[1]),
    ]
    expert, count = pl.program_id(0), pl.num_programs(0)
    buffers = (gate_buf, up_buf, down_buf)
    owns = (w_gate, w_up, w_down)
    experts_here = w_gate.shape[0]
    tokens = own.shape[0]
    capacity = tokens * TOPK // EXPERTS
    slot = expert % 2

    @pl.when(expert == 0)
    def _():
        load_line(info, own, ups, downs, everyone, line_sem)
        load_experts(info, owns, chunks, 0, 0, buffers, sems)
        earlier = lax.broadcasted_iota(jnp.int32, (tokens, tokens), 0)
        later = lax.broadcasted_iota(jnp.int32, (tokens, tokens), 1)
        triangle = jnp.where(earlier < later, 1.0, 0.0).astype(bf16)
        number = lax.broadcasted_iota(jnp.int32, (EXPERTS, tokens), 0)
        wait_line(everyone, line_sem)
        for block in range(ranks):
            span = slice(block * tokens, (block + 1) * tokens)
            named = routes[0:1, span] == number
            for k in range(1, TOPK):
                named = named | (routes[k : k + 1, span] == number)
            logits = jnp.where(named, dot(router[...], everyone[block], 1, 1), MASKED)
            expo = jnp.where(named, jnp.exp(logits - jnp.max(logits, axis=0, keepdims=True)), 0.0)
            weight = expo / jnp.sum(expo, axis=0, keepdims=True)
            held = named & (usable[:, span] > 0)
            rank = dot(jnp.where(held, 1.0, 0.0).astype(bf16), triangle)
            code = jnp.where(held & (rank < capacity), rank, -1.0)
            gates[block] = weight
            codes[block] = code
            for e in range(experts_here):
                hit = slot_hits(slot_rows(info, code, e, experts_here), capacity)
                hits[block, e * capacity : (e + 1) * capacity, :] = jnp.where(hit, 1.0, 0.0).astype(bf16)
            rows[block] = dot(hits[block], everyone[block]).astype(bf16)
        for copy in kept:
            copy.start()

    @pl.when(expert + 1 < count)
    def _():
        load_experts(info, owns, chunks, expert + 1, 1 - slot, buffers, sems)

    place = pl.multiple_of(expert * capacity, capacity)
    mine = jnp.concatenate([rows[block, pl.ds(place, capacity), :] for block in range(ranks)], axis=0)
    for index in range(3):
        wait_experts(slot, index, buffers, sems)
    gate_pre = dot(mine, gate_buf[slot])
    up_pre = dot(mine, up_buf[slot])
    gate_out[0] = gate_pre.astype(bf16)
    up_out[0] = up_pre.astype(bf16)
    activated = (gate_pre * jax.nn.sigmoid(gate_pre) * up_pre).astype(bf16)
    produced = dot(activated, down_buf[slot]).astype(bf16)
    for block in range(ranks):
        results[block, pl.ds(place, capacity), :] = produced[block * capacity : (block + 1) * capacity]

    @pl.when(expert + 1 == count)
    def _():
        for block in range(ranks):
            weighted = []
            for e in range(experts_here):
                weight = slot_rows(info, gates[block], e, experts_here)
                hit = hits[block, e * capacity : (e + 1) * capacity, :].astype(f32)
                weighted.append((hit * weight).astype(bf16))
            sums[block] = dot(jnp.concatenate(weighted, axis=0), results[block], 0, 0).astype(bf16)
        for copy in kept:
            copy.wait()


def experts_back_kernel(pieces, ranks, chunk_count, info, own, *rest):
    ups, downs = rest[: ranks - 1], rest[ranks - 1 : 2 * ranks - 2]
    rest = rest[2 * ranks - 2 :]
    everyone, gates, codes, router, gate_pre, up_pre, w_gate, w_up, w_down = rest[:9]
    rest = rest[9:]
    chunks = [rest[c * pieces : (c + 1) * pieces] for c in range(chunk_count)]
    rest = rest[chunk_count * pieces :]
    sums, grad_router, rows_out, gate_out, up_out, active_out = rest[:6]
    incoming, hits, columns, d_gates, d_rows, gate_buf, up_buf, down_buf = rest[6:14]
    grad_rows, sems, line_sem, out_sem = rest[14:]
    kept = pltpu.make_async_copy(grad_rows, rows_out, out_sem)
    expert, count = pl.program_id(0), pl.num_programs(0)
    buffers = (gate_buf, up_buf, down_buf)
    owns = (w_gate, w_up, w_down)
    experts_here = w_gate.shape[0]
    tokens = own.shape[0]
    capacity = tokens * TOPK // EXPERTS
    slot = expert % 2

    @pl.when(expert == 0)
    def _():
        load_line(info, own, ups, downs, incoming, line_sem)
        load_experts(info, owns, chunks, 0, 0, buffers, sems)
        for block in range(ranks):
            for e in range(experts_here):
                hit = slot_hits(slot_rows(info, codes[block], e, experts_here), capacity)
                span = slice(e * capacity, (e + 1) * capacity)
                hits[block, span, :] = jnp.where(hit, 1.0, 0.0).astype(bf16)
                weight = slot_rows(info, gates[block], e, experts_here)
                column = jnp.sum(jnp.where(hit, weight, 0.0), axis=1, keepdims=True)
                columns[block, span, :] = jnp.broadcast_to(column, (capacity, LANES))
        wait_line(incoming, line_sem)
        for block in range(ranks):
            grad_rows[block] = dot(hits[block], incoming[block]).astype(bf16)
        kept.start()

    @pl.when(expert + 1 < count)
    def _():
        load_experts(info, owns, chunks, expert + 1, 1 - slot, buffers, sems)

    place = pl.multiple_of(expert * capacity, capacity)
    mine = jnp.concatenate([grad_rows[block, pl.ds(place, capacity), :] for block in range(ranks)], axis=0)
    weight = jnp.concatenate(
        [columns[block, pl.ds(place, capacity), :] for block in range(ranks)], axis=0
    )[:, :1]
    gate = gate_pre[0].astype(f32)
    up = up_pre[0].astype(f32)
    sigma = jax.nn.sigmoid(gate)
    silu = gate * sigma
    activated = silu * up
    for index in range(3):
        wait_experts(slot, index, buffers, sems)
    unweighted = dot(mine, down_buf[slot], 1, 1)
    d_weight = jnp.sum(unweighted * activated, axis=1, keepdims=True)
    for block in range(ranks):
        hit = hits[block, pl.ds(place, capacity), :].astype(f32)
        spread = hit * d_weight[block * capacity : (block + 1) * capacity]
        d_gates[block, pl.ds(expert, 1), :] = jnp.sum(spread, axis=0, keepdims=True)
    d_active = unweighted * weight
    active_out[0] = (activated * weight).astype(bf16)
    d_gate = (d_active * up * sigma * (1.0 + gate * (1.0 - sigma))).astype(bf16)
    d_up = (d_active * silu).astype(bf16)
    gate_out[0] = d_gate
    up_out[0] = d_up
    produced = (dot(d_gate, gate_buf[slot], 1, 1) + dot(d_up, up_buf[slot], 1, 1)).astype(bf16)
    for block in range(ranks):
        d_rows[block, pl.ds(place, capacity), :] = produced[block * capacity : (block + 1) * capacity]

    @pl.when(expert + 1 == count)
    def _():
        number = lax.broadcasted_iota(jnp.int32, (EXPERTS, tokens), 0)
        router_total = jnp.zeros(grad_router.shape, f32)
        for block in range(ranks):
            weight = gates[block]
            own_grads = jnp.zeros((EXPERTS, tokens), f32)
            for e in range(experts_here):
                here = number == info[2] * experts_here + e
                own_grads = jnp.where(here, d_gates[block, e : e + 1, :], own_grads)
            inner = jnp.sum(weight * own_grads, axis=0, keepdims=True)
            d_logits = (weight * (own_grads - inner)).astype(bf16)
            router_total = router_total + dot(d_logits, everyone[block])
            back = dot(hits[block], d_rows[block], 0, 0) + dot(d_logits, router[...], 0, 0)
            sums[block] = back.astype(bf16)
        grad_router[...] = router_total
        kept.wait()


def expert_grads_kernel(info, *refs):
    *arrays, out = refs
    ranks, capacity, width = arrays[0].shape
    pairs = out.shape[0]
    hidden = arrays[4].shape[2]
    wide, narrow, half = width // (2 * pairs), hidden // (2 * pairs), width // 2
    sides = [arrays[:5], arrays[5:]]
    incoming = [grad_rows[...].reshape(ranks * capacity, width) for rows, grad_rows, *_ in sides]
    for pair in range(pairs):
        owner = 2 * pair + info[1] % 2
        column = pl.multiple_of(owner * wide, wide)
        gate = up = None
        for rows, grad_rows, d_gate, d_up, activated in sides:
            mine = rows[:, :, pl.ds(column, wide)].reshape(ranks * capacity, wide)
            gate_term, up_term = dot(mine, d_gate[0], 0, 0), dot(mine, d_up[0], 0, 0)
            gate = gate_term if gate is None else gate + gate_term
            up = up_term if up is None else up + up_term
        out[pair, 0, :wide] = gate.astype(bf16)
        out[pair, 0, wide : 2 * wide] = up.astype(bf16)
        if narrow % LANES == 0:
            column = pl.multiple_of(owner * narrow, narrow)
            down = sum(
                dot(side[4][0, :, pl.ds(column, narrow)], rows, 0, 0) for side, rows in zip(sides, incoming)
            ).astype(bf16)
            out[pair, 0, 2 * wide : 2 * wide + narrow] = down[:, :half]
            out[pair, 0, 2 * wide + narrow :] = down[:, half:]
    if narrow % LANES:
        down = sum(dot(side[4][0], rows, 0, 0) for side, rows in zip(sides, incoming)).astype(bf16)
        for p in range(2 * pairs):

            @pl.when(info[1] % 2 == p % 2)
            def _():
                part = down[p * narrow : (p + 1) * narrow]
                out[p // 2, 0, 2 * wide : 2 * wide + narrow] = part[:, :half]
                out[p // 2, 0, 2 * wide + narrow :] = part[:, half:]


def layer_project(x, weights, tables, info, waits=()):
    (gain_attn, gain_moe, router, owns, dense_parts) = weights
    w_query, w_key, w_value, w_out = owns[:4]
    cosine, sine = tables[:2]
    rows, width = x.shape
    pieces = dp_size()
    kv_width = 2 * KV_HEADS * HEAD_DIM
    return call(
        functools.partial(project_kernel, pieces),
        (struct((rows, width), bf16), struct((rows, kv_width), bf16)),
        [SMEM] + [VMEM] * 4 + [ANY] * (3 + pieces),
        (VMEM, VMEM),
        [pltpu.VMEM((width, width + kv_width), bf16), pltpu.SemaphoreType.DMA],
        flops=2 * rows * width * (width + kv_width),
        bytes_accessed=2 * width * (width + kv_width),
        name="project",
        waits=waits,
    )(info, x, gain_attn, cosine, sine, w_query, w_key, w_value, *dense_parts)


def earlier_keys(keyval, tables):
    earlier, moving = [], keyval
    for _ in range(tables[-1]):
        moving = shifted(moving, "expert", 1)
        earlier.append(moving)
    return earlier


def layer_attend(x, query, keyval, earlier, weights, tables, info, waits=()):
    (gain_attn, gain_moe, router, owns, dense_parts) = weights
    w_out = owns[3]
    cosine, sine, query_docs, key_docs, usable, reach = tables
    rows, width = x.shape
    pieces = dp_size()
    kv_width = 2 * KV_HEADS * HEAD_DIM
    keys = (reach + 1) * rows
    return call(
        functools.partial(attend_kernel, pieces, reach),
        (
            struct((rows, width), bf16),
            struct((rows, LANES), f32),
            struct((rows, width), f32),
            struct((rows, width), bf16),
        ),
        [SMEM, VMEM] + [ANY] * (1 + reach) + [VMEM] * 4 + [ANY] * (1 + pieces),
        (VMEM,) * 4,
        [
            pltpu.VMEM((keys, kv_width), bf16),
            pltpu.VMEM((rows, keys), f32),
            pltpu.VMEM((width, width), bf16),
            pltpu.SemaphoreType.DMA,
            pltpu.SemaphoreType.DMA,
        ],
        flops=16 * rows * keys * width,
        bytes_accessed=2 * width * width,
        name="attend",
        waits=waits,
    )(info, query, keyval, *earlier, query_docs, key_docs, x, gain_moe, w_out, *dense_parts)


def layer_experts(x, query, keyval, earlier, attended, line_blocks, weights, tables, info, routes, waits=()):
    (gain_attn, gain_moe, router, owns, dense_parts, expert_parts) = weights
    w_gate, w_up, w_down = owns[4:]
    usable = tables[4]
    mixed, log_total, middle, routed = attended
    ups, downs = line_blocks
    rows, width = x.shape
    pieces = dp_size()
    ranks = lax.axis_size("expert")
    experts_here, _, hidden = w_gate.shape
    capacity = rows * TOPK // EXPERTS
    slots = experts_here * capacity
    sums, everyone, expert_rows, gates, codes, gate_pre, up_pre = call(
        functools.partial(experts_kernel, pieces, ranks, len(expert_parts)),
        (
            struct((ranks, rows, width), bf16),
            struct((ranks, rows, width), bf16),
            struct((ranks, slots, width), bf16),
            struct((ranks, EXPERTS, rows), f32),
            struct((ranks, EXPERTS, rows), f32),
            struct((experts_here, ranks * capacity, hidden), bf16),
            struct((experts_here, ranks * capacity, hidden), bf16),
        ),
        [SMEM] + [ANY] * (2 * ranks - 1) + [VMEM] * 3 + [ANY] * (3 + pieces * len(expert_parts)),
        (VMEM, ANY, ANY, VMEM, VMEM)
        + (pl.BlockSpec((1, ranks * capacity, hidden), lambda e: (e, 0, 0)),) * 2,
        [
            pltpu.VMEM((ranks, slots, rows), bf16),
            pltpu.VMEM((ranks, slots, width), bf16),
            pltpu.VMEM((2, width, hidden), bf16),
            pltpu.VMEM((2, width, hidden), bf16),
            pltpu.VMEM((2, hidden, width), bf16),
            pltpu.VMEM((ranks, rows, width), bf16),
            pltpu.VMEM((ranks, slots, width), bf16),
            pltpu.SemaphoreType.DMA((2, 3)),
            pltpu.SemaphoreType.DMA,
            pltpu.SemaphoreType.DMA((2,)),
        ],
        grid=(experts_here,),
        flops=6 * experts_here * ranks * capacity * width * hidden,
        bytes_accessed=6 * experts_here * width * hidden,
        name="experts",
        waits=waits,
    )(
        info, routed, *ups, *downs, routes, usable, router, w_gate, w_up, w_down,
        *[piece for chunk in expert_parts for piece in chunk],
    )
    kept = (x, query, keyval, earlier, mixed, log_total, middle, everyone, expert_rows, gates, codes, gate_pre, up_pre)
    return middle, sums, kept


def layer_result(middle, sums, ties={}):
    return (middle + line_reduce(sums, ties)).astype(bf16)


def layer_backward(layer, grad, grad_line, kept, weights, tables, info, waits={}):
    (gain_attn, gain_moe, router, owns, dense_parts, expert_parts) = weights
    w_query, w_key, w_value, w_out, w_gate, w_up, w_down = owns
    cosine, sine, query_docs, key_docs, usable, reach = tables
    (x, query, keyval, earlier, mixed, log_total, middle, everyone, expert_rows, gates, codes, gate_pre, up_pre) = kept
    rows, width = x.shape
    ranks = lax.axis_size("expert")
    pieces = dp_size()
    kv_width = 2 * KV_HEADS * HEAD_DIM
    keys = (reach + 1) * rows
    experts_here, _, hidden = w_gate.shape
    capacity = rows * TOPK // EXPERTS
    slots = experts_here * capacity
    ups, downs = grad_line
    per_expert = pl.BlockSpec((1, ranks * capacity, hidden), lambda e: (e, 0, 0))
    sums, grad_router, grad_rows, d_gate, d_up, activated = call(
        functools.partial(experts_back_kernel, pieces, ranks, len(expert_parts)),
        (
            struct((ranks, rows, width), bf16),
            struct((EXPERTS, width), f32),
            struct((ranks, slots, width), bf16),
        )
        + (struct((experts_here, ranks * capacity, hidden), bf16),) * 3,
        [SMEM] + [ANY] * (2 * ranks - 1) + [VMEM] * 4 + [per_expert] * 2
        + [ANY] * (3 + pieces * len(expert_parts)),
        (VMEM, VMEM, ANY) + (per_expert,) * 3,
        [
            pltpu.VMEM((ranks, rows, width), bf16),
            pltpu.VMEM((ranks, slots, rows), bf16),
            pltpu.VMEM((ranks, slots, LANES), f32),
            pltpu.VMEM((ranks, max(8, experts_here), rows), f32),
            pltpu.VMEM((ranks, slots, width), bf16),
            pltpu.VMEM((2, width, hidden), bf16),
            pltpu.VMEM((2, width, hidden), bf16),
            pltpu.VMEM((2, hidden, width), bf16),
            pltpu.VMEM((ranks, slots, width), bf16),
            pltpu.SemaphoreType.DMA((2, 3)),
            pltpu.SemaphoreType.DMA,
            pltpu.SemaphoreType.DMA,
        ],
        grid=(experts_here,),
        flops=6 * experts_here * ranks * capacity * width * hidden,
        bytes_accessed=6 * experts_here * width * hidden,
        name="experts_back",
        waits=waits.get("experts_back", ()),
    )(
        info, grad, *ups, *downs, everyone, gates, codes, router, gate_pre, up_pre, w_gate, w_up, w_down,
        *[piece for chunk in expert_parts for piece in chunk],
    )
    wide, narrow = width // pieces, hidden // pieces
    piece_rows = 2 * wide + 2 * narrow
    chunk_count = min(2 if layer == 1 else 4, experts_here)
    per_chunk = experts_here // chunk_count
    marks = []
    if "reduce" in waits:
        sums, *waits["reduce"] = tie(sums, *waits["reduce"])
    if layer == 1:
        d_routed = lax.psum_scatter(sums, "expert", scatter_dimension=0, tiled=True)
        marks.append([])
    else:
        d_routed = line_reduce(sums, marks=marks)
    marks += marks[-1:] * 2
    own_terms = (expert_rows, grad_rows, d_gate, d_up, activated)
    near_terms = [swapped(term, "near", 1) for term in own_terms]
    pairs = []

    def gradients(*others):
        c = len(pairs)
        place = functools.partial(lambda c, e: (c * per_chunk + e, 0, 0), c)
        row_place = functools.partial(lambda c, e: (0, c * per_chunk + e, 0), c)
        in_specs = [pl.BlockSpec((ranks, capacity, width), row_place)] * 2 + [
            pl.BlockSpec((1, ranks * capacity, hidden), place)
        ] * 3
        pairs.append(
            call(
                expert_grads_kernel,
                struct((pieces // 2, per_chunk, piece_rows, hidden), bf16),
                [SMEM] + in_specs * 2,
                pl.BlockSpec((pieces // 2, 1, piece_rows, hidden), lambda e: (0, e, 0, 0)),
                [],
                grid=(per_chunk,),
                flops=6 * per_chunk * ranks * capacity * width * hidden,
                bytes_accessed=9 * per_chunk * width * hidden,
                name="expert_grads",
                waits=[*others, *pairs[-1:]],
            )(info, *own_terms, *near_terms)
        )

    gradients(*marks[0], *waits.get("expert_grads", ()))
    if layer == 0:
        gradients(*marks[1])
    else:
        pairs[0], d_routed = tie(pairs[0], d_routed)
        d_routed = d_routed[0].astype(f32)
    outs = call(
        functools.partial(attend_back_kernel, pieces, reach),
        (
            struct((rows, width), f32),
            struct((rows, width), bf16),
            struct((rows, kv_width), f32),
        )
        + (struct((rows, kv_width), bf16),) * reach
        + (struct((pieces // 2, width // pieces, width), bf16),) * 2
        + (struct((1, width), f32),),
        [SMEM] + [VMEM] * 7 + [ANY] * (1 + reach) + [VMEM] * 4 + [ANY] * (1 + pieces),
        (VMEM,) * (6 + reach),
        [
            pltpu.VMEM((keys, kv_width), bf16),
            pltpu.VMEM((rows, keys), f32),
            pltpu.VMEM((width, width), bf16),
            pltpu.VMEM((rows, width), bf16),
            pltpu.VMEM((kv_width, keys), f32),
            pltpu.SemaphoreType.DMA,
            pltpu.SemaphoreType.DMA,
        ],
        flops=40 * rows * keys * width,
        bytes_accessed=2 * width * width,
        name="attend_back",
        waits=pairs[:1],
    )(
        info, d_routed, grad[:, :width], middle, gain_moe, mixed, query, log_total, keyval, *earlier,
        query_docs, key_docs, cosine, sine, w_out, *dense_parts,
    )
    d_middle, d_query, d_own = outs[:3]
    d_earlier = outs[3 : 3 + reach]
    out_keep, out_send, grad_gain_moe = outs[3 + reach :]
    gradients(d_query)
    moving = d_earlier[reach - 1]
    for s in reversed(range(reach)):
        moving = shifted(moving, "expert", -1)
        if s > 0:
            moving = (moving.astype(f32) + d_earlier[s - 1].astype(f32)).astype(bf16)
    piece_struct = struct((pieces // 2, width // pieces, width), bf16)
    d_normed, query_keep, query_send = call(
        functools.partial(query_back_kernel, pieces),
        (struct((rows, width), f32), piece_struct, piece_struct),
        [SMEM] + [VMEM] * 3 + [ANY] * (1 + pieces),
        (VMEM,) * 3,
        [pltpu.VMEM((width, width), bf16), pltpu.SemaphoreType.DMA],
        flops=4 * rows * width * width,
        bytes_accessed=4 * width * width,
        name="query_back",
        waits=pairs[-1:],
    )(info, x, gain_attn, d_query, w_query, *dense_parts)
    if layer == 0:
        gradients(d_normed)
    kv_struct = struct((pieces // 2, width // pieces, kv_width + LANES), bf16)
    d_x, kv_keep, kv_send = call(
        functools.partial(keyval_back_kernel, pieces),
        (struct((rows, width), bf16), kv_struct, kv_struct),
        [SMEM] + [VMEM] * 10 + [ANY] * (2 + pieces),
        (VMEM,) * 3,
        [
            pltpu.VMEM((width, kv_width), bf16),
            pltpu.VMEM((rows, kv_width), bf16),
            pltpu.SemaphoreType.DMA,
        ],
        flops=4 * rows * width * kv_width,
        bytes_accessed=4 * width * kv_width,
        name="keyval_back",
        waits=pairs[-1:] if layer == 0 else (),
    )(
        info, x, gain_attn, d_own, moving, d_normed, d_middle, cosine, sine, grad_router, grad_gain_moe,
        w_key, w_value, *dense_parts,
    )
    dense = jnp.concatenate(
        [
            near_sum(keep, send)
            for keep, send in ((out_keep, out_send), (query_keep, query_send), (kv_keep, kv_send))
        ],
        axis=2,
    )
    expert_sums = [lax.psum_scatter(pair, "far", scatter_dimension=0, tiled=True)[0] for pair in pairs]
    return d_x, expert_sums, dense


def doc_ids(lengths, positions):
    endings = jnp.cumsum(lengths)
    return jnp.sum((positions[:, None] >= endings[None, :]).astype(jnp.int32), axis=1)


def per_device(
    inputs, cotangent, gain_attn, w_query, w_key, w_value, w_out, gain_moe, w_router, w_gate, w_up, w_down,
    doc_lengths, routes,
):
    rows, width = inputs.shape[2:]
    ranks = lax.axis_size("expert")
    pieces = dp_size()
    section = lax.axis_index("section")
    place = lax.axis_index("far") * 2 + lax.axis_index("near")
    line = lax.axis_index("expert")
    experts_here, _, hidden = w_gate.shape[1:]
    first = section == 0

    def mine(values):
        return lax.dynamic_index_in_dim(values, section, 0, False)

    def other(values):
        return lax.dynamic_index_in_dim(values, 1 - section, 0, False)

    x = mine(inputs[:, 0])
    top = mine(cotangent[:, 0])
    lengths = mine(doc_lengths[:, 0])

    wide, narrow = width // pieces, hidden // pieces
    where = jnp.stack([jnp.int32(0), place, line]).astype(jnp.int32)
    dense_own = (w_query[0], w_key[0], w_value[0], w_out[0])
    small = jnp.concatenate([w_router[0].T.astype(f32), gain_attn, gain_moe], axis=0)
    other_small = swapped(small, "section", 1)
    here = routes[0, :, 0]
    my_routes = mine(here)
    other_routes = swapped(other(here), "section", 1)
    dense_piece, other_small, other_routes = tie(pack_dense(where, dense_own, pieces), other_small, other_routes)
    dense_first_hop = swapped(dense_piece, "section", 1)
    both = jnp.concatenate(
        [jnp.where(first, my_routes, other_routes), jnp.where(first, other_routes, my_routes)], axis=1
    )
    named = jnp.pad(both.astype(bf16), ((0, 0), (0, LANES - 2 * TOPK)))
    top_named = jnp.concatenate([top, named], axis=1)
    top_line = line_gather(top_named)
    dense_first_hop, top_line[0][0], top_line[1][0] = tie(dense_first_hop, top_line[0][0], top_line[1][0])
    cyclic = [top_named] + [
        jnp.where(line >= s, top_line[0][s - 1], top_line[1][ranks - s - 1]) for s in range(1, ranks)
    ]
    cyclic = jnp.stack([block[:, width : width + 2 * TOPK] for block in cyclic[::-1]] * 2)
    both = lax.dynamic_slice_in_dim(cyclic, ranks - 1 - line, ranks, 0).reshape(ranks * rows, 2 * TOPK)
    both = both.T.astype(jnp.int32).reshape(2, TOPK, ranks * rows)
    def with_line(piece, bit):
        if bit == 1:
            piece, top_line[0][-1], top_line[1][-1] = tie(piece, top_line[0][-1], top_line[1][-1])
        return piece

    dense_parts = spread_pieces(dense_first_hop, with_line)
    sizes = [2, 2, 2, 1, 1] if experts_here == 8 else [1] * experts_here
    packs = [
        pack_experts(where, (w_gate[0], w_up[0], w_down[0]), pieces, sum(sizes[:c]), size)
        for c, size in enumerate(sizes)
    ]

    owns = (w_query[0], w_key[0], w_value[0], w_out[0], w_gate[0], w_up[0], w_down[0])
    offset = line * rows
    reach = min((WINDOW - 1) // rows + 1, ranks - 1)
    positions = offset + jnp.arange(rows, dtype=jnp.int32)
    key_places = offset - reach * rows + jnp.arange((reach + 1) * rows, dtype=jnp.int32)
    query_docs = doc_ids(lengths, positions)[:, None]
    key_docs = jnp.where(key_places >= 0, doc_ids(lengths, key_places), -1)[None, :]
    usable = (doc_ids(lengths, jnp.arange(ranks * rows, dtype=jnp.int32)) < NDOC).astype(jnp.int32)[None, :]
    half = HEAD_DIM // 2
    inverse = 10000.0 ** (-(jnp.arange(half, dtype=f32) * (2.0 / HEAD_DIM)))
    angles = positions.astype(f32)[:, None] * inverse[None, :]
    cosine = jnp.tile(jnp.cos(angles), (1, 4))
    sine = jnp.sin(angles)
    sine = jnp.concatenate([-sine, sine, -sine, sine], axis=1)
    tables = (cosine, sine, query_docs, key_docs, usable, reach)

    weights = []
    infos = []
    for layer in range(2):
        held = section == layer
        table = jnp.where(held, small, other_small)
        vectors = (table[EXPERTS : EXPERTS + 1], table[EXPERTS + 1 :], table[:EXPERTS].astype(bf16))
        weights.append(vectors + (owns, dense_parts))
        infos.append(jnp.stack([held.astype(jnp.int32), place, line]).astype(jnp.int32))

    marks = []

    def next_chunk(*mark):
        chunk, = crossing[:1]
        del crossing[0]
        if mark:
            chunk, seen = tie(chunk, *mark)
            marks.append(seen)
        expert_parts.append(spread_pieces(chunk))
        if packs:
            piece, _ = tie(packs.pop(0), chunk)
            crossing.append(swapped(piece, "section", 1))

    expert_parts = []
    piece, dense_gone = tie(packs.pop(0), dense_first_hop)
    crossing = [swapped(piece, "section", 1)]
    if packs:
        crossing.append(swapped(packs.pop(0), "section", 1))
    query, keyval = layer_project(x, weights[0], tables, infos[0], [dense_gone])
    next_chunk()
    earlier = earlier_keys(keyval, tables)
    next_chunk(earlier[-1])
    attended = layer_attend(x, query, keyval, earlier, weights[0], tables, infos[0])
    line_blocks = line_gather(attended[-1])
    for block in line_blocks[0]:
        if crossing:
            next_chunk(block)
    while crossing:
        next_chunk()
    layers = [weight + (expert_parts,) for weight in weights]
    middle, sums, kept_first = layer_experts(
        x, query, keyval, earlier, attended, line_blocks, layers[0], tables, infos[0], both[0], marks
    )
    between = layer_result(middle, sums)
    query, keyval = layer_project(between, weights[1], tables, infos[1])
    earlier = earlier_keys(keyval, tables)
    attended = layer_attend(between, query, keyval, earlier, weights[1], tables, infos[1])
    middle, sums, kept_second = layer_experts(
        between, query, keyval, earlier, attended, line_gather(attended[-1]), layers[1], tables, infos[1], both[1]
    )
    d_between, experts_second, dense_second = layer_backward(
        1, top_named, top_line, kept_second, layers[1], tables, infos[1]
    )
    between_line = line_gather(d_between)
    half = experts_second[0].shape[0] // 2
    def to_give(of_first, of_second):
        return jnp.where(first, of_second, of_first)

    dense_second = lax.psum_scatter(dense_second, "far", scatter_dimension=0, tiled=True)[0]
    waits = {"experts_back": experts_second[:1], "reduce": experts_second[1:], "expert_grads": [dense_second]}
    d_first, experts_first, dense_first = layer_backward(
        0, d_between, between_line, kept_first, layers[0], tables, infos[0], waits
    )
    experts_second[1:] = waits["reduce"]
    second = [part for of_second in experts_second for part in (of_second[:half], of_second[half:])]
    sums, d_first, dense_first = tie(sums, d_first, dense_first)
    got = [swapped(to_give(a, b), "section", 1) for a, b in zip(experts_first[:2], second)]
    for bit in fetch_bits()[:-1]:
        parts = dense_first.reshape((2, -1) + dense_first.shape[1:])
        high = (place // bit) % 2
        keep = lax.dynamic_index_in_dim(parts, high, 0, False)
        send = lax.dynamic_index_in_dim(parts, 1 - high, 0, False)
        dense_first = (keep.astype(f32) + dp_swapped(send, bit).astype(f32)).astype(bf16)
    got_grad = swapped(to_give(d_first, d_between), "section", 1)
    ties = {2: [dense_first, *got], 3: [got_grad]}
    final = layer_result(middle, sums, ties)
    got_grad, (dense_first, *got) = ties[3][0], ties[2]
    got_output = swapped(to_give(between, final), "section", 1)
    last = len(experts_first) - 1
    got += [None] * (last - 1)
    behind = 0
    for c in range(2, last + 1):
        experts_first[c], got[behind] = tie(experts_first[c], got[behind])
        got[c] = swapped(to_give(experts_first[c], second[c]), "section", 1)
        behind = c
    dense = jnp.concatenate([dense_first.reshape(dense_second.shape), dense_second], axis=1)
    ties = {3: got[2:3]}
    dense = line_reduce(dense.reshape(ranks, -1, dense.shape[1]), ties).astype(bf16)
    dense_first, dense_second = jnp.split(dense, 2, axis=1)
    got[2] = ties[3][0]

    def by_section(of_first, of_second, got):
        held = jnp.where(first, of_first, of_second)
        return jnp.stack([jnp.where(first, held, got), jnp.where(first, got, held)])

    def total(of_first, of_second, got):
        return jnp.where(first, of_first, of_second).astype(f32) + got.astype(f32)

    outputs = by_section(between, final, got_output)
    input_grads = by_section(d_first, d_between, got_grad)
    chunks = [total(*terms) for terms in zip(experts_first, second, got)]
    grad_gate = jnp.concatenate([c[:, :wide] for c in chunks], axis=0)
    grad_up = jnp.concatenate([c[:, wide : 2 * wide] for c in chunks], axis=0)
    grad_down = jnp.concatenate(
        [
            jnp.concatenate([c[:, 2 * wide : 2 * wide + narrow], c[:, 2 * wide + narrow :]], axis=2)
            for c in chunks
        ],
        axis=0,
    )
    dense = total(dense_first, dense_second, swapped(to_give(dense_first, dense_second), "section", 1))
    grad_out, grad_query, grad_keyval = dense[:, :width], dense[:, width : 2 * width], dense[:, 2 * width : 3 * width]
    vectors = dense[:, 3 * width :]
    kv_half = KV_HEADS * HEAD_DIM
    return (
        outputs[None, :, None],
        input_grads[None, :, None],
        vectors[:, EXPERTS + 1][None],
        grad_query[None],
        grad_keyval[:, :kv_half][None],
        grad_keyval[:, kv_half:][None],
        grad_out[None],
        vectors[:, EXPERTS][None],
        vectors[:, :EXPERTS][None],
        grad_gate[None],
        grad_up[None],
        grad_down[None],
    )


def solution(mesh):
    placed = (
        P(None, ("far", "near"), "expert", None),
        P(None, ("far", "near"), "expert", None),
        P("section", None),
        P("section", None, None),
        P("section", None, None),
        P("section", None, None),
        P("section", None, None),
        P("section", None),
        P("section", None, None),
        P("section", "expert", None, None),
        P("section", "expert", None, None),
        P("section", "expert", None, None),
        P(None, ("far", "near"), None),
        P("section", None, ("far", "near"), "expert", None),
    )
    sections, dp, ranks = mesh.devices.shape
    devices = mesh.devices.reshape(sections, dp // 2, 2, ranks)
    split = jax.sharding.Mesh(devices, ("section", "far", "near", "expert"))
    return jax.shard_map(
        per_device,
        mesh=split,
        in_specs=placed,
        out_specs=(
            P("section", None, ("far", "near"), "expert", None),
            P("section", None, ("far", "near"), "expert", None),
            P("section", ("far", "near", "expert")),
            P("section", ("far", "near", "expert"), None),
            P("section", ("far", "near", "expert"), None),
            P("section", ("far", "near", "expert"), None),
            P("section", ("far", "near", "expert"), None),
            P("section", ("far", "near", "expert")),
            P("section", ("far", "near", "expert"), None),
            P("section", "expert", ("far", "near"), None),
            P("section", "expert", ("far", "near"), None),
            P("section", "expert", ("far", "near"), None),
        ),
        check_vma=False,
    )
```

```python
import functools

import jax
import jax.numpy as jnp
from jax import lax
from jax.experimental import pallas as pl
from jax.experimental.pallas import tpu as pltpu
from jax.sharding import PartitionSpec as P

HEADS = 16
KV_HEADS = 8
HEAD_DIM = 64
EXPERTS = 32
TOPK = 8
WINDOW = 512
NDOC = 4
EPSILON = 1e-06
MASKED = -1e30
LANES = 128
VMEM_BYTES = 56 * 1024 * 1024
bf16 = jnp.bfloat16
f32 = jnp.float32


def shifted(value, axis, steps, sources=None):
    count = lax.axis_size(axis)
    initial, last = (max(0, -steps), min(count, count - steps))
    names = range(initial, last) if sources is None else sources
    return lax.ppermute(value, axis, [(source, source + steps) for source in names])


def swapped(value, axis, bit):
    count = lax.axis_size(axis)
    return lax.ppermute(value, axis, [(source, source ^ bit) for source in range(count)])


def tie(*values):
    return lax.optimization_barrier(values)


def line_gather(block):
    ups, downs = [], []
    up, down = block, block
    for _ in range(lax.axis_size("expert") - 1):
        up = shifted(up, "expert", 1)
        down = shifted(down, "expert", -1)
        ups.append(up)
        downs.append(down)
    return ups, downs


def line_reduce(parts, ties={}, marks=None):
    ranks = lax.axis_size("expert")
    me = lax.axis_index("expert")

    def pick(index):
        return lax.dynamic_index_in_dim(parts, jnp.clip(index, 0, ranks - 1), 0, False)

    up = down = None
    for step in range(1, ranks):
        up_part = pick(me + ranks - step)
        down_part = pick(me - ranks + step)
        up = up_part if up is None else (up.astype(f32) + up_part.astype(f32)).astype(bf16)
        down = down_part if down is None else (down.astype(f32) + down_part.astype(f32)).astype(bf16)
        if step in ties:
            up, down, *ties[step] = tie(up, down, *ties[step])
        up = shifted(up, "expert", 1, range(0, step))
        down = shifted(down, "expert", -1, range(ranks - step, ranks))
        if marks is not None:
            marks.append([up, down])
    return pick(me).astype(f32) + up.astype(f32) + down.astype(f32)


def dp_size():
    return lax.axis_size("far") * lax.axis_size("near")


def dp_swapped(value, bit):
    return swapped(value, "near", 1) if bit == 1 else swapped(value, "far", bit // 2)


def fetch_bits():
    bits, bit = [], dp_size() // 2
    while bit >= 1:
        bits.append(bit)
        bit //= 2
    return bits


def spread_pieces(piece, before=None):
    pieces = {0: piece}
    for bit in fetch_bits():
        for k in list(pieces):
            if before is not None and k == max(pieces):
                pieces[k] = before(pieces[k], bit)
            pieces[k | bit] = dp_swapped(pieces[k], bit)
    return [pieces[k] for k in range(len(pieces))]


def near_sum(keep, send):
    return (keep.astype(f32) + swapped(send, "near", 1).astype(f32)).astype(bf16)


def call(
    kernel, out_shape, in_specs, out_specs, scratch, grid=None, flops=0, bytes_accessed=0, name=None, waits=()
):
    extra = {} if grid is None else {"grid": grid}
    begin, end = len(in_specs), len(in_specs) + len(waits)
    run = pl.pallas_call(
        lambda *refs: kernel(*refs[:begin], *refs[end:]),
        out_shape=out_shape,
        in_specs=[*in_specs, *[ANY] * len(waits)],
        out_specs=out_specs,
        scratch_shapes=scratch,
        compiler_params=pltpu.CompilerParams(vmem_limit_bytes=VMEM_BYTES),
        cost_estimate=pl.CostEstimate(flops=flops, bytes_accessed=bytes_accessed, transcendentals=0),
        name=name,
        **extra,
    )
    return lambda *args: run(*args, *waits)


SMEM = pl.BlockSpec(memory_space=pltpu.SMEM)
VMEM = pl.BlockSpec(memory_space=pltpu.VMEM)
ANY = pl.BlockSpec(memory_space=pl.ANY)


def struct(shape, dtype):
    return jax.ShapeDtypeStruct(shape, dtype)


def dot(left, right, left_dim=1, right_dim=0):
    return lax.dot_general(left, right, (((left_dim,), (right_dim,)), ((), ())), preferred_element_type=f32)


def upper_lanes(shape):
    return lax.broadcasted_iota(jnp.int32, shape, 1) % LANES >= HEAD_DIM


def half_swap(tile):
    lane = lax.broadcasted_iota(jnp.int32, tile.shape, 1)
    half = HEAD_DIM // 2
    return jnp.where(
        lane % HEAD_DIM < half, pltpu.roll(tile, LANES - half, 1), pltpu.roll(tile, half, 1)
    )


def load_dense(info, owns, pieces, first, width, target, sem):
    rows = target.shape[0] // len(pieces)

    @pl.when(info[0] == 1)
    def _():
        start = 0
        for own in owns:
            size = own.shape[1]
            pltpu.make_async_copy(own, target.at[:, pl.ds(start, size)], sem).start()
            start += size

    @pl.when(info[0] == 0)
    def _():
        for k, piece in enumerate(pieces):
            place = pl.multiple_of((info[1] ^ k) * rows, rows)
            pltpu.make_async_copy(
                piece.at[:, pl.ds(first, width)], target.at[pl.ds(place, rows), :], sem
            ).start()


def wait_dense(target, sem):
    pltpu.make_async_copy(target, target, sem).wait()


def load_experts(info, owns, chunks, expert, slot, buffers, sems):
    gate_buf, up_buf, down_buf = buffers
    pieces = len(chunks[0])
    wide = gate_buf.shape[1] // pieces
    narrow = down_buf.shape[1] // pieces
    half = down_buf.shape[2] // 2

    @pl.when(info[0] == 1)
    def _():
        for own, buf, index in zip(owns, buffers, range(3)):
            pltpu.make_async_copy(own.at[expert], buf.at[slot], sems.at[slot, index]).start()

    begin = 0
    for chunk in chunks:
        first, begin = begin, begin + chunk[0].shape[0]

        @pl.when((info[0] == 0) & (expert >= first) & (expert < begin))
        def _():
            local = expert - first
            for k, piece in enumerate(chunk):
                owner = info[1] ^ k
                row = pl.multiple_of(owner * wide, wide)
                low = pl.multiple_of(owner * narrow, narrow)
                pltpu.make_async_copy(
                    piece.at[local, pl.ds(0, wide)], gate_buf.at[slot, pl.ds(row, wide)], sems.at[slot, 0]
                ).start()
                pltpu.make_async_copy(
                    piece.at[local, pl.ds(wide, wide)], up_buf.at[slot, pl.ds(row, wide)], sems.at[slot, 1]
                ).start()
                for side in range(2):
                    pltpu.make_async_copy(
                        piece.at[local, pl.ds(2 * wide + side * narrow, narrow)],
                        down_buf.at[slot, pl.ds(low, narrow), pl.ds(side * half, half)],
                        sems.at[slot, 2],
                    ).start()


def wait_experts(slot, index, buffers, sems):
    pltpu.make_async_copy(buffers[index].at[slot], buffers[index].at[slot], sems.at[slot, index]).wait()


def load_line(info, own, ups, downs, target, sem):
    ranks = target.shape[0]
    me = info[2]
    columns = pl.ds(0, target.shape[2])
    pltpu.make_async_copy(own.at[:, columns], target.at[me], sem).start()
    for s in range(1, ranks):

        @pl.when(me >= s)
        def _():
            pltpu.make_async_copy(ups[s - 1].at[:, columns], target.at[me - s], sem).start()

        @pl.when(me < s)
        def _():
            pltpu.make_async_copy(downs[ranks - s - 1].at[:, columns], target.at[me - s + ranks], sem).start()


def wait_line(target, sem):
    pltpu.make_async_copy(target, target, sem).wait()


def write_pieces(info, value, keep, send, place):
    pieces = 2 * keep.shape[0]
    rows = value.shape[0] // pieces
    for p in range(pieces):
        part = value[p * rows : (p + 1) * rows].astype(keep.dtype)
        same = info[1] % 2 == p % 2

        @pl.when(same)
        def _():
            keep[(p // 2,) + place] = part

        @pl.when(jnp.logical_not(same))
        def _():
            send[(p // 2,) + place] = part


def rms(values):
    return lax.rsqrt(jnp.mean(values * values, axis=-1, keepdims=True) + EPSILON)


def mask_bias(info, query_docs, key_docs, bias):
    rows, keys = bias.shape
    row = lax.broadcasted_iota(jnp.int32, (rows, keys), 0)
    col = lax.broadcasted_iota(jnp.int32, (rows, keys), 1)
    distance = row + (keys - rows) - col
    allowed = (distance >= 0) & (distance < WINDOW) & (query_docs[...] == key_docs[...])
    bias[...] = jnp.where(allowed, 0.0, MASKED)


def load_keys(own, earlier, target, sem):
    rows = own.shape[0]
    reach = len(earlier)
    pltpu.make_async_copy(own, target.at[pl.ds(reach * rows, rows)], sem).start()
    for s, part in enumerate(earlier):
        pltpu.make_async_copy(part, target.at[pl.ds((reach - 1 - s) * rows, rows)], sem).start()


def doubled(pair, which):
    wide = pair.astype(f32)
    turned = pltpu.roll(wide, HEAD_DIM, 1)
    upper = upper_lanes(wide.shape)
    picked = jnp.where(upper, turned, wide) if which == 0 else jnp.where(upper, wide, turned)
    return picked.astype(bf16)


def one_head(tile, which, upper):
    return jnp.where(upper, tile, 0.0) if which == 1 else jnp.where(upper, 0.0, tile)


def pack_dense_kernel(info, *refs):
    begin = 0
    for matrix in refs[:-1]:
        width = matrix.shape[1]
        refs[-1][:, begin : begin + width] = matrix[...]
        begin += width


def pack_experts_kernel(info, gate, up, down, out):
    wide, narrow = gate.shape[1], down.shape[1]
    half = out.shape[2]
    out[0, :wide] = gate[0]
    out[0, wide : 2 * wide] = up[0]
    out[0, 2 * wide : 2 * wide + narrow] = down[0, :, :half]
    out[0, 2 * wide + narrow :] = down[0, :, half:]


def packed(kernel, out_shape, grid, in_specs, out_specs, name):
    size = 4 * functools.reduce(lambda a, b: a * b, out_shape.shape)
    return pl.pallas_call(
        kernel,
        out_shape=out_shape,
        grid_spec=pltpu.PrefetchScalarGridSpec(
            num_scalar_prefetch=1, grid=grid, in_specs=in_specs, out_specs=out_specs
        ),
        cost_estimate=pl.CostEstimate(flops=0, bytes_accessed=size, transcendentals=0),
        name=name,
    )


def pack_dense(info, matrices, pieces):
    rows = matrices[0].shape[0] // pieces
    total = sum(matrix.shape[1] for matrix in matrices)
    return packed(
        pack_dense_kernel,
        struct((rows, total), bf16),
        (1,),
        [pl.BlockSpec((rows, matrix.shape[1]), lambda i, info: (info[1], 0)) for matrix in matrices],
        pl.BlockSpec((rows, total), lambda i, info: (0, 0)),
        "pack_dense",
    )(info, *matrices)


def pack_experts(info, matrices, pieces, first, count):
    gate, up, down = matrices
    wide, narrow = gate.shape[1] // pieces, down.shape[1] // pieces
    hidden, width = gate.shape[2], down.shape[2]

    def own(e, info):
        return (first + e, info[1], 0)

    return packed(
        pack_experts_kernel,
        struct((count, 2 * wide + 2 * narrow, hidden), bf16),
        (count,),
        [
            pl.BlockSpec((1, wide, hidden), own),
            pl.BlockSpec((1, wide, hidden), own),
            pl.BlockSpec((1, narrow, width), own),
        ],
        pl.BlockSpec((1, 2 * wide + 2 * narrow, hidden), lambda e, info: (e, 0, 0)),
        "pack_experts",
    )(info, gate, up, down)


def project_kernel(pieces, info, x, gain, cosine, sine, w_query, w_key, w_value, *rest):
    parts = rest[:pieces]
    query, keyval, weights, sem = rest[pieces:]
    width = weights.shape[1]
    load_dense(info, (w_query, w_key, w_value), parts, 0, width, weights, sem)
    hidden = x[...].astype(f32)
    normed = (hidden * rms(hidden) * gain[...]).astype(bf16)
    wait_dense(weights, sem)
    q_width, k_width = w_query.shape[1], w_key.shape[1]
    cos, sin = cosine[...], sine[...]
    step = 2 * LANES
    for begin in range(0, width, step):
        product = dot(normed, weights[:, begin : begin + step])
        for inner in range(0, step, LANES):
            tile = product[:, inner : inner + LANES]
            place = begin + inner
            if place < q_width + k_width:
                tile = tile * cos + half_swap(tile) * sin
            if place < q_width:
                query[:, place : place + LANES] = tile.astype(bf16)
            else:
                place -= q_width
                keyval[:, place : place + LANES] = tile.astype(bf16)


def attend_kernel(pieces, reach, info, query, own_kv, *rest):
    earlier = rest[:reach]
    query_docs, key_docs, x, gain, w_out = rest[reach : reach + 5]
    parts = rest[reach + 5 : reach + 5 + pieces]
    mixed, log_total, middle, routed = rest[reach + 5 + pieces : reach + 9 + pieces]
    keyval, bias, weights, kv_sem, w_sem = rest[reach + 9 + pieces :]
    load_keys(own_kv, earlier, keyval, kv_sem)
    first = 2 * x.shape[1]
    load_dense(info, (w_out,), parts, first, x.shape[1], weights, w_sem)
    mask_bias(info, query_docs, key_docs, bias)
    log_total[...] = jnp.zeros_like(log_total)
    pltpu.make_async_copy(keyval, keyval, kv_sem).wait()
    kv_width = KV_HEADS * HEAD_DIM
    rows = query.shape[0]
    upper = upper_lanes((rows, LANES))
    lane = lax.broadcasted_iota(jnp.int32, (rows, LANES), 1)

    @pl.loop(0, KV_HEADS // 2)
    def _(pair):
        k_pair = keyval[:, pl.ds(pl.multiple_of(pair * LANES, LANES), LANES)]
        v_pair = keyval[:, pl.ds(pl.multiple_of(kv_width + pair * LANES, LANES), LANES)]
        for head in range(2):
            keys, values = doubled(k_pair, head), doubled(v_pair, head)
            place = pl.multiple_of((pair * 2 + head) * LANES, LANES)
            tile = query[:, pl.ds(place, LANES)].astype(f32) * HEAD_DIM ** (-0.5)
            results = []
            for g in range(2):
                scores = dot(one_head(tile, g, upper).astype(bf16), keys, 1, 1) + bias[...]
                peak = jnp.max(scores, axis=1, keepdims=True)
                expo = jnp.exp(scores - peak)
                total = jnp.sum(expo, axis=1, keepdims=True)
                results.append(dot(expo.astype(bf16), values) * (1.0 / total))
                index = (pair * 2 + head) * 2 + g
                log_total[...] = jnp.where(lane == index, peak + jnp.log(total), log_total[...])
            mixed[:, pl.ds(place, LANES)] = jnp.where(upper, results[1], results[0]).astype(bf16)

    wait_dense(weights, w_sem)
    between = x[...].astype(f32) + dot(mixed[...], weights[...])
    middle[...] = between
    routed[...] = (between * rms(between) * gain[...]).astype(bf16)


def attend_back_kernel(pieces, reach, info, d_routed, grad, middle, gain, mixed, query, log_total, own_kv, *rest):
    earlier = rest[:reach]
    query_docs, key_docs, cosine, sine, w_out = rest[reach : reach + 5]
    rest = rest[reach + 5 :]
    parts = rest[:pieces]
    rest = rest[pieces:]
    d_middle, d_query, d_own = rest[:3]
    d_earlier = rest[3 : 3 + reach]
    keep, send, grad_gain = rest[3 + reach : 6 + reach]
    keyval, bias, weights, d_mixed, d_kv, kv_sem, w_sem = rest[6 + reach :]
    load_keys(own_kv, earlier, keyval, kv_sem)
    first = 2 * middle.shape[1]
    load_dense(info, (w_out,), parts, first, middle.shape[1], weights, w_sem)
    mask_bias(info, query_docs, key_docs, bias)
    between = middle[...]
    scale = rms(between)
    normal = between * scale
    routed = d_routed[...]
    grad_gain[...] = jnp.sum(routed * normal, axis=0, keepdims=True)
    d_norm = routed * gain[...]
    total = grad[...].astype(f32) + scale * (
        d_norm - normal * jnp.mean(d_norm * normal, axis=1, keepdims=True)
    )
    d_middle[...] = total
    branch = total.astype(bf16)
    wait_dense(weights, w_sem)
    d_mixed[...] = dot(branch, weights[...], 1, 1).astype(bf16)
    write_pieces(info, dot(mixed[...], branch, 0, 0), keep, send, ())
    pltpu.make_async_copy(keyval, keyval, kv_sem).wait()
    kv_width = KV_HEADS * HEAD_DIM
    rows = query.shape[0]
    upper = upper_lanes((rows, LANES))
    lane = lax.broadcasted_iota(jnp.int32, (rows, LANES), 1)
    cos, sin = cosine[...], sine[...]

    @pl.loop(0, KV_HEADS // 2)
    def _(pair):
        k_pair = keyval[:, pl.ds(pl.multiple_of(pair * LANES, LANES), LANES)]
        v_pair = keyval[:, pl.ds(pl.multiple_of(kv_width + pair * LANES, LANES), LANES)]
        for head in range(2):
            keys, values = doubled(k_pair, head), doubled(v_pair, head)
            place = pl.multiple_of((pair * 2 + head) * LANES, LANES)
            tile = query[:, pl.ds(place, LANES)].astype(f32) * HEAD_DIM ** (-0.5)
            d_tile = d_mixed[:, pl.ds(place, LANES)].astype(f32)
            inner = d_tile * mixed[:, pl.ds(place, LANES)].astype(f32)
            dq, dk, dv = [], None, None
            for g in range(2):
                index = (pair * 2 + head) * 2 + g
                log_column = jnp.sum(jnp.where(lane == index, log_total[...], 0.0), axis=1, keepdims=True)
                weight = jnp.sum(one_head(inner, g, upper), axis=1, keepdims=True)
                own_query = one_head(tile, g, upper).astype(bf16)
                own_grad = one_head(d_tile, g, upper).astype(bf16)
                scores = dot(own_query, keys, 1, 1) + bias[...]
                probs = jnp.exp(scores - log_column)
                d_probs = dot(own_grad, values, 1, 1)
                d_scores = (probs * (d_probs - weight)).astype(bf16)
                dq.append(dot(d_scores, keys))
                k_term = dot(own_query, d_scores, 0, 0)
                v_term = dot(own_grad, probs.astype(bf16), 0, 0)
                dk = k_term if dk is None else dk + k_term
                dv = v_term if dv is None else dv + v_term
            whole = jnp.where(upper, dq[1], dq[0]) * HEAD_DIM ** (-0.5)
            whole = whole * cos - half_swap(whole) * sin
            d_query[:, pl.ds(place, LANES)] = whole.astype(bf16)
            k_row = pl.multiple_of((pair * 2 + head) * HEAD_DIM, HEAD_DIM)
            v_row = pl.multiple_of(kv_width + (pair * 2 + head) * HEAD_DIM, HEAD_DIM)
            d_kv[pl.ds(k_row, HEAD_DIM), :] = dk[:HEAD_DIM] + dk[HEAD_DIM:]
            d_kv[pl.ds(v_row, HEAD_DIM), :] = dv[:HEAD_DIM] + dv[HEAD_DIM:]

    for block in range(reach + 1):
        turned = d_kv[:, block * rows : (block + 1) * rows].T
        if block == reach:
            d_own[...] = turned
        else:
            d_earlier[reach - 1 - block][...] = turned.astype(bf16)


def query_back_kernel(pieces, info, x, gain, d_query, w_query, *rest):
    parts = rest[:pieces]
    d_normed, keep, send, weights, sem = rest[pieces:]
    load_dense(info, (w_query,), parts, 0, weights.shape[1], weights, sem)
    hidden = x[...].astype(f32)
    normed = (hidden * rms(hidden) * gain[...]).astype(bf16)
    write_pieces(info, dot(normed, d_query[...], 0, 0), keep, send, ())
    wait_dense(weights, sem)
    d_normed[...] = dot(d_query[...], weights[...], 1, 1)


def keyval_back_kernel(
    pieces, info, x, gain, d_own, d_others, d_normed, d_middle, cosine, sine, grad_router, grad_gain_moe,
    w_key, w_value, *rest,
):
    parts = rest[:pieces]
    d_x, keep, send, weights, d_pre, sem = rest[pieces:]
    load_dense(info, (w_key, w_value), parts, x.shape[1], weights.shape[1], weights, sem)
    hidden = x[...].astype(f32)
    scale = rms(hidden)
    normal = hidden * scale
    normed = (normal * gain[...]).astype(bf16)
    cos, sin = cosine[...], sine[...]
    width = w_key.shape[1]
    for place in range(0, 2 * width, LANES):
        tile = d_own[:, place : place + LANES] + d_others[:, place : place + LANES].astype(f32)
        if place < width:
            tile = tile * cos - half_swap(tile) * sin
        d_pre[:, place : place + LANES] = tile.astype(bf16)
    wait_dense(weights, sem)
    total = d_normed[...] + dot(d_pre[...], weights[...], 1, 1)
    grad_gain = jnp.sum(total * normal, axis=0, keepdims=True)
    tall = jnp.concatenate(
        [grad_router[...], jnp.zeros((LANES - EXPERTS, total.shape[1]), f32)], axis=0
    )
    row = lax.broadcasted_iota(jnp.int32, tall.shape, 0)
    tall = jnp.where(row == EXPERTS, grad_gain_moe[...], jnp.where(row == EXPERTS + 1, grad_gain, tall))
    d_norm = total * gain[...]
    d_x[...] = (
        d_middle[...]
        + scale * (d_norm - normal * jnp.mean(d_norm * normal, axis=1, keepdims=True))
    ).astype(bf16)
    both = 2 * width
    write_pieces(info, dot(normed, d_pre[...], 0, 0), keep, send, (slice(None), slice(0, both)))
    write_pieces(info, tall.T, keep, send, (slice(None), slice(both, both + LANES)))


def slot_rows(info, table, local, experts_here):
    row = lax.broadcasted_iota(jnp.int32, table.shape, 0)
    picked = jnp.where(row == info[2] * experts_here + local, table, 0.0)
    return jnp.sum(picked, axis=0, keepdims=True)


def slot_hits(codes, capacity):
    slot = lax.broadcasted_iota(jnp.int32, (capacity, codes.shape[1]), 0).astype(f32)
    return slot == codes


def experts_kernel(pieces, ranks, chunk_count, info, own, *rest):
    ups, downs = rest[: ranks - 1], rest[ranks - 1 : 2 * ranks - 2]
    rest = rest[2 * ranks - 2 :]
    routes, usable, router, w_gate, w_up, w_down = rest[:6]
    rest = rest[6:]
    chunks = [rest[c * pieces : (c + 1) * pieces] for c in range(chunk_count)]
    rest = rest[chunk_count * pieces :]
    sums, everyone_out, rows_out, gates, codes, gate_out, up_out = rest[:7]
    hits, results, gate_buf, up_buf, down_buf, everyone, rows, sems, line_sem, out_sems = rest[7:]
    kept = [
        pltpu.make_async_copy(everyone, everyone_out, out_sems.at[0]),
        pltpu.make_async_copy(rows, rows_out, out_sems.at[1]),
    ]
    expert, count = pl.program_id(0), pl.num_programs(0)
    buffers = (gate_buf, up_buf, down_buf)
    owns = (w_gate, w_up, w_down)
    experts_here = w_gate.shape[0]
    tokens = own.shape[0]
    capacity = tokens * TOPK // EXPERTS
    slot = expert % 2

    @pl.when(expert == 0)
    def _():
        load_line(info, own, ups, downs, everyone, line_sem)
        load_experts(info, owns, chunks, 0, 0, buffers, sems)
        earlier = lax.broadcasted_iota(jnp.int32, (tokens, tokens), 0)
        later = lax.broadcasted_iota(jnp.int32, (tokens, tokens), 1)
        triangle = jnp.where(earlier < later, 1.0, 0.0).astype(bf16)
        number = lax.broadcasted_iota(jnp.int32, (EXPERTS, tokens), 0)
        wait_line(everyone, line_sem)
        for block in range(ranks):
            span = slice(block * tokens, (block + 1) * tokens)
            named = routes[0:1, span] == number
            for k in range(1, TOPK):
                named = named | (routes[k : k + 1, span] == number)
            logits = jnp.where(named, dot(router[...], everyone[block], 1, 1), MASKED)
            expo = jnp.where(named, jnp.exp(logits - jnp.max(logits, axis=0, keepdims=True)), 0.0)
            weight = expo / jnp.sum(expo, axis=0, keepdims=True)
            held = named & (usable[:, span] > 0)
            rank = dot(jnp.where(held, 1.0, 0.0).astype(bf16), triangle)
            code = jnp.where(held & (rank < capacity), rank, -1.0)
            gates[block] = weight
            codes[block] = code
            for e in range(experts_here):
                hit = slot_hits(slot_rows(info, code, e, experts_here), capacity)
                hits[block, e * capacity : (e + 1) * capacity, :] = jnp.where(hit, 1.0, 0.0).astype(bf16)
            rows[block] = dot(hits[block], everyone[block]).astype(bf16)
        for copy in kept:
            copy.start()

    @pl.when(expert + 1 < count)
    def _():
        load_experts(info, owns, chunks, expert + 1, 1 - slot, buffers, sems)

    place = pl.multiple_of(expert * capacity, capacity)
    mine = jnp.concatenate([rows[block, pl.ds(place, capacity), :] for block in range(ranks)], axis=0)
    for index in range(3):
        wait_experts(slot, index, buffers, sems)
    gate_pre = dot(mine, gate_buf[slot])
    up_pre = dot(mine, up_buf[slot])
    gate_out[0] = gate_pre.astype(bf16)
    up_out[0] = up_pre.astype(bf16)
    activated = (gate_pre * jax.nn.sigmoid(gate_pre) * up_pre).astype(bf16)
    produced = dot(activated, down_buf[slot]).astype(bf16)
    for block in range(ranks):
        results[block, pl.ds(place, capacity), :] = produced[block * capacity : (block + 1) * capacity]

    @pl.when(expert + 1 == count)
    def _():
        for block in range(ranks):
            weighted = []
            for e in range(experts_here):
                weight = slot_rows(info, gates[block], e, experts_here)
                hit = hits[block, e * capacity : (e + 1) * capacity, :].astype(f32)
                weighted.append((hit * weight).astype(bf16))
            sums[block] = dot(jnp.concatenate(weighted, axis=0), results[block], 0, 0).astype(bf16)
        for copy in kept:
            copy.wait()


def experts_back_kernel(pieces, ranks, chunk_count, info, own, *rest):
    ups, downs = rest[: ranks - 1], rest[ranks - 1 : 2 * ranks - 2]
    rest = rest[2 * ranks - 2 :]
    everyone, gates, codes, router, gate_pre, up_pre, w_gate, w_up, w_down = rest[:9]
    rest = rest[9:]
    chunks = [rest[c * pieces : (c + 1) * pieces] for c in range(chunk_count)]
    rest = rest[chunk_count * pieces :]
    sums, grad_router, rows_out, gate_out, up_out, active_out = rest[:6]
    incoming, hits, columns, d_gates, d_rows, gate_buf, up_buf, down_buf = rest[6:14]
    grad_rows, sems, line_sem, out_sem = rest[14:]
    kept = pltpu.make_async_copy(grad_rows, rows_out, out_sem)
    expert, count = pl.program_id(0), pl.num_programs(0)
    buffers = (gate_buf, up_buf, down_buf)
    owns = (w_gate, w_up, w_down)
    experts_here = w_gate.shape[0]
    tokens = own.shape[0]
    capacity = tokens * TOPK // EXPERTS
    slot = expert % 2

    @pl.when(expert == 0)
    def _():
        load_line(info, own, ups, downs, incoming, line_sem)
        load_experts(info, owns, chunks, 0, 0, buffers, sems)
        for block in range(ranks):
            for e in range(experts_here):
                hit = slot_hits(slot_rows(info, codes[block], e, experts_here), capacity)
                span = slice(e * capacity, (e + 1) * capacity)
                hits[block, span, :] = jnp.where(hit, 1.0, 0.0).astype(bf16)
                weight = slot_rows(info, gates[block], e, experts_here)
                column = jnp.sum(jnp.where(hit, weight, 0.0), axis=1, keepdims=True)
                columns[block, span, :] = jnp.broadcast_to(column, (capacity, LANES))
        wait_line(incoming, line_sem)
        for block in range(ranks):
            grad_rows[block] = dot(hits[block], incoming[block]).astype(bf16)
        kept.start()

    @pl.when(expert + 1 < count)
    def _():
        load_experts(info, owns, chunks, expert + 1, 1 - slot, buffers, sems)

    place = pl.multiple_of(expert * capacity, capacity)
    mine = jnp.concatenate([grad_rows[block, pl.ds(place, capacity), :] for block in range(ranks)], axis=0)
    weight = jnp.concatenate(
        [columns[block, pl.ds(place, capacity), :] for block in range(ranks)], axis=0
    )[:, :1]
    gate = gate_pre[0].astype(f32)
    up = up_pre[0].astype(f32)
    sigma = jax.nn.sigmoid(gate)
    silu = gate * sigma
    activated = silu * up
    for index in range(3):
        wait_experts(slot, index, buffers, sems)
    unweighted = dot(mine, down_buf[slot], 1, 1)
    d_weight = jnp.sum(unweighted * activated, axis=1, keepdims=True)
    for block in range(ranks):
        hit = hits[block, pl.ds(place, capacity), :].astype(f32)
        spread = hit * d_weight[block * capacity : (block + 1) * capacity]
        d_gates[block, pl.ds(expert, 1), :] = jnp.sum(spread, axis=0, keepdims=True)
    d_active = unweighted * weight
    active_out[0] = (activated * weight).astype(bf16)
    d_gate = (d_active * up * sigma * (1.0 + gate * (1.0 - sigma))).astype(bf16)
    d_up = (d_active * silu).astype(bf16)
    gate_out[0] = d_gate
    up_out[0] = d_up
    produced = (dot(d_gate, gate_buf[slot], 1, 1) + dot(d_up, up_buf[slot], 1, 1)).astype(bf16)
    for block in range(ranks):
        d_rows[block, pl.ds(place, capacity), :] = produced[block * capacity : (block + 1) * capacity]

    @pl.when(expert + 1 == count)
    def _():
        number = lax.broadcasted_iota(jnp.int32, (EXPERTS, tokens), 0)
        router_total = jnp.zeros(grad_router.shape, f32)
        for block in range(ranks):
            weight = gates[block]
            own_grads = jnp.zeros((EXPERTS, tokens), f32)
            for e in range(experts_here):
                here = number == info[2] * experts_here + e
                own_grads = jnp.where(here, d_gates[block, e : e + 1, :], own_grads)
            inner = jnp.sum(weight * own_grads, axis=0, keepdims=True)
            d_logits = (weight * (own_grads - inner)).astype(bf16)
            router_total = router_total + dot(d_logits, everyone[block])
            back = dot(hits[block], d_rows[block], 0, 0) + dot(d_logits, router[...], 0, 0)
            sums[block] = back.astype(bf16)
        grad_router[...] = router_total
        kept.wait()


def expert_grads_kernel(info, *refs):
    *arrays, out = refs
    ranks, capacity, width = arrays[0].shape
    pairs = out.shape[0]
    hidden = arrays[4].shape[2]
    wide, narrow, half = width // (2 * pairs), hidden // (2 * pairs), width // 2
    sides = [arrays[:5], arrays[5:]]
    incoming = [grad_rows[...].reshape(ranks * capacity, width) for rows, grad_rows, *_ in sides]
    for pair in range(pairs):
        owner = 2 * pair + info[1] % 2
        column = pl.multiple_of(owner * wide, wide)
        gate = up = None
        for rows, grad_rows, d_gate, d_up, activated in sides:
            mine = rows[:, :, pl.ds(column, wide)].reshape(ranks * capacity, wide)
            gate_term, up_term = dot(mine, d_gate[0], 0, 0), dot(mine, d_up[0], 0, 0)
            gate = gate_term if gate is None else gate + gate_term
            up = up_term if up is None else up + up_term
        out[pair, 0, :wide] = gate.astype(bf16)
        out[pair, 0, wide : 2 * wide] = up.astype(bf16)
        if narrow % LANES == 0:
            column = pl.multiple_of(owner * narrow, narrow)
            down = sum(
                dot(side[4][0, :, pl.ds(column, narrow)], rows, 0, 0) for side, rows in zip(sides, incoming)
            ).astype(bf16)
            out[pair, 0, 2 * wide : 2 * wide + narrow] = down[:, :half]
            out[pair, 0, 2 * wide + narrow :] = down[:, half:]
    if narrow % LANES:
        down = sum(dot(side[4][0], rows, 0, 0) for side, rows in zip(sides, incoming)).astype(bf16)
        for p in range(2 * pairs):

            @pl.when(info[1] % 2 == p % 2)
            def _():
                part = down[p * narrow : (p + 1) * narrow]
                out[p // 2, 0, 2 * wide : 2 * wide + narrow] = part[:, :half]
                out[p // 2, 0, 2 * wide + narrow :] = part[:, half:]


def layer_project(x, weights, tables, info, waits=()):
    (gain_attn, gain_moe, router, owns, dense_parts) = weights
    w_query, w_key, w_value, w_out = owns[:4]
    cosine, sine = tables[:2]
    rows, width = x.shape
    pieces = dp_size()
    kv_width = 2 * KV_HEADS * HEAD_DIM
    return call(
        functools.partial(project_kernel, pieces),
        (struct((rows, width), bf16), struct((rows, kv_width), bf16)),
        [SMEM] + [VMEM] * 4 + [ANY] * (3 + pieces),
        (VMEM, VMEM),
        [pltpu.VMEM((width, width + kv_width), bf16), pltpu.SemaphoreType.DMA],
        flops=2 * rows * width * (width + kv_width),
        bytes_accessed=2 * width * (width + kv_width),
        name="project",
        waits=waits,
    )(info, x, gain_attn, cosine, sine, w_query, w_key, w_value, *dense_parts)


def earlier_keys(keyval, tables):
    earlier, moving = [], keyval
    for _ in range(tables[-1]):
        moving = shifted(moving, "expert", 1)
        earlier.append(moving)
    return earlier


def layer_attend(x, query, keyval, earlier, weights, tables, info, waits=()):
    (gain_attn, gain_moe, router, owns, dense_parts) = weights
    w_out = owns[3]
    cosine, sine, query_docs, key_docs, usable, reach = tables
    rows, width = x.shape
    pieces = dp_size()
    kv_width = 2 * KV_HEADS * HEAD_DIM
    keys = (reach + 1) * rows
    return call(
        functools.partial(attend_kernel, pieces, reach),
        (
            struct((rows, width), bf16),
            struct((rows, LANES), f32),
            struct((rows, width), f32),
            struct((rows, width), bf16),
        ),
        [SMEM, VMEM] + [ANY] * (1 + reach) + [VMEM] * 4 + [ANY] * (1 + pieces),
        (VMEM,) * 4,
        [
            pltpu.VMEM((keys, kv_width), bf16),
            pltpu.VMEM((rows, keys), f32),
            pltpu.VMEM((width, width), bf16),
            pltpu.SemaphoreType.DMA,
            pltpu.SemaphoreType.DMA,
        ],
        flops=16 * rows * keys * width,
        bytes_accessed=2 * width * width,
        name="attend",
        waits=waits,
    )(info, query, keyval, *earlier, query_docs, key_docs, x, gain_moe, w_out, *dense_parts)


def layer_experts(x, query, keyval, earlier, attended, line_blocks, weights, tables, info, routes, waits=()):
    (gain_attn, gain_moe, router, owns, dense_parts, expert_parts) = weights
    w_gate, w_up, w_down = owns[4:]
    usable = tables[4]
    mixed, log_total, middle, routed = attended
    ups, downs = line_blocks
    rows, width = x.shape
    pieces = dp_size()
    ranks = lax.axis_size("expert")
    experts_here, _, hidden = w_gate.shape
    capacity = rows * TOPK // EXPERTS
    slots = experts_here * capacity
    sums, everyone, expert_rows, gates, codes, gate_pre, up_pre = call(
        functools.partial(experts_kernel, pieces, ranks, len(expert_parts)),
        (
            struct((ranks, rows, width), bf16),
            struct((ranks, rows, width), bf16),
            struct((ranks, slots, width), bf16),
            struct((ranks, EXPERTS, rows), f32),
            struct((ranks, EXPERTS, rows), f32),
            struct((experts_here, ranks * capacity, hidden), bf16),
            struct((experts_here, ranks * capacity, hidden), bf16),
        ),
        [SMEM] + [ANY] * (2 * ranks - 1) + [VMEM] * 3 + [ANY] * (3 + pieces * len(expert_parts)),
        (VMEM, ANY, ANY, VMEM, VMEM)
        + (pl.BlockSpec((1, ranks * capacity, hidden), lambda e: (e, 0, 0)),) * 2,
        [
            pltpu.VMEM((ranks, slots, rows), bf16),
            pltpu.VMEM((ranks, slots, width), bf16),
            pltpu.VMEM((2, width, hidden), bf16),
            pltpu.VMEM((2, width, hidden), bf16),
            pltpu.VMEM((2, hidden, width), bf16),
            pltpu.VMEM((ranks, rows, width), bf16),
            pltpu.VMEM((ranks, slots, width), bf16),
            pltpu.SemaphoreType.DMA((2, 3)),
            pltpu.SemaphoreType.DMA,
            pltpu.SemaphoreType.DMA((2,)),
        ],
        grid=(experts_here,),
        flops=6 * experts_here * ranks * capacity * width * hidden,
        bytes_accessed=6 * experts_here * width * hidden,
        name="experts",
        waits=waits,
    )(
        info, routed, *ups, *downs, routes, usable, router, w_gate, w_up, w_down,
        *[piece for chunk in expert_parts for piece in chunk],
    )
    kept = (x, query, keyval, earlier, mixed, log_total, middle, everyone, expert_rows, gates, codes, gate_pre, up_pre)
    return middle, sums, kept


def layer_result(middle, sums, ties={}):
    return (middle + line_reduce(sums, ties)).astype(bf16)


def layer_backward(layer, grad, grad_line, kept, weights, tables, info, waits={}):
    (gain_attn, gain_moe, router, owns, dense_parts, expert_parts) = weights
    w_query, w_key, w_value, w_out, w_gate, w_up, w_down = owns
    cosine, sine, query_docs, key_docs, usable, reach = tables
    (x, query, keyval, earlier, mixed, log_total, middle, everyone, expert_rows, gates, codes, gate_pre, up_pre) = kept
    rows, width = x.shape
    ranks = lax.axis_size("expert")
    pieces = dp_size()
    kv_width = 2 * KV_HEADS * HEAD_DIM
    keys = (reach + 1) * rows
    experts_here, _, hidden = w_gate.shape
    capacity = rows * TOPK // EXPERTS
    slots = experts_here * capacity
    ups, downs = grad_line
    per_expert = pl.BlockSpec((1, ranks * capacity, hidden), lambda e: (e, 0, 0))
    sums, grad_router, grad_rows, d_gate, d_up, activated = call(
        functools.partial(experts_back_kernel, pieces, ranks, len(expert_parts)),
        (
            struct((ranks, rows, width), bf16),
            struct((EXPERTS, width), f32),
            struct((ranks, slots, width), bf16),
        )
        + (struct((experts_here, ranks * capacity, hidden), bf16),) * 3,
        [SMEM] + [ANY] * (2 * ranks - 1) + [VMEM] * 4 + [per_expert] * 2
        + [ANY] * (3 + pieces * len(expert_parts)),
        (VMEM, VMEM, ANY) + (per_expert,) * 3,
        [
            pltpu.VMEM((ranks, rows, width), bf16),
            pltpu.VMEM((ranks, slots, rows), bf16),
            pltpu.VMEM((ranks, slots, LANES), f32),
            pltpu.VMEM((ranks, max(8, experts_here), rows), f32),
            pltpu.VMEM((ranks, slots, width), bf16),
            pltpu.VMEM((2, width, hidden), bf16),
            pltpu.VMEM((2, width, hidden), bf16),
            pltpu.VMEM((2, hidden, width), bf16),
            pltpu.VMEM((ranks, slots, width), bf16),
            pltpu.SemaphoreType.DMA((2, 3)),
            pltpu.SemaphoreType.DMA,
            pltpu.SemaphoreType.DMA,
        ],
        grid=(experts_here,),
        flops=6 * experts_here * ranks * capacity * width * hidden,
        bytes_accessed=6 * experts_here * width * hidden,
        name="experts_back",
        waits=waits.get("experts_back", ()),
    )(
        info, grad, *ups, *downs, everyone, gates, codes, router, gate_pre, up_pre, w_gate, w_up, w_down,
        *[piece for chunk in expert_parts for piece in chunk],
    )
    wide, narrow = width // pieces, hidden // pieces
    piece_rows = 2 * wide + 2 * narrow
    chunk_count = min(2 if layer == 1 else 4, experts_here)
    per_chunk = experts_here // chunk_count
    marks = []
    if "reduce" in waits:
        sums, *waits["reduce"] = tie(sums, *waits["reduce"])
    if layer == 1:
        d_routed = lax.psum_scatter(sums, "expert", scatter_dimension=0, tiled=True)
        marks.append([])
    else:
        d_routed = line_reduce(sums, marks=marks)
    marks += marks[-1:] * 2
    own_terms = (expert_rows, grad_rows, d_gate, d_up, activated)
    near_terms = [swapped(term, "near", 1) for term in own_terms]
    pairs = []

    def gradients(*others):
        c = len(pairs)
        place = functools.partial(lambda c, e: (c * per_chunk + e, 0, 0), c)
        row_place = functools.partial(lambda c, e: (0, c * per_chunk + e, 0), c)
        in_specs = [pl.BlockSpec((ranks, capacity, width), row_place)] * 2 + [
            pl.BlockSpec((1, ranks * capacity, hidden), place)
        ] * 3
        pairs.append(
            call(
                expert_grads_kernel,
                struct((pieces // 2, per_chunk, piece_rows, hidden), bf16),
                [SMEM] + in_specs * 2,
                pl.BlockSpec((pieces // 2, 1, piece_rows, hidden), lambda e: (0, e, 0, 0)),
                [],
                grid=(per_chunk,),
                flops=6 * per_chunk * ranks * capacity * width * hidden,
                bytes_accessed=9 * per_chunk * width * hidden,
                name="expert_grads",
                waits=[*others, *pairs[-1:]],
            )(info, *own_terms, *near_terms)
        )

    gradients(*marks[0], *waits.get("expert_grads", ()))
    if layer == 0:
        gradients(*marks[1])
    else:
        pairs[0], d_routed = tie(pairs[0], d_routed)
        d_routed = d_routed[0].astype(f32)
    outs = call(
        functools.partial(attend_back_kernel, pieces, reach),
        (
            struct((rows, width), f32),
            struct((rows, width), bf16),
            struct((rows, kv_width), f32),
        )
        + (struct((rows, kv_width), bf16),) * reach
        + (struct((pieces // 2, width // pieces, width), bf16),) * 2
        + (struct((1, width), f32),),
        [SMEM] + [VMEM] * 7 + [ANY] * (1 + reach) + [VMEM] * 4 + [ANY] * (1 + pieces),
        (VMEM,) * (6 + reach),
        [
            pltpu.VMEM((keys, kv_width), bf16),
            pltpu.VMEM((rows, keys), f32),
            pltpu.VMEM((width, width), bf16),
            pltpu.VMEM((rows, width), bf16),
            pltpu.VMEM((kv_width, keys), f32),
            pltpu.SemaphoreType.DMA,
            pltpu.SemaphoreType.DMA,
        ],
        flops=40 * rows * keys * width,
        bytes_accessed=2 * width * width,
        name="attend_back",
        waits=pairs[:1],
    )(
        info, d_routed, grad[:, :width], middle, gain_moe, mixed, query, log_total, keyval, *earlier,
        query_docs, key_docs, cosine, sine, w_out, *dense_parts,
    )
    d_middle, d_query, d_own = outs[:3]
    d_earlier = outs[3 : 3 + reach]
    out_keep, out_send, grad_gain_moe = outs[3 + reach :]
    gradients(d_query)
    moving = d_earlier[reach - 1]
    for s in reversed(range(reach)):
        moving = shifted(moving, "expert", -1)
        if s > 0:
            moving = (moving.astype(f32) + d_earlier[s - 1].astype(f32)).astype(bf16)
    piece_struct = struct((pieces // 2, width // pieces, width), bf16)
    d_normed, query_keep, query_send = call(
        functools.partial(query_back_kernel, pieces),
        (struct((rows, width), f32), piece_struct, piece_struct),
        [SMEM] + [VMEM] * 3 + [ANY] * (1 + pieces),
        (VMEM,) * 3,
        [pltpu.VMEM((width, width), bf16), pltpu.SemaphoreType.DMA],
        flops=4 * rows * width * width,
        bytes_accessed=4 * width * width,
        name="query_back",
        waits=pairs[-1:],
    )(info, x, gain_attn, d_query, w_query, *dense_parts)
    if layer == 0:
        gradients(d_normed)
    kv_struct = struct((pieces // 2, width // pieces, kv_width + LANES), bf16)
    d_x, kv_keep, kv_send = call(
        functools.partial(keyval_back_kernel, pieces),
        (struct((rows, width), bf16), kv_struct, kv_struct),
        [SMEM] + [VMEM] * 10 + [ANY] * (2 + pieces),
        (VMEM,) * 3,
        [
            pltpu.VMEM((width, kv_width), bf16),
            pltpu.VMEM((rows, kv_width), bf16),
            pltpu.SemaphoreType.DMA,
        ],
        flops=4 * rows * width * kv_width,
        bytes_accessed=4 * width * kv_width,
        name="keyval_back",
        waits=pairs[-1:] if layer == 0 else (),
    )(
        info, x, gain_attn, d_own, moving, d_normed, d_middle, cosine, sine, grad_router, grad_gain_moe,
        w_key, w_value, *dense_parts,
    )
    dense = jnp.concatenate(
        [
            near_sum(keep, send)
            for keep, send in ((out_keep, out_send), (query_keep, query_send), (kv_keep, kv_send))
        ],
        axis=2,
    )
    expert_sums = [lax.psum_scatter(pair, "far", scatter_dimension=0, tiled=True)[0] for pair in pairs]
    return d_x, expert_sums, dense


def doc_ids(lengths, positions):
    endings = jnp.cumsum(lengths)
    return jnp.sum((positions[:, None] >= endings[None, :]).astype(jnp.int32), axis=1)


def per_device(
    inputs, cotangent, gain_attn, w_query, w_key, w_value, w_out, gain_moe, w_router, w_gate, w_up, w_down,
    doc_lengths, routes,
):
    rows, width = inputs.shape[2:]
    ranks = lax.axis_size("expert")
    pieces = dp_size()
    section = lax.axis_index("section")
    place = lax.axis_index("far") * 2 + lax.axis_index("near")
    line = lax.axis_index("expert")
    experts_here, _, hidden = w_gate.shape[1:]
    first = section == 0

    def mine(values):
        return lax.dynamic_index_in_dim(values, section, 0, False)

    def other(values):
        return lax.dynamic_index_in_dim(values, 1 - section, 0, False)

    x = mine(inputs[:, 0])
    top = mine(cotangent[:, 0])
    lengths = mine(doc_lengths[:, 0])

    wide, narrow = width // pieces, hidden // pieces
    where = jnp.stack([jnp.int32(0), place, line]).astype(jnp.int32)
    dense_own = (w_query[0], w_key[0], w_value[0], w_out[0])
    small = jnp.concatenate([w_router[0].T.astype(f32), gain_attn, gain_moe], axis=0)
    other_small = swapped(small, "section", 1)
    here = routes[0, :, 0]
    my_routes = mine(here)
    other_routes = swapped(other(here), "section", 1)
    dense_piece, other_small, other_routes = tie(pack_dense(where, dense_own, pieces), other_small, other_routes)
    dense_first_hop = swapped(dense_piece, "section", 1)
    both = jnp.concatenate(
        [jnp.where(first, my_routes, other_routes), jnp.where(first, other_routes, my_routes)], axis=1
    )
    named = jnp.pad(both.astype(bf16), ((0, 0), (0, LANES - 2 * TOPK)))
    top_named = jnp.concatenate([top, named], axis=1)
    top_line = line_gather(top_named)
    dense_first_hop, top_line[0][0], top_line[1][0] = tie(dense_first_hop, top_line[0][0], top_line[1][0])
    cyclic = [top_named] + [
        jnp.where(line >= s, top_line[0][s - 1], top_line[1][ranks - s - 1]) for s in range(1, ranks)
    ]
    cyclic = jnp.stack([block[:, width : width + 2 * TOPK] for block in cyclic[::-1]] * 2)
    both = lax.dynamic_slice_in_dim(cyclic, ranks - 1 - line, ranks, 0).reshape(ranks * rows, 2 * TOPK)
    both = both.T.astype(jnp.int32).reshape(2, TOPK, ranks * rows)
    def with_line(piece, bit):
        if bit == 1:
            piece, top_line[0][-1], top_line[1][-1] = tie(piece, top_line[0][-1], top_line[1][-1])
        return piece

    dense_parts = spread_pieces(dense_first_hop, with_line)
    sizes = [2, 2, 2, 1, 1] if experts_here == 8 else [1] * experts_here
    packs = [
        pack_experts(where, (w_gate[0], w_up[0], w_down[0]), pieces, sum(sizes[:c]), size)
        for c, size in enumerate(sizes)
    ]

    owns = (w_query[0], w_key[0], w_value[0], w_out[0], w_gate[0], w_up[0], w_down[0])
    offset = line * rows
    reach = min((WINDOW - 1) // rows + 1, ranks - 1)
    positions = offset + jnp.arange(rows, dtype=jnp.int32)
    key_places = offset - reach * rows + jnp.arange((reach + 1) * rows, dtype=jnp.int32)
    query_docs = doc_ids(lengths, positions)[:, None]
    key_docs = jnp.where(key_places >= 0, doc_ids(lengths, key_places), -1)[None, :]
    usable = (doc_ids(lengths, jnp.arange(ranks * rows, dtype=jnp.int32)) < NDOC).astype(jnp.int32)[None, :]
    half = HEAD_DIM // 2
    inverse = 10000.0 ** (-(jnp.arange(half, dtype=f32) * (2.0 / HEAD_DIM)))
    angles = positions.astype(f32)[:, None] * inverse[None, :]
    cosine = jnp.tile(jnp.cos(angles), (1, 4))
    sine = jnp.sin(angles)
    sine = jnp.concatenate([-sine, sine, -sine, sine], axis=1)
    tables = (cosine, sine, query_docs, key_docs, usable, reach)

    weights = []
    infos = []
    for layer in range(2):
        held = section == layer
        table = jnp.where(held, small, other_small)
        vectors = (table[EXPERTS : EXPERTS + 1], table[EXPERTS + 1 :], table[:EXPERTS].astype(bf16))
        weights.append(vectors + (owns, dense_parts))
        infos.append(jnp.stack([held.astype(jnp.int32), place, line]).astype(jnp.int32))

    marks = []

    def next_chunk(*mark):
        chunk, = crossing[:1]
        del crossing[0]
        if mark:
            chunk, seen = tie(chunk, *mark)
            marks.append(seen)
        expert_parts.append(spread_pieces(chunk))
        if packs:
            piece, _ = tie(packs.pop(0), chunk)
            crossing.append(swapped(piece, "section", 1))

    expert_parts = []
    piece, dense_gone = tie(packs.pop(0), dense_first_hop)
    crossing = [swapped(piece, "section", 1)]
    if packs:
        crossing.append(swapped(packs.pop(0), "section", 1))
    query, keyval = layer_project(x, weights[0], tables, infos[0], [dense_gone])
    next_chunk()
    earlier = earlier_keys(keyval, tables)
    next_chunk(earlier[-1])
    attended = layer_attend(x, query, keyval, earlier, weights[0], tables, infos[0])
    line_blocks = line_gather(attended[-1])
    for block in line_blocks[0][1:2] * 2 + line_blocks[0][2:3]:
        if crossing:
            next_chunk(block)
    while crossing:
        next_chunk()
    layers = [weight + (expert_parts,) for weight in weights]
    middle, sums, kept_first = layer_experts(
        x, query, keyval, earlier, attended, line_blocks, layers[0], tables, infos[0], both[0], marks
    )
    between = lax.psum_scatter(sums, "expert", scatter_dimension=0, tiled=True)[0]
    between = (middle + between.astype(f32)).astype(bf16)
    query, keyval = layer_project(between, weights[1], tables, infos[1])
    earlier = earlier_keys(keyval, tables)
    attended = layer_attend(between, query, keyval, earlier, weights[1], tables, infos[1])
    middle, sums, kept_second = layer_experts(
        between, query, keyval, earlier, attended, line_gather(attended[-1]), layers[1], tables, infos[1], both[1]
    )
    d_between, experts_second, dense_second = layer_backward(
        1, top_named, top_line, kept_second, layers[1], tables, infos[1]
    )
    between_line = line_gather(d_between)
    half = experts_second[0].shape[0] // 2
    def to_give(of_first, of_second):
        return jnp.where(first, of_second, of_first)

    dense_second = lax.psum_scatter(dense_second, "far", scatter_dimension=0, tiled=True)[0]
    waits = {"experts_back": experts_second[:1], "reduce": experts_second[1:], "expert_grads": [dense_second]}
    d_first, experts_first, dense_first = layer_backward(
        0, d_between, between_line, kept_first, layers[0], tables, infos[0], waits
    )
    experts_second[1:] = waits["reduce"]
    second = [part for of_second in experts_second for part in (of_second[:half], of_second[half:])]
    sums, d_first, dense_first = tie(sums, d_first, dense_first)
    got = [swapped(to_give(a, b), "section", 1) for a, b in zip(experts_first[:2], second)]
    for bit in fetch_bits()[:-1]:
        parts = dense_first.reshape((2, -1) + dense_first.shape[1:])
        high = (place // bit) % 2
        keep = lax.dynamic_index_in_dim(parts, high, 0, False)
        send = lax.dynamic_index_in_dim(parts, 1 - high, 0, False)
        dense_first = (keep.astype(f32) + dp_swapped(send, bit).astype(f32)).astype(bf16)
    got_grad = swapped(to_give(d_first, d_between), "section", 1)
    ties = {2: [dense_first, *got], 3: [got_grad]}
    final = layer_result(middle, sums, ties)
    got_grad, (dense_first, *got) = ties[3][0], ties[2]
    got_output = swapped(to_give(between, final), "section", 1)
    last = len(experts_first) - 1
    got += [None] * (last - 1)
    behind = 0
    for c in range(2, last + 1):
        experts_first[c], got[behind] = tie(experts_first[c], got[behind])
        got[c] = swapped(to_give(experts_first[c], second[c]), "section", 1)
        behind = c
    dense = jnp.concatenate([dense_first.reshape(dense_second.shape), dense_second], axis=1)
    ties = {3: got[2:3]}
    dense = line_reduce(dense.reshape(ranks, -1, dense.shape[1]), ties).astype(bf16)
    dense_first, dense_second = jnp.split(dense, 2, axis=1)
    got[2] = ties[3][0]

    def by_section(of_first, of_second, got):
        held = jnp.where(first, of_first, of_second)
        return jnp.stack([jnp.where(first, held, got), jnp.where(first, got, held)])

    def total(of_first, of_second, got):
        return jnp.where(first, of_first, of_second).astype(f32) + got.astype(f32)

    outputs = by_section(between, final, got_output)
    input_grads = by_section(d_first, d_between, got_grad)
    chunks = [total(*terms) for terms in zip(experts_first, second, got)]
    grad_gate = jnp.concatenate([c[:, :wide] for c in chunks], axis=0)
    grad_up = jnp.concatenate([c[:, wide : 2 * wide] for c in chunks], axis=0)
    grad_down = jnp.concatenate(
        [
            jnp.concatenate([c[:, 2 * wide : 2 * wide + narrow], c[:, 2 * wide + narrow :]], axis=2)
            for c in chunks
        ],
        axis=0,
    )
    dense = total(dense_first, dense_second, swapped(to_give(dense_first, dense_second), "section", 1))
    grad_out, grad_query, grad_keyval = dense[:, :width], dense[:, width : 2 * width], dense[:, 2 * width : 3 * width]
    vectors = dense[:, 3 * width :]
    kv_half = KV_HEADS * HEAD_DIM
    return (
        outputs[None, :, None],
        input_grads[None, :, None],
        vectors[:, EXPERTS + 1][None],
        grad_query[None],
        grad_keyval[:, :kv_half][None],
        grad_keyval[:, kv_half:][None],
        grad_out[None],
        vectors[:, EXPERTS][None],
        vectors[:, :EXPERTS][None],
        grad_gate[None],
        grad_up[None],
        grad_down[None],
    )


def solution(mesh):
    placed = (
        P(None, ("far", "near"), "expert", None),
        P(None, ("far", "near"), "expert", None),
        P("section", None),
        P("section", None, None),
        P("section", None, None),
        P("section", None, None),
        P("section", None, None),
        P("section", None),
        P("section", None, None),
        P("section", "expert", None, None),
        P("section", "expert", None, None),
        P("section", "expert", None, None),
        P(None, ("far", "near"), None),
        P("section", None, ("far", "near"), "expert", None),
    )
    sections, dp, ranks = mesh.devices.shape
    devices = mesh.devices.reshape(sections, dp // 2, 2, ranks)
    split = jax.sharding.Mesh(devices, ("section", "far", "near", "expert"))
    return jax.shard_map(
        per_device,
        mesh=split,
        in_specs=placed,
        out_specs=(
            P("section", None, ("far", "near"), "expert", None),
            P("section", None, ("far", "near"), "expert", None),
            P("section", ("far", "near", "expert")),
            P("section", ("far", "near", "expert"), None),
            P("section", ("far", "near", "expert"), None),
            P("section", ("far", "near", "expert"), None),
            P("section", ("far", "near", "expert"), None),
            P("section", ("far", "near", "expert")),
            P("section", ("far", "near", "expert"), None),
            P("section", "expert", ("far", "near"), None),
            P("section", "expert", ("far", "near"), None),
            P("section", "expert", ("far", "near"), None),
        ),
        check_vma=False,
    )
```
